256 devices in a mesh: lon: 8 (over z_lo, core), lat: 32 (over y, z_hi, x).
Axes of the slice: x: 4, y: 4, z: 8 (z_hi: 2, z_lo: 4; z = z_hi * 4 + z_lo), core: 2. Of those that a mesh axis runs over, the one named last changes fastest.
Arguments:
- east_adjoint: float32 [8, 2048, 2048], P(None, 'lat', 'lon'), may hold values from -6 to 6
- north_adjoint: float32 [8, 2048, 2048], P(None, 'lat', 'lon'), may hold values from -6 to 6
- height_adjoint: float32 [8, 2048, 2048], P(None, 'lat', 'lon'), may hold values from -6 to 6
- zonal_courant: float32 [8, 2048], P(None, 'lat'), may hold values from -0.4 to 0.4
- meridional_courant: float32 [8, 2048], P(None, 'lat'), may hold values from -0.4 to 0.4
- vertical_inverse: float32 [8, 8], replicated, may hold values from -2 to 2
- pass_counts: int32 [512], replicated, may hold values from 1 to 16, as said below
Outputs:
- east_result: float32 [8, 2048, 2048], P(None, 'lat', 'lon')
- north_result: float32 [8, 2048, 2048], P(None, 'lat', 'lon')
- height_result: float32 [8, 2048, 2048], P(None, 'lat', 'lon')
The draws below stay inside these ranges and needn't reach their ends.
Inputs may be any that keep to these rules, and one draw needn't show every extreme that they name: `pass_counts`: the rows next to the two poles (entries 0 and 511) have exactly 16 passes; every row of both bands has at least one.
All inputs are finite; a program needn't handle non-finite values.
Results may differ from the reference program's by a relative error of at most 0.00007.
Values sent between devices are 32-bit elements; how exact they have to be, the bound alone decides.
No kernel may reach another device: no remote copies, remote signals or barrier semaphores. Data moves between devices by JAX's collectives and lax.ppermute only.
A program may use at most 64 MiB of HBM per device.

```python
import jax
import jax.numpy as jnp
from jax import lax

LEV = 8
MAXP = 16
BAND = 256
NLAT = 2048
NLON = 2048


def draw_pass_counts(key, part):
    key = jax.random.fold_in(key, 11)
    counts = jax.random.randint(key, (2 * BAND,), 1, MAXP + 1, dtype=jnp.int32)
    places = jnp.arange(2 * BAND, dtype=jnp.int32)
    at_poles = (places == 0) | (places == 2 * BAND - 1)
    return jnp.where(at_poles, MAXP, counts).astype(jnp.int32)


def steps_of(own_key, extent, cuts, smallest, largest):
    def one(dim, parts):
        steps = jax.random.uniform(jax.random.fold_in(jax.random.fold_in(own_key, 6), dim), (parts,), jnp.float32, smallest / len(cuts), largest / len(cuts))
        return jnp.repeat(jnp.exp(steps), extent[dim] // parts).reshape((-1,) + (1,) * (len(extent) - dim - 1))

    gain = one(*cuts[0])
    for cut in cuts[1:]:
        gain = gain * one(*cut)
    return gain


def scatter_about(own_key, dims, width, most, pieces=(), held_as=jnp.bfloat16):
    drawn = jax.random.normal(own_key, dims, jnp.float32) * width
    if len(pieces) > 0:
        drawn = steps_of(own_key, dims, pieces, -0.22, 0.18) * drawn
    return jnp.clip(drawn, min=-most, max=most).astype(held_as)


def setup_inputs(seed: int = 0) -> dict:
    key_list = jax.random.split(jax.random.key(seed), 8)
    east_adjoint = scatter_about(key_list[0], (LEV, NLAT, NLON), 1.0, 6.0, ((1, 32), (2, 8)), jnp.float32)
    north_adjoint = scatter_about(key_list[1], (LEV, NLAT, NLON), 1.0, 6.0, ((1, 32), (2, 8)), jnp.float32)
    height_adjoint = scatter_about(key_list[2], (LEV, NLAT, NLON), 1.0, 6.0, ((1, 32), (2, 8)), jnp.float32)
    zonal_courant = jnp.clip(jax.random.uniform(key_list[3], (LEV, NLAT), jnp.float32, -0.4, 0.4) * steps_of(key_list[3], (LEV, NLAT), ((1, 32),), -0.4, 0.0), -0.4, 0.4)
    meridional_courant = jnp.clip(jax.random.uniform(key_list[4], (LEV, NLAT), jnp.float32, -0.4, 0.4) * steps_of(key_list[4], (LEV, NLAT), ((1, 32),), -0.4, 0.0), -0.4, 0.4)
    vertical_inverse = scatter_about(key_list[5], (LEV, LEV), LEV ** -0.5, 2.0, (), jnp.float32)
    pass_counts = draw_pass_counts(jax.random.fold_in(key_list[7], 71), 0)
    return dict(east_adjoint=east_adjoint, north_adjoint=north_adjoint, height_adjoint=height_adjoint, zonal_courant=zonal_courant, meridional_courant=meridional_courant, vertical_inverse=vertical_inverse, pass_counts=pass_counts)


gravity_weight = 0.3
divergence_weight = 0.3


def zonal(values):
    return jnp.roll(values, -1, axis=-1) - jnp.roll(values, 1, axis=-1)


def meridional(values, pole_signs):
    half_turn = values.shape[-1] // 2
    top_row = pole_signs * jnp.roll(values[..., :1, :], half_turn, axis=-1)
    bottom = pole_signs * jnp.roll(values[..., -1:, :], half_turn, axis=-1)
    previous = jnp.concatenate([top_row, values[..., :-1, :]], axis=-2)
    following = jnp.concatenate([values[..., 1:, :], bottom], axis=-2)
    return following - previous


def smooth(values, counts):
    limits = counts[:, None]

    def one_pass(repeat, current):
        blurred = 0.25 * (jnp.roll(current, 1, -1) + jnp.roll(current, -1, -1)) + 0.5 * current
        return jnp.where(repeat < limits, blurred, current)

    return lax.fori_loop(0, MAXP, one_pass, values)


def reference(east_adjoint, north_adjoint, height_adjoint, zonal_courant, meridional_courant, vertical_inverse, pass_counts):
    stacked = jnp.stack([east_adjoint, north_adjoint, height_adjoint])
    northern = smooth(stacked[:, :, :BAND], pass_counts[:BAND])
    southern = smooth(stacked[:, :, NLAT - BAND:], pass_counts[BAND:])
    filtered = jnp.concatenate([northern, stacked[:, :, BAND:NLAT - BAND], southern], axis=2)
    east_wind = filtered[0]
    north_wind = filtered[1]
    height = filtered[2]
    height = height + gravity_weight * (zonal(east_wind) + meridional(north_wind, -1.0))
    height = jnp.einsum("kl,kan->lan", vertical_inverse, height, precision=lax.Precision.HIGHEST)
    east_wind = east_wind + divergence_weight * zonal(height)
    north_wind = north_wind + divergence_weight * meridional(height, 1.0)
    fields = jnp.stack([east_wind, north_wind, height])
    pole_signs = jnp.array([1.0, 1.0, -1.0], jnp.float32).reshape(3, 1, 1, 1)
    result = fields + zonal(zonal_courant[None, :, :, None] * fields) + meridional(meridional_courant[None, :, :, None] * fields, pole_signs)
    return (result[0], result[1], result[2])
```

```python
import jax
import jax.numpy as jnp
from jax import lax
from jax.experimental import pallas as pl
from jax.experimental.pallas import tpu as pltpu
from jax.sharding import PartitionSpec as P

MAXP = 16
REACH = 3
WIDE = MAXP + REACH
LANES = 128
PITCH = 21
SPAN = 3 * LANES
KEEP = LANES - 2 * MAXP

gravity_weight = 0.3
divergence_weight = 0.3

VMEM = pl.BlockSpec(memory_space=pltpu.VMEM)
SMEM = pl.BlockSpec(memory_space=pltpu.SMEM)
ANY = pl.BlockSpec(memory_space=pl.ANY)

EDGE_SLOTS = ((0, 0), (0, 1), (1, 0), (1, 1), (1, 2), (2, 0), (2, 1))


def lanes():
    return lax.broadcasted_iota(jnp.int32, (8, LANES), 1)


def turn(values, steps):
    return pltpu.roll(values, steps % values.shape[-1], values.ndim - 1)


def zonal(values):
    return turn(values, -1) - turn(values, 1)


def is_even(axis):
    return lax.rem(lax.axis_index(axis), 2) == 0


def row_count(counts_ref, row, rows, lat_blocks):
    band = counts_ref.shape[0] // 2
    blocks = band // rows
    position = lax.axis_index("lat")
    north = position < blocks
    south = position >= lat_blocks - blocks
    place = jnp.where(north, position, jnp.where(south, position - lat_blocks + 2 * blocks, 0))
    return jnp.where(north | south, counts_ref[place * rows + row], 0)


def undo(count):
    power = jnp.left_shift(1, MAXP - count).astype(jnp.float32)
    return power * power * (2.0 ** (-2 * MAXP))


def spread(first, second, left, right, group):
    lane = lanes()
    moved = turn(first, WIDE)
    a = jnp.where(lane < WIDE, turn(left, -PITCH * group), moved)
    cut = LANES - (KEEP - WIDE)
    b = jnp.where(lane < cut, turn(first, cut), turn(second, cut))
    cut = 2 * LANES - (2 * KEEP - WIDE)
    c = jnp.where(lane < cut, turn(second, cut), turn(right, cut - PITCH * group))
    return a, b, c


def gather(a, b, c):
    lane = lanes()
    a = turn(a, -WIDE)
    b = turn(b, KEEP - WIDE)
    c = turn(c, 2 * KEEP - WIDE)
    low = KEEP - REACH
    first = jnp.where(lane < low, a, b)
    second = jnp.where(lane < 2 * low + REACH - LANES, b, c)
    third = jnp.where(lane < LANES // 2, c, a)
    return first, second, third


def smooth(tile):
    half = tile + turn(tile, 1)
    return half + turn(half, -1)


def pack_kernel(e_ref, n_ref, h_ref, a_ref, b_ref, rows_ref):
    even = is_even("lon")
    lane = lax.broadcasted_iota(jnp.int32, (32, LANES), 1)
    for level in range(8):
        left = right = None
        for group in range(6):
            ref = (e_ref, n_ref, h_ref)[group // 2]
            band = pl.ds(32 * (group % 2), 32)
            first = turn(ref[level, band, :LANES], PITCH * group)
            second = turn(ref[level, band, LANES:], PITCH * group + WIDE)
            if group:
                left = jnp.where(lane < PITCH * group, left, first)
                right = jnp.where(lane < PITCH * group, right, second)
            else:
                left, right = first, second
        a_ref[pl.ds(32 * level, 32)] = jnp.where(even, right, left)
        b_ref[pl.ds(32 * level, 32)] = jnp.where(even, left, right)
    for side in range(2):
        for slot, (field, distance) in enumerate(EDGE_SLOTS):
            row = 63 - distance if side else distance
            ref = (e_ref, n_ref, h_ref)[field]
            rows_ref[side, slot] = ref[:, row, :]


def prepare_kernel(e_ref, n_ref, h_ref, zon_ref, mer_ref, x_ref, zb_ref, mb_ref, copy_ref):
    for f, ref in enumerate((e_ref, n_ref, h_ref)):
        for t in range(2):
            for level in range(8):
                copy_ref[t, pl.ds(64 * level, 64)] = ref[level, :, t * LANES : (t + 1) * LANES]

        def relay(chunk, _):
            for i in range(8):
                row = 8 * chunk + i
                for t in range(2):
                    x_ref[f, row, :, pl.ds(t * LANES, LANES)] = copy_ref[
                        t, pl.ds(row, 8, stride=64), :
                    ]
            return 0

        lax.fori_loop(0, 8, relay, 0)
    mb_ref[0] = jnp.zeros((8, LANES), jnp.float32)
    mb_ref[65] = jnp.zeros((8, LANES), jnp.float32)
    for row in range(64):
        zb_ref[row] = jnp.broadcast_to(zon_ref[:, row : row + 1], (8, LANES))
        mb_ref[row + 1] = jnp.broadcast_to(mer_ref[:, row : row + 1], (8, LANES))


def edge_kernel(lat_blocks, rows_ref, ra_ref, rb_ref, counts_ref, mer_ref, a_ref, b_ref):
    even_lon = is_even("lon")
    even_lat = is_even("lat")
    lane = lanes()
    packs = []
    for side in range(2):
        tiles, limits, scales = [], [], []
        for slot, (field, distance) in enumerate(EDGE_SLOTS):
            row = 63 - distance if side else distance
            half = row // 32
            place = pl.ds(row % 32, 8, stride=32)
            ra, rb = ra_ref[place, :], rb_ref[place, :]
            left = jnp.where(even_lon, rb, ra)
            right = jnp.where(even_lon, ra, rb)
            count = row_count(counts_ref, row, 64, lat_blocks)
            limits.append(count)
            scales.append(undo(count))
            both = rows_ref[side, slot]
            tiles.append(spread(both[:, :LANES], both[:, LANES:], left, right, 2 * field + half))

        def one_pass(repeat, current):
            return [
                tuple(jnp.where(repeat < limit, smooth(t), t) for t in three)
                for limit, three in zip(limits, current)
            ]

        for repeat in range(MAXP):
            tiles = one_pass(repeat, tiles)
        row = 63 if side else 0
        pack = jnp.broadcast_to(mer_ref[:, row : row + 1], (8, LANES))
        out = []
        for slot, (three, scale) in enumerate(zip(tiles, scales)):
            first, second, third = (t * scale for t in gather(*three))
            out += [first, second]
            start = 2 * REACH * slot
            third = turn(third, REACH + start)
            pack = jnp.where((lane >= start) & (lane < start + 2 * REACH), third, pack)
        packs.append(out + [pack])
    for place, (top, bottom) in enumerate(zip(*packs)):
        a_ref[pl.ds(8 * place, 8)] = jnp.where(even_lat, bottom, top)
        b_ref[pl.ds(8 * place, 8)] = jnp.where(even_lat, top, bottom)


def mixing(v_ref):
    level = lax.broadcasted_iota(jnp.int32, (8, LANES), 0)
    columns = []
    for k in range(8):
        column = jnp.full((8, LANES), v_ref[k, 0], jnp.float32)
        for l in range(1, 8):
            column = jnp.where(level == l, v_ref[k, l], column)
        columns.append(column)
    return columns


def mix(columns, height):
    tiles = []
    for t in range(height.shape[-1] // LANES):
        tile = height[..., t * LANES : (t + 1) * LANES]
        total = None
        for k, column in enumerate(columns):
            term = column * jnp.broadcast_to(tile[..., k : k + 1, :], tile.shape)
            total = term if total is None else total + term
        tiles.append(total)
    return jnp.concatenate(tiles, axis=-1)


def wide(column):
    return jnp.concatenate([column] * (SPAN // LANES), axis=-1)


def main_kernel(
    lat_blocks,
    x_ref, ra_ref, rb_ref, counts_ref, zb_ref, mb_ref, v_ref,
    oe_ref, on_ref, oh_ref, tile_ref, edge_ref,
    f_ref, h2_ref, ob_ref, sems,
):
    even_lon = is_even("lon")
    for f in range(3):
        f_ref[f, 0] = jnp.zeros((8, SPAN), jnp.float32)
        f_ref[f, 65] = jnp.zeros((8, SPAN), jnp.float32)
    h2_ref[0] = jnp.zeros((8, SPAN), jnp.float32)
    h2_ref[65] = jnp.zeros((8, SPAN), jnp.float32)

    def filter_row(low, _):
        place = pl.ds(low, 8, stride=32)
        ra, rb = ra_ref[place, :], rb_ref[place, :]
        left = jnp.where(even_lon, rb, ra)
        right = jnp.where(even_lon, ra, rb)
        for half in range(2):
            row = low + 32 * half
            count = row_count(counts_ref, row, 64, lat_blocks)
            tiles = []
            for f in range(3):
                first, second = x_ref[f, row, :, :LANES], x_ref[f, row, :, LANES:]
                tiles += list(spread(first, second, left, right, 2 * f + half))
            tiles = lax.fori_loop(0, count, lambda _, ts: [smooth(t) for t in ts], tiles)
            scale = undo(count)
            for f in range(3):
                three = gather(*tiles[3 * f : 3 * f + 3])
                for t in range(3):
                    f_ref[f, row + 1, :, pl.ds(t * LANES, LANES)] = three[t] * scale
        return 0

    lax.fori_loop(0, 32, filter_row, 0)
    for d in range(4):
        for side in range(2):
            row = 63 - d if side else d
            edge_ref[side, d] = f_ref[0, row + 1]
            edge_ref[side, 4 + d] = f_ref[1, row + 1]
            if d == 0:
                edge_ref[side, 8] = f_ref[2, row + 1]

    columns = mixing(v_ref)

    def heights(chunk, _):
        start = chunk * 4
        own = pl.ds(start + 1, 4)
        slope = f_ref[1, pl.ds(start + 2, 4)] - f_ref[1, pl.ds(start, 4)]
        height = f_ref[2, own] + gravity_weight * (zonal(f_ref[0, own]) + slope)
        h2_ref[own] = mix(columns, height)
        return 0

    lax.fori_loop(0, 16, heights, 0)

    def winds(chunk, _):
        start = chunk * 4
        own = pl.ds(start + 1, 4)
        f_ref[0, own] = f_ref[0, own] + divergence_weight * zonal(h2_ref[own])
        slope = h2_ref[pl.ds(start + 2, 4)] - h2_ref[pl.ds(start, 4)]
        f_ref[1, own] = f_ref[1, own] + divergence_weight * slope
        return 0

    lax.fori_loop(0, 16, winds, 0)

    def results(chunk, _):
        start = chunk * 2
        own = pl.ds(start + 1, 2)
        before, after = pl.ds(start, 2), pl.ds(start + 2, 2)
        zb = wide(zb_ref[pl.ds(start, 2)])
        mb_before, mb_after = wide(mb_ref[before]), wide(mb_ref[after])
        for f in range(3):
            ref = h2_ref if f == 2 else f_ref.at[f]
            field = ref[own]
            value = field + zb * zonal(field) + (mb_after * ref[after] - mb_before * ref[before])
            for i in range(2):
                for t in range(2):
                    ob_ref[f, t, pl.ds(start + i, 8, stride=64), :] = value[
                        i, :, t * LANES : (t + 1) * LANES
                    ]
        return 0

    lax.fori_loop(0, 32, results, 0)
    copies = []
    for f, out in enumerate((oe_ref, on_ref, oh_ref)):
        for t in range(2):
            part = pl.ds(t * LANES, LANES)
            block = ob_ref.at[f, t].reshape(8, 64, LANES)
            copy = pltpu.make_async_copy(
                block.at[:, pl.ds(8, 48)], out.at[:, pl.ds(8, 48), part], sems.at[f, t]
            )
            copy.start()
            copies.append(copy)
            tile_ref[f, :, :8, part] = block[:, :8]
            tile_ref[f, :, 8:, part] = block[:, 56:]
    for d in range(1, 5):
        for side in range(2):
            row = 63 - d if side else d
            edge_ref[side, 8 + d] = h2_ref[row + 1]
    for copy in copies:
        copy.wait()


def finish_kernel(
    lat_blocks,
    edge_ref, tile_ref, ga_ref, gb_ref, zon_ref, mer_ref, v_ref, ie_ref, in_ref, ih_ref,
    oe_ref, on_ref, oh_ref,
    ob_ref, sems,
):
    position = lax.axis_index("lat")
    even_lat = is_even("lat")
    lane = lanes()
    columns = mixing(v_ref)
    copies = []
    for side in range(2):
        top = side == 0
        sense = 1.0 if top else -1.0
        pole = position == (0 if top else lat_blocks - 1)
        turned = jnp.where(pole, -1.0, 1.0)

        def ghost_tile(place):
            a, b = ga_ref[pl.ds(8 * place, 8)], gb_ref[pl.ds(8 * place, 8)]
            return jnp.where(even_lat, b, a) if top else jnp.where(even_lat, a, b)

        pack = ghost_tile(2 * len(EDGE_SLOTS))

        def ghost(field, distance):
            slot = EDGE_SLOTS.index((field, distance))
            third = turn(pack, -REACH - 2 * REACH * slot)
            row = jnp.concatenate([ghost_tile(2 * slot), ghost_tile(2 * slot + 1), third], axis=-1)
            return row * turned if field == 1 else row

        e = {d: edge_ref[side, d] for d in range(4)}
        n = {d: edge_ref[side, 4 + d] for d in range(4)}
        h = {0: edge_ref[side, 8]}
        h2 = {d: edge_ref[side, 8 + d] for d in range(1, 5)}
        for d in range(2):
            e[-1 - d] = ghost(0, d)
            h[-1 - d] = ghost(2, d)
        for d in range(3):
            n[-1 - d] = ghost(1, d)
        for d in (-2, -1, 0):
            slope = sense * (n[d + 1] - n[d - 1])
            h2[d] = mix(columns, h[d] + gravity_weight * (zonal(e[d]) + slope))
        e1, n1 = {}, {}
        for d in range(-1, 4):
            e1[d] = e[d] + divergence_weight * zonal(h2[d])
            n1[d] = n[d] + (divergence_weight * sense) * (h2[d + 1] - h2[d - 1])
        mer_ghost = wide(jnp.where(lane < LANES // 2, turn(pack, LANES // 2), pack))

        def coefficient(ref, d):
            row = d if top else 63 - d
            return jnp.broadcast_to(ref[:, row : row + 1], (8, SPAN))

        zon = {d: coefficient(zon_ref, d) for d in range(3)}
        mer = {d: coefficient(mer_ref, d) for d in range(4)}
        for f, field in enumerate((e1, n1, h2)):
            mer[-1] = mer_ghost if f == 0 else mer_ghost * turned
            ob_ref[f, side] = tile_ref[f, :, 8 * side : 8 * side + 8]
            for d in range(3):
                slope = mer[d + 1] * field[d + 1] - mer[d - 1] * field[d - 1]
                value = field[d] + zon[d] * zonal(field[d]) + sense * slope
                ob_ref[f, side, :, d if top else 7 - d] = value[:, : 2 * LANES]
            out = (oe_ref, on_ref, oh_ref)[f]
            copy = pltpu.make_async_copy(
                ob_ref.at[f, side], out.at[:, pl.ds(56 * side, 8)], sems.at[f, side]
            )
            copy.start()
            copies.append(copy)
    for copy in copies:
        copy.wait()


def body(
    lat_blocks, lon_blocks, axes,
    east_adjoint, north_adjoint, height_adjoint,
    zonal_courant, meridional_courant, vertical_inverse, pass_counts,
):
    f32 = jnp.float32
    fields = (east_adjoint, north_adjoint, height_adjoint)

    def in_vmem(*dims):
        return pltpu.VMEM(dims, f32)

    def params():
        return pltpu.CompilerParams(vmem_limit_bytes=32 * 1024 * 1024)

    lon_a, lon_b, rows = pl.pallas_call(
        pack_kernel,
        out_shape=(in_vmem(256, LANES), in_vmem(256, LANES), in_vmem(2, len(EDGE_SLOTS), 8, 256)),
        in_specs=[VMEM] * 3,
        out_specs=(VMEM,) * 3,
        compiler_params=params(),
        name="pack",
    )(*fields)

    def other_lon(o):
        return (((o + 1) ^ 1) - 1) % lon_blocks

    by_row, zon_wide, mer_wide = pl.pallas_call(
        prepare_kernel,
        out_shape=(in_vmem(3, 64, 8, 256), in_vmem(64, 8, LANES), in_vmem(66, 8, LANES)),
        in_specs=[VMEM] * 5,
        out_specs=(VMEM,) * 3,
        scratch_shapes=[pltpu.VMEM((2, 512, LANES), f32)],
        compiler_params=params(),
        cost_estimate=pl.CostEstimate(flops=4000000, bytes_accessed=6000000, transcendentals=0),
        name="prepare",
    )(*fields, zonal_courant, meridional_courant)

    recv_b = lax.ppermute(lon_b, "lon", [(o, other_lon(o)) for o in range(lon_blocks)])
    recv_a = lax.ppermute(lon_a, "lon", [(o, o ^ 1) for o in range(lon_blocks)])

    places = 8 * (2 * len(EDGE_SLOTS) + 1)
    lat_a, lat_b = pl.pallas_call(
        lambda *refs: edge_kernel(lat_blocks, *refs),
        out_shape=(in_vmem(places, LANES),) * 2,
        in_specs=[VMEM, VMEM, VMEM, SMEM, VMEM],
        out_specs=(VMEM,) * 2,
        compiler_params=params(),
        name="edge",
    )(rows, recv_a, recv_b, pass_counts, meridional_courant)

    def index(a, o):
        return o * lat_blocks + a if axes[0] == "lon" else a * lon_blocks + o

    def other_lat(a, o):
        if a in (0, lat_blocks - 1):
            return a, (o + lon_blocks // 2) % lon_blocks
        return ((a + 1) ^ 1) - 1, o

    pairs = [
        (index(a, o), index(*other_lat(a, o))) for a in range(lat_blocks) for o in range(lon_blocks)
    ]
    ghost_b = lax.ppermute(lat_b, axes, pairs)
    ghost_a = lax.ppermute(lat_a, "lat", [(a, a ^ 1) for a in range(lat_blocks)])

    block = jax.ShapeDtypeStruct(east_adjoint.shape, f32)
    *results, tiles, edges = pl.pallas_call(
        lambda *refs: main_kernel(lat_blocks, *refs),
        out_shape=(block,) * 3 + (in_vmem(3, 8, 16, 256), in_vmem(2, 13, 8, SPAN)),
        in_specs=[VMEM] * 3 + [SMEM, VMEM, VMEM, SMEM],
        out_specs=(ANY,) * 3 + (VMEM,) * 2,
        scratch_shapes=[
            pltpu.VMEM((3, 66, 8, SPAN), f32),
            pltpu.VMEM((66, 8, SPAN), f32),
            pltpu.VMEM((3, 2, 512, LANES), f32),
            pltpu.SemaphoreType.DMA((3, 2)),
        ],
        compiler_params=params(),
        cost_estimate=pl.CostEstimate(flops=200000000, bytes_accessed=20000000, transcendentals=0),
        name="main",
    )(
        by_row, recv_a, recv_b, pass_counts, zon_wide, mer_wide, vertical_inverse
    )

    return pl.pallas_call(
        lambda *refs: finish_kernel(lat_blocks, *refs),
        out_shape=(block,) * 3,
        in_specs=[VMEM] * 6 + [SMEM] + [ANY] * 3,
        out_specs=(ANY,) * 3,
        input_output_aliases={7: 0, 8: 1, 9: 2},
        scratch_shapes=[
            pltpu.VMEM((3, 2, 8, 8, 256), f32),
            pltpu.SemaphoreType.DMA((3, 2)),
        ],
        compiler_params=params(),
        name="finish",
    )(
        edges, tiles, ghost_a, ghost_b, zonal_courant, meridional_courant, vertical_inverse, *results
    )


def solution(mesh):
    sizes = dict(mesh.shape)
    axes = tuple(mesh.axis_names)
    spread_out = P(None, "lat", "lon")
    return jax.shard_map(
        lambda *args: body(sizes["lat"], sizes["lon"], axes, *args),
        mesh=mesh,
        in_specs=(spread_out,) * 3 + (P(None, "lat"), P(None, "lat"), P(), P()),
        out_specs=(spread_out,) * 3,
        check_vma=False,
    )
```

```python
import jax
import jax.numpy as jnp
from jax import lax
from jax.experimental import pallas as pl
from jax.experimental.pallas import tpu as pltpu
from jax.sharding import PartitionSpec as P

MAXP = 16
REACH = 3
WIDE = MAXP + REACH
LANES = 128
SPAN = 3 * LANES
SHARE = 33

gravity_weight = 0.3
divergence_weight = 0.3

VMEM = pl.BlockSpec(memory_space=pltpu.VMEM)
SMEM = pl.BlockSpec(memory_space=pltpu.SMEM)
ANY = pl.BlockSpec(memory_space=pl.ANY)

EDGE_SLOTS = ((0, 0), (0, 1), (1, 0), (1, 1), (1, 2), (2, 0), (2, 1))


HEIGHTS = 8 * WIDE + 4
EDGES = 8 * WIDE + 88
PAYLOAD = EDGES + 24


def lanes():
    return lax.broadcasted_iota(jnp.int32, (8, LANES), 1)


def turn(values, steps):
    return pltpu.roll(values, steps % values.shape[-1], values.ndim - 1)


def zonal(values):
    return turn(values, -1) - turn(values, 1)


def is_even(axis):
    return lax.rem(lax.axis_index(axis), 2) == 0


def row_count(counts_ref, row, rows, lat_blocks):
    band = counts_ref.shape[0] // 2
    blocks = band // rows
    position = lax.axis_index("lat")
    north = position < blocks
    south = position >= lat_blocks - blocks
    place = jnp.where(north, position, jnp.where(south, position - lat_blocks + 2 * blocks, 0))
    return jnp.where(north | south, counts_ref[place * rows + row], 0)


def undo(count):
    power = jnp.left_shift(1, MAXP - count).astype(jnp.float32)
    return power * power * (2.0 ** (-2 * MAXP))


class Stream:
    GROUPS = (1, 1, 2, 4, 8)

    def __init__(self, masks):
        self.masks = masks

    def start(self):
        zero = jnp.zeros((8, LANES), jnp.float32)
        return [zero] * (2 * MAXP + sum(self.GROUPS))

    def step(self, state, tile):
        state = list(state)
        at, later = 0, 2 * MAXP
        for mask, size in zip(self.masks, self.GROUPS):
            entered = tile
            for _ in range(size):
                half = state[at] + tile
                state[at], tile = tile, state[at + 1] + half
                state[at + 1] = half
                at += 2
            delayed = state[later]
            state[later : later + size] = state[later + 1 : later + size] + [entered]
            later += size
            tile = jnp.where(mask, tile, delayed)
        return state, tile


def group_masks(count):
    rest = count - 1
    bits = [jnp.bitwise_and(jnp.right_shift(rest, b), 1) == 1 for b in range(4)]
    used = count > 0
    return [used] + [used & bit for bit in bits]


def pack_kernel(
    e_hbm, n_hbm, h_hbm, a_ref, b_ref, wind_ref, height_ref, edge_ref, x_ref, t_ref, sems
):
    copies = []
    for f, ref in enumerate((e_hbm, n_hbm, h_hbm)):
        copy = pltpu.make_async_copy(ref, x_ref.at[f], sems.at[f])
        copy.start()
        copies.append(copy)
    winds = wind_ref.reshape(256 * 8, LANES)
    for f in range(3):
        copies[f].wait()
        for q in range(4):
            for t in range(2):
                part = x_ref[f, pl.ds(2 * q, 2), :, pl.ds(LANES * t, LANES)]
                turned = part.reshape(LANES, LANES).T
                if f < 2:
                    winds[pl.ds(1024 * t + 4 * f + q, LANES, stride=8), :] = turned
                else:
                    height_ref[pl.ds(512 * t + q, LANES, stride=4), :] = turned
    for side in range(2):
        for slot, (field, distance) in enumerate(EDGE_SLOTS):
            row = 63 - distance if side else distance
            place = 8 * (len(EDGE_SLOTS) * side + slot)
            t_ref[pl.ds(place, 8), :] = x_ref[field, :, row, :]
    t_ref[pl.ds(112, 16), :] = jnp.zeros((16, 256), jnp.float32)
    for t in range(2):
        edge_ref[pl.ds(LANES * t, LANES), :] = t_ref[:, LANES * t : LANES * (t + 1)].T
    even = is_even("lon")
    last = 256 - WIDE
    for ref, right in ((a_ref, even), (b_ref, jnp.logical_not(even))):
        first = jnp.where(right, last, 0)
        ref[pl.ds(0, 8 * WIDE), :] = wind_ref[pl.ds(first, WIDE)].reshape(8 * WIDE, LANES)
        ref[pl.ds(HEIGHTS, 4 * WIDE), :] = jnp.where(
            right, height_ref[pl.ds(4 * last, 4 * WIDE), :], height_ref[pl.ds(0, 4 * WIDE), :]
        )
        ref[pl.ds(EDGES, WIDE), :] = jnp.where(
            right, edge_ref[pl.ds(last, WIDE), :], edge_ref[pl.ds(0, WIDE), :]
        )


def edge_kernel(
    lat_blocks, own_ref, ra_ref, rb_ref, counts_ref, mer_ref, a_ref, b_ref, z_ref, o_ref
):
    even_lon = is_even("lon")
    even_lat = is_even("lat")
    lane = lanes()
    halo = pl.ds(EDGES, WIDE)
    z_ref[pl.ds(24, 256), :] = own_ref[...]
    z_ref[pl.ds(24 - WIDE, WIDE), :] = jnp.where(even_lon, rb_ref[halo, :], ra_ref[halo, :])
    z_ref[pl.ds(280, WIDE), :] = jnp.where(even_lon, ra_ref[halo, :], rb_ref[halo, :])
    z_ref[pl.ds(280 + WIDE, 5), :] = jnp.zeros((5, LANES), jnp.float32)
    count = jnp.zeros((8, LANES), jnp.int32)
    for side in range(2):
        for slot, (_, distance) in enumerate(EDGE_SLOTS):
            row = 63 - distance if side else distance
            place = 8 * (len(EDGE_SLOTS) * side + slot)
            value = row_count(counts_ref, row, 64, lat_blocks)
            count = jnp.where(lane >= place, value, count)
    stream = Stream(group_masks(count))
    scale = undo(count)
    state = stream.start()
    for i in range(SHARE + 2 * MAXP):
        state, tile = stream.step(state, z_ref[pl.ds(24 - WIDE + i, 8, stride=SHARE), :])
        if i >= 2 * MAXP:
            o_ref[pl.ds(i - 2 * MAXP, 8, stride=SHARE), :] = tile * scale
    first = o_ref[pl.ds(REACH, LANES), :].T
    second = o_ref[pl.ds(REACH + LANES, LANES), :].T
    o_ref[pl.ds(REACH, REACH), :] = o_ref[pl.ds(REACH + 2 * LANES, REACH), :]
    third = o_ref[pl.ds(0, LANES), :].T
    packs = []
    for side in range(2):
        row = 63 if side else 0
        pack = jnp.broadcast_to(mer_ref[:, row : row + 1], (8, LANES))
        out = []
        for slot in range(len(EDGE_SLOTS)):
            place = 8 * (len(EDGE_SLOTS) * side + slot)
            out += [first[place : place + 8], second[place : place + 8]]
            start = 2 * REACH * slot
            inside = (lane >= start) & (lane < start + 2 * REACH)
            pack = jnp.where(inside, turn(third[place : place + 8], start), pack)
        packs.append(out + [pack])
    for place, (top, bottom) in enumerate(zip(*packs)):
        a_ref[pl.ds(8 * place, 8)] = jnp.where(even_lat, bottom, top)
        b_ref[pl.ds(8 * place, 8)] = jnp.where(even_lat, top, bottom)


def following(rows):
    count = rows.shape[0]
    return pltpu.roll(rows, count - 1, 0) - pltpu.roll(rows, 1, 0)


def main_kernel(
    lat_blocks,
    wind_ref, height_ref, ra_ref, rb_ref, counts_ref, zon_ref, mer_ref, v_ref,
    oe_ref, on_ref, oh_ref, tile_ref, edge_ref,
    f_ref, h3_ref, wo_ref, ho_ref, c_ref, zb_ref, mb_ref, ob_ref, sems,
):
    even_lon = is_even("lon")
    lane = lanes()
    level = lax.broadcasted_iota(jnp.int32, (8, LANES), 0)
    count = jnp.zeros((8, LANES), jnp.int32)
    for row in range(64):
        value = row_count(counts_ref, row, 64, lat_blocks)
        count = jnp.where(jnp.bitwise_and(lane, 63) == row, value, count)
    stream = Stream(group_masks(count))
    scale = undo(count)

    def left(place):
        return jnp.where(even_lon, rb_ref[place, :], ra_ref[place, :])

    def right(place):
        return jnp.where(even_lon, ra_ref[place, :], rb_ref[place, :])

    state = stream.start()
    for i in range(WIDE):
        state, _ = stream.step(state, left(pl.ds(8 * i, 8)))

    def own_winds(chunk, state):
        for u in range(8):
            i = 8 * chunk + u
            state, tile = stream.step(state, wind_ref[i])
            wo_ref[i + REACH] = tile * scale
        return tuple(state)

    state = lax.fori_loop(0, 32, own_winds, tuple(state))
    for i in range(WIDE):
        state, tile = stream.step(state, right(pl.ds(8 * i, 8)))
        wo_ref[256 + REACH + i] = tile * scale

    def own_height(column, upper):
        if upper:
            return height_ref[pl.ds(4 * column - 4, 8), :]
        return height_ref[pl.ds(4 * column, 8), :]

    state = stream.start()
    steps = 2 * MAXP + 131

    def height_step(state, k, low, high):
        state, tile = stream.step(state, jnp.where(level < 4, low, high))
        ho_ref[k] = tile * scale
        return state

    for k in range(WIDE):
        low = left(pl.ds(HEIGHTS + 4 * k, 8))
        state = height_step(state, k, low, own_height(k + 112, True))

    def own_heights(chunk, state):
        for u in range(0, 10, 2):
            k = WIDE + 1 + 10 * chunk + u
            state = step_pair(state, k, 10 * chunk + u)
        return tuple(state)

    def step_pair(state, k, column):
        place = pl.multiple_of(4 * column, 8)
        a, b = height_ref[pl.ds(place, 8), :], height_ref[pl.ds(place + 8, 8), :]
        c, d = height_ref[pl.ds(place + 528, 8), :], height_ref[pl.ds(place + 536, 8), :]
        state = height_step(state, k, pltpu.roll(a, 4, 0), pltpu.roll(c, 4, 0))
        return height_step(state, k + 1, b, c)

    state = height_step(state, WIDE, own_height(0, False), own_height(131, True))
    state = lax.fori_loop(0, 12, own_heights, tuple(state))
    for k in range(WIDE + 121, steps):
        low = own_height(k - WIDE, False)
        if k + 112 < 256:
            high = own_height(k + 112, True)
        else:
            high = right(pl.ds(HEIGHTS + 4 * (k + 112 - 256) - 4, 8))
        state = height_step(state, k, low, high)

    wo = wo_ref.reshape(wo_ref.shape[0] * 8, LANES)
    ho = ho_ref.reshape(ho_ref.shape[0] * 8, LANES)
    c_ref[...] = jnp.zeros_like(c_ref)
    for f in range(3):
        for q in range(4):
            if f < 2:
                source, block = wo, 4 * f + q
                starts = (WIDE, WIDE + LANES, WIDE + 2 * LANES, WIDE - REACH)
                blocks = (block,) * 4
            else:
                source = ho
                starts = (35, 32, 160, 32)
                blocks = (q, q + 4, q + 4, q)
            for t in range(2):
                tall = source[pl.ds(8 * starts[t] + blocks[t], LANES, stride=8), :]
                f_ref[f, t, pl.ds(LANES * q, LANES), :] = tall.T
            c_ref[pl.ds(0, REACH), :] = source[pl.ds(8 * starts[2] + blocks[2], REACH, stride=8), :]
            c_ref[pl.ds(LANES - REACH, REACH), :] = source[
                pl.ds(8 * starts[3] + blocks[3], REACH, stride=8), :
            ]
            f_ref[f, 2, pl.ds(LANES * q, LANES), :] = c_ref[...].T

    def keep_edge(slot, field, distance):
        for side in range(2):
            row = 63 - distance if side else distance
            for t in range(3):
                edge_ref[side, slot, :, pl.ds(LANES * t, LANES)] = field[
                    t, pl.ds(row, 8, stride=64), :
                ]

    for d in range(4):
        keep_edge(d, f_ref.at[0], d)
        keep_edge(4 + d, f_ref.at[1], d)
    keep_edge(8, f_ref.at[2], 0)
    for l in range(8):
        zb_ref[l] = jnp.broadcast_to(zon_ref[l : l + 1, :], (LANES, 64)).T
        mb_ref[l] = jnp.broadcast_to(mer_ref[l : l + 1, :], (LANES, 64)).T

    def whole(f, place):
        return jnp.concatenate([f_ref[f, t, place, :] for t in range(3)], axis=-1)

    def keep(f, place, values):
        for t in range(3):
            f_ref[f, t, place, :] = values[:, LANES * t : LANES * (t + 1)]

    def heights(l, _):
        place = pl.ds(64 * l, 64)
        slope = zonal(whole(0, place)) + following(whole(1, place))
        value = whole(2, place) + gravity_weight * slope
        for t in range(3):
            h3_ref[t, l] = value[:, LANES * t : LANES * (t + 1)]
        return 0

    lax.fori_loop(0, 8, heights, 0)

    def mix_rows(chunk, _):
        place = pl.ds(pl.multiple_of(8 * chunk, 8), 8)
        for t in range(3):
            old = [h3_ref[t, k, place, :] for k in range(8)]
            for l in range(8):
                total = v_ref[0, l] * old[0]
                for k in range(1, 8):
                    total = total + v_ref[k, l] * old[k]
                f_ref[2, t, pl.ds(pl.multiple_of(64 * l + 8 * chunk, 8), 8), :] = total
        return 0

    lax.fori_loop(0, 8, mix_rows, 0)
    for d in range(1, 5):
        keep_edge(8 + d, f_ref.at[2], d)

    def results(l, _):
        place = pl.ds(64 * l, 64)
        h2 = whole(2, place)
        h2_zonal = zonal(h2)
        e1 = whole(0, place) + divergence_weight * h2_zonal
        n1 = whole(1, place) + divergence_weight * following(h2)
        zon = jnp.concatenate([zb_ref[l]] * 2, axis=-1)
        mer = jnp.concatenate([mb_ref[l]] * 2, axis=-1)
        for f, field in enumerate((e1, n1, h2)):
            slope = (h2_zonal if f == 2 else zonal(field))[:, :256]
            near = field[:, :256]
            ob_ref[f, l] = near + zon * slope + following(mer * near)
        return 0

    lax.fori_loop(0, 8, results, 0)
    copies = []
    for f, out in enumerate((oe_ref, on_ref, oh_ref)):
        copy = pltpu.make_async_copy(
            ob_ref.at[f, :, pl.ds(8, 48)], out.at[:, pl.ds(8, 48)], sems.at[f]
        )
        copy.start()
        copies.append(copy)
        tile_ref[f, :, :8] = ob_ref[f, :, :8]
        tile_ref[f, :, 8:] = ob_ref[f, :, 56:]
    for copy in copies:
        copy.wait()


def mixing(v_ref):
    level = lax.broadcasted_iota(jnp.int32, (8, LANES), 0)
    columns = []
    for k in range(8):
        column = jnp.full((8, LANES), v_ref[k, 0], jnp.float32)
        for l in range(1, 8):
            column = jnp.where(level == l, v_ref[k, l], column)
        columns.append(column)
    return columns


def mix(columns, height):
    tiles = []
    for t in range(height.shape[-1] // LANES):
        tile = height[..., t * LANES : (t + 1) * LANES]
        total = None
        for k, column in enumerate(columns):
            term = column * jnp.broadcast_to(tile[..., k : k + 1, :], tile.shape)
            total = term if total is None else total + term
        tiles.append(total)
    return jnp.concatenate(tiles, axis=-1)


def wide(column):
    return jnp.concatenate([column] * (SPAN // LANES), axis=-1)


def finish_kernel(
    lat_blocks,
    edge_ref, tile_ref, ga_ref, gb_ref, zon_ref, mer_ref, v_ref, ie_ref, in_ref, ih_ref,
    oe_ref, on_ref, oh_ref,
    ob_ref, sems,
):
    position = lax.axis_index("lat")
    even_lat = is_even("lat")
    lane = lanes()
    columns = mixing(v_ref)
    copies = []
    for side in range(2):
        top = side == 0
        sense = 1.0 if top else -1.0
        pole = position == (0 if top else lat_blocks - 1)
        turned = jnp.where(pole, -1.0, 1.0)

        def ghost_tile(place):
            a, b = ga_ref[pl.ds(8 * place, 8)], gb_ref[pl.ds(8 * place, 8)]
            return jnp.where(even_lat, b, a) if top else jnp.where(even_lat, a, b)

        pack = ghost_tile(2 * len(EDGE_SLOTS))

        def ghost(field, distance):
            slot = EDGE_SLOTS.index((field, distance))
            third = turn(pack, -REACH - 2 * REACH * slot)
            row = jnp.concatenate([ghost_tile(2 * slot), ghost_tile(2 * slot + 1), third], axis=-1)
            return row * turned if field == 1 else row

        e = {d: edge_ref[side, d] for d in range(4)}
        n = {d: edge_ref[side, 4 + d] for d in range(4)}
        h = {0: edge_ref[side, 8]}
        h2 = {d: edge_ref[side, 8 + d] for d in range(1, 5)}
        for d in range(2):
            e[-1 - d] = ghost(0, d)
            h[-1 - d] = ghost(2, d)
        for d in range(3):
            n[-1 - d] = ghost(1, d)
        for d in (-2, -1, 0):
            slope = sense * (n[d + 1] - n[d - 1])
            h2[d] = mix(columns, h[d] + gravity_weight * (zonal(e[d]) + slope))
        e1, n1 = {}, {}
        for d in range(-1, 4):
            e1[d] = e[d] + divergence_weight * zonal(h2[d])
            n1[d] = n[d] + (divergence_weight * sense) * (h2[d + 1] - h2[d - 1])
        mer_ghost = wide(jnp.where(lane < LANES // 2, turn(pack, LANES // 2), pack))

        def coefficient(ref, d):
            row = d if top else 63 - d
            return jnp.broadcast_to(ref[:, row : row + 1], (8, SPAN))

        zon = {d: coefficient(zon_ref, d) for d in range(3)}
        mer = {d: coefficient(mer_ref, d) for d in range(4)}
        for f, field in enumerate((e1, n1, h2)):
            mer[-1] = mer_ghost if f == 0 else mer_ghost * turned
            ob_ref[f, side] = tile_ref[f, :, 8 * side : 8 * side + 8]
            for d in range(3):
                slope = mer[d + 1] * field[d + 1] - mer[d - 1] * field[d - 1]
                value = field[d] + zon[d] * zonal(field[d]) + sense * slope
                ob_ref[f, side, :, d if top else 7 - d] = value[:, : 2 * LANES]
            out = (oe_ref, on_ref, oh_ref)[f]
            copy = pltpu.make_async_copy(
                ob_ref.at[f, side], out.at[:, pl.ds(56 * side, 8)], sems.at[f, side]
            )
            copy.start()
            copies.append(copy)
    for copy in copies:
        copy.wait()


def body(
    lat_blocks, lon_blocks, axes,
    east_adjoint, north_adjoint, height_adjoint,
    zonal_courant, meridional_courant, vertical_inverse, pass_counts,
):
    f32 = jnp.float32
    fields = (east_adjoint, north_adjoint, height_adjoint)

    def in_vmem(*dims):
        return pltpu.VMEM(dims, f32)

    def params():
        return pltpu.CompilerParams(vmem_limit_bytes=40 * 1024 * 1024)

    lon_a, lon_b, winds, heights, edge_rows = pl.pallas_call(
        pack_kernel,
        out_shape=(
            in_vmem(PAYLOAD, LANES), in_vmem(PAYLOAD, LANES),
            in_vmem(256, 8, LANES), in_vmem(1024, LANES), in_vmem(256, LANES),
        ),
        in_specs=[ANY] * 3,
        out_specs=(VMEM,) * 5,
        scratch_shapes=[
            pltpu.VMEM((3, 8, 64, 256), f32),
            pltpu.VMEM((LANES, 256), f32),
            pltpu.SemaphoreType.DMA((3,)),
        ],
        compiler_params=params(),
        name="pack",
    )(*fields)

    def other_lon(o):
        return (((o + 1) ^ 1) - 1) % lon_blocks

    recv_b = lax.ppermute(lon_b, "lon", [(o, other_lon(o)) for o in range(lon_blocks)])
    recv_a = lax.ppermute(lon_a, "lon", [(o, o ^ 1) for o in range(lon_blocks)])

    places = 8 * (2 * len(EDGE_SLOTS) + 1)
    lat_a, lat_b = pl.pallas_call(
        lambda *refs: edge_kernel(lat_blocks, *refs),
        out_shape=(in_vmem(places, LANES),) * 2,
        in_specs=[VMEM, VMEM, VMEM, SMEM, VMEM],
        out_specs=(VMEM,) * 2,
        scratch_shapes=[pltpu.VMEM((304, LANES), f32), pltpu.VMEM((264, LANES), f32)],
        compiler_params=params(),
        name="edge",
    )(edge_rows, recv_a, recv_b, pass_counts, meridional_courant)

    def index(a, o):
        return o * lat_blocks + a if axes[0] == "lon" else a * lon_blocks + o

    def other_lat(a, o):
        if a in (0, lat_blocks - 1):
            return a, (o + lon_blocks // 2) % lon_blocks
        return ((a + 1) ^ 1) - 1, o

    pairs = [
        (index(a, o), index(*other_lat(a, o))) for a in range(lat_blocks) for o in range(lon_blocks)
    ]
    ghost_b = lax.ppermute(lat_b, axes, pairs)
    ghost_a = lax.ppermute(lat_a, "lat", [(a, a ^ 1) for a in range(lat_blocks)])

    block = jax.ShapeDtypeStruct(east_adjoint.shape, f32)
    *results, tiles, edges = pl.pallas_call(
        lambda *refs: main_kernel(lat_blocks, *refs),
        out_shape=(block,) * 3 + (in_vmem(3, 8, 16, 256), in_vmem(2, 13, 8, SPAN)),
        in_specs=[VMEM] * 4 + [SMEM, VMEM, VMEM, SMEM],
        out_specs=(ANY,) * 3 + (VMEM,) * 2,
        scratch_shapes=[
            pltpu.VMEM((3, 3, 512, LANES), f32),
            pltpu.VMEM((3, 8, 64, LANES), f32),
            pltpu.VMEM((280, 8, LANES), f32),
            pltpu.VMEM((168, 8, LANES), f32),
            pltpu.VMEM((LANES, LANES), f32),
            pltpu.VMEM((8, 64, LANES), f32),
            pltpu.VMEM((8, 64, LANES), f32),
            pltpu.VMEM((3, 8, 64, 256), f32),
            pltpu.SemaphoreType.DMA((3,)),
        ],
        compiler_params=params(),
        cost_estimate=pl.CostEstimate(flops=200000000, bytes_accessed=20000000, transcendentals=0),
        name="main",
    )(
        winds, heights, recv_a, recv_b,
        pass_counts, zonal_courant, meridional_courant, vertical_inverse,
    )

    return pl.pallas_call(
        lambda *refs: finish_kernel(lat_blocks, *refs),
        out_shape=(block,) * 3,
        in_specs=[VMEM] * 6 + [SMEM] + [ANY] * 3,
        out_specs=(ANY,) * 3,
        input_output_aliases={7: 0, 8: 1, 9: 2},
        scratch_shapes=[
            pltpu.VMEM((3, 2, 8, 8, 256), f32),
            pltpu.SemaphoreType.DMA((3, 2)),
        ],
        compiler_params=params(),
        name="finish",
    )(
        edges, tiles, ghost_a, ghost_b, zonal_courant, meridional_courant, vertical_inverse, *results
    )


def solution(mesh):
    sizes = dict(mesh.shape)
    axes = tuple(mesh.axis_names)
    spread_out = P(None, "lat", "lon")
    return jax.shard_map(
        lambda *args: body(sizes["lat"], sizes["lon"], axes, *args),
        mesh=mesh,
        in_specs=(spread_out,) * 3 + (P(None, "lat"), P(None, "lat"), P(), P()),
        out_specs=(spread_out,) * 3,
        check_vma=False,
    )
```

```python
import jax
import jax.numpy as jnp
from jax import lax
from jax.experimental import pallas as pl
from jax.experimental.pallas import tpu as pltpu
from jax.sharding import PartitionSpec as P

MAXP = 16
REACH = 3
WIDE = MAXP + REACH
LANES = 128
SPAN = 3 * LANES
SHARE = 33

gravity_weight = 0.3
divergence_weight = 0.3

VMEM = pl.BlockSpec(memory_space=pltpu.VMEM)
SMEM = pl.BlockSpec(memory_space=pltpu.SMEM)
HBM = pl.BlockSpec(memory_space=pltpu.HBM)

EDGE_SLOTS = ((0, 0), (0, 1), (1, 0), (1, 1), (1, 2), (2, 0), (2, 1))


HEIGHTS = 8 * WIDE + 4
EDGES = 8 * WIDE + 88
PAYLOAD = EDGES + 24


def lanes():
    return lax.broadcasted_iota(jnp.int32, (8, LANES), 1)


def turn(values, steps):
    return pltpu.roll(values, steps % values.shape[-1], values.ndim - 1)


def zonal(values):
    return turn(values, -1) - turn(values, 1)


def is_even(axis):
    return lax.rem(lax.axis_index(axis), 2) == 0


def row_count(counts_ref, row, rows, lat_blocks):
    band = counts_ref.shape[0] // 2
    blocks = band // rows
    position = lax.axis_index("lat")
    north = position < blocks
    south = position >= lat_blocks - blocks
    place = jnp.where(north, position, jnp.where(south, position - lat_blocks + 2 * blocks, 0))
    return jnp.where(north | south, counts_ref[place * rows + row], 0)


def undo(count):
    power = jnp.left_shift(1, MAXP - count).astype(jnp.float32)
    return power * power * (2.0 ** (-2 * MAXP))


class Stream:
    GROUPS = (1, 1, 2, 4, 8)

    def __init__(self, masks):
        self.masks = masks

    def start(self):
        zero = jnp.zeros((8, LANES), jnp.float32)
        return [zero] * (2 * MAXP + sum(self.GROUPS))

    def step(self, state, tile):
        state = list(state)
        at, later = 0, 2 * MAXP
        for mask, size in zip(self.masks, self.GROUPS):
            entered = tile
            for _ in range(size):
                half = state[at] + tile
                state[at], tile = tile, state[at + 1] + half
                state[at + 1] = half
                at += 2
            delayed = state[later]
            state[later : later + size] = state[later + 1 : later + size] + [entered]
            later += size
            tile = jnp.where(mask, tile, delayed)
        return state, tile


def group_masks(count):
    rest = count - 1
    bits = [jnp.bitwise_and(jnp.right_shift(rest, b), 1) == 1 for b in range(4)]
    used = count > 0
    return [used] + [used & bit for bit in bits]


def pack_kernel(
    e_hbm, n_hbm, h_hbm, a_ref, b_ref, wind_ref, height_ref, edge_ref, x_ref, t_ref, sems
):
    copies = []
    for f, ref in enumerate((e_hbm, n_hbm, h_hbm)):
        copy = pltpu.make_async_copy(ref, x_ref.at[f], sems.at[f])
        copy.start()
        copies.append(copy)
    winds = wind_ref.reshape(256 * 8, LANES)
    for f in range(3):
        copies[f].wait()
        for q in range(4):
            for t in range(2):
                part = x_ref[f, pl.ds(2 * q, 2), :, pl.ds(LANES * t, LANES)]
                turned = part.reshape(LANES, LANES).T
                if f < 2:
                    winds[pl.ds(1024 * t + 4 * f + q, LANES, stride=8), :] = turned
                else:
                    height_ref[pl.ds(512 * t + q, LANES, stride=4), :] = turned
    for side in range(2):
        for slot, (field, distance) in enumerate(EDGE_SLOTS):
            row = 63 - distance if side else distance
            place = 8 * (len(EDGE_SLOTS) * side + slot)
            t_ref[pl.ds(place, 8), :] = x_ref[field, :, row, :]
    t_ref[pl.ds(112, 16), :] = jnp.zeros((16, 256), jnp.float32)
    for t in range(2):
        edge_ref[pl.ds(LANES * t, LANES), :] = t_ref[:, LANES * t : LANES * (t + 1)].T
    even = is_even("lon")
    last = 256 - WIDE
    for ref, right in ((a_ref, even), (b_ref, jnp.logical_not(even))):
        first = jnp.where(right, last, 0)
        ref[pl.ds(0, 8 * WIDE), :] = wind_ref[pl.ds(first, WIDE)].reshape(8 * WIDE, LANES)
        ref[pl.ds(HEIGHTS, 4 * WIDE), :] = jnp.where(
            right, height_ref[pl.ds(4 * last, 4 * WIDE), :], height_ref[pl.ds(0, 4 * WIDE), :]
        )
        ref[pl.ds(EDGES, WIDE), :] = jnp.where(
            right, edge_ref[pl.ds(last, WIDE), :], edge_ref[pl.ds(0, WIDE), :]
        )


def edge_kernel(own_ref, ra_ref, rb_ref, count_ref, mer_ref, a_ref, b_ref, z_ref, o_ref):
    even_lon = is_even("lon")
    even_lat = is_even("lat")
    lane = lanes()
    halo = pl.ds(EDGES, WIDE)
    z_ref[pl.ds(24, 256), :] = own_ref[...]
    z_ref[pl.ds(24 - WIDE, WIDE), :] = jnp.where(even_lon, rb_ref[halo, :], ra_ref[halo, :])
    z_ref[pl.ds(280, WIDE), :] = jnp.where(even_lon, ra_ref[halo, :], rb_ref[halo, :])
    z_ref[pl.ds(280 + WIDE, 5), :] = jnp.zeros((5, LANES), jnp.float32)
    count = count_ref[...]
    stream = Stream(group_masks(count))
    scale = undo(count)
    state = stream.start()
    for i in range(SHARE + 2 * MAXP):
        state, tile = stream.step(state, z_ref[pl.ds(24 - WIDE + i, 8, stride=SHARE), :])
        if i >= 2 * MAXP:
            o_ref[pl.ds(i - 2 * MAXP, 8, stride=SHARE), :] = tile * scale
    first = o_ref[pl.ds(REACH, LANES), :].T
    second = o_ref[pl.ds(REACH + LANES, LANES), :].T
    o_ref[pl.ds(REACH, REACH), :] = o_ref[pl.ds(REACH + 2 * LANES, REACH), :]
    third = o_ref[pl.ds(0, LANES), :].T
    packs = []
    for side in range(2):
        row = 63 if side else 0
        pack = jnp.broadcast_to(mer_ref[:, row : row + 1], (8, LANES))
        out = []
        for slot in range(len(EDGE_SLOTS)):
            place = 8 * (len(EDGE_SLOTS) * side + slot)
            out += [first[place : place + 8], second[place : place + 8]]
            start = 2 * REACH * slot
            inside = (lane >= start) & (lane < start + 2 * REACH)
            pack = jnp.where(inside, turn(third[place : place + 8], start), pack)
        packs.append(out + [pack])
    for place, (top, bottom) in enumerate(zip(*packs)):
        a_ref[pl.ds(8 * place, 8)] = jnp.where(even_lat, bottom, top)
        b_ref[pl.ds(8 * place, 8)] = jnp.where(even_lat, top, bottom)


def following(rows):
    count = rows.shape[0]
    return pltpu.roll(rows, count - 1, 0) - pltpu.roll(rows, 1, 0)


def is_polar(lat_blocks, rows, band):
    position = lax.axis_index("lat")
    return (position < band // rows) | (position >= lat_blocks - band // rows)


def stencils(f_ref, h3_ref, v_ref, zb_ref, mb_ref, keep_heights, write):
    tiles = f_ref.shape[1]

    def whole(f, place):
        return jnp.concatenate([f_ref[f, t, place, :] for t in range(tiles)], axis=-1)

    def heights(l, _):
        place = pl.ds(pl.multiple_of(64 * l, 64), 64)
        slope = zonal(whole(0, place)) + following(whole(1, place))
        value = whole(2, place) + gravity_weight * slope
        for t in range(tiles):
            h3_ref[t, l] = value[:, LANES * t : LANES * (t + 1)]
        return 0

    lax.fori_loop(0, 8, heights, 0)

    def mix_rows(chunk, _):
        place = pl.ds(pl.multiple_of(8 * chunk, 8), 8)
        for t in range(tiles):
            old = [h3_ref[t, k, place, :] for k in range(8)]
            for l in range(8):
                total = v_ref[0, l] * old[0]
                for k in range(1, 8):
                    total = total + v_ref[k, l] * old[k]
                f_ref[2, t, pl.ds(pl.multiple_of(64 * l + 8 * chunk, 8), 8), :] = total
        return 0

    lax.fori_loop(0, 8, mix_rows, 0)
    keep_heights()

    def results(l, _):
        place = pl.ds(pl.multiple_of(64 * l, 64), 64)
        h2 = whole(2, place)
        h2_zonal = zonal(h2)
        e1 = whole(0, place) + divergence_weight * h2_zonal
        n1 = whole(1, place) + divergence_weight * following(h2)
        zon = jnp.concatenate([zb_ref[l]] * tiles, axis=-1)
        mer = jnp.concatenate([mb_ref[l]] * tiles, axis=-1)
        for f, field in enumerate((e1, n1, h2)):
            slope = h2_zonal if f == 2 else zonal(field)
            write(f, l, field + zon * slope + following(mer * field))
        return 0

    lax.fori_loop(0, 8, results, 0)


def edge_row(side, distance):
    return 63 - distance if side else distance


def interior_kernel(
    lat_blocks,
    x_ref, wind_ref, height_ref, counts_ref, zon_ref, mer_ref, v_ref,
    ob_ref, edge_ref, zb_ref, mb_ref, count_ref, edge_count_ref,
    f_ref, h3_ref, wo_ref, ho_ref,
):
    lane = lanes()
    level = lax.broadcasted_iota(jnp.int32, (8, LANES), 0)
    polar = is_polar(lat_blocks, 64, counts_ref.shape[0] // 2)

    @pl.when(polar)
    def _():
        count = jnp.zeros((8, LANES), jnp.int32)
        for row in range(64):
            value = row_count(counts_ref, row, 64, lat_blocks)
            count = jnp.where(jnp.bitwise_and(lane, 63) == row, value, count)
        count_ref[...] = count
        count = jnp.zeros((8, LANES), jnp.int32)
        for side in range(2):
            for slot, (_, distance) in enumerate(EDGE_SLOTS):
                value = row_count(counts_ref, edge_row(side, distance), 64, lat_blocks)
                place = 8 * (len(EDGE_SLOTS) * side + slot)
                count = jnp.where(lane >= place, value, count)
        edge_count_ref[...] = count

    @pl.when(jnp.logical_not(polar))
    def _():
        count_ref[...] = jnp.zeros((8, LANES), jnp.int32)
        edge_count_ref[...] = jnp.zeros((8, LANES), jnp.int32)

    @pl.when(polar)
    def _():
        count = count_ref[...]
        stream = Stream(group_masks(count))
        scale = undo(count)

        def winds(chunk, state):
            for u in range(8):
                i = 8 * chunk + u
                state, tile = stream.step(state, wind_ref[i])
                wo_ref[i] = tile * scale
            return tuple(state)

        lax.fori_loop(0, 32, winds, tuple(stream.start()))

        def heights(chunk, state):
            for u in range(0, 8, 2):
                i = 8 * chunk + u
                low = height_ref[pl.ds(pl.multiple_of(4 * i, 8), 8), :]
                high = height_ref[pl.ds(pl.multiple_of(4 * i + 448, 8), 8), :]
                pair = jnp.where(level < 4, low, pltpu.roll(high, 4, 0))
                state, tile = stream.step(state, pair)
                ho_ref[i] = tile * scale
                pair = jnp.where(level < 4, pltpu.roll(low, 4, 0), high)
                state, tile = stream.step(state, pair)
                ho_ref[i + 1] = tile * scale
            return tuple(state)

        lax.fori_loop(0, 18, heights, tuple(stream.start()))
        wo = wo_ref.reshape(wo_ref.shape[0] * 8, LANES)
        ho = ho_ref.reshape(ho_ref.shape[0] * 8, LANES)
        for f in range(3):
            for q in range(4):
                for t in range(2):
                    if f < 2:
                        tall = wo[pl.ds(8 * (MAXP + LANES * t) + 4 * f + q, LANES, stride=8), :]
                    else:
                        tall = ho[pl.ds(8 * MAXP * (1 + t) + q + 4 * t, LANES, stride=8), :]
                    f_ref[f, t, pl.ds(LANES * q, LANES), :] = tall.T

    @pl.when(jnp.logical_not(polar))
    def _():
        for f in range(3):
            for l in range(8):
                for t in range(2):
                    f_ref[f, t, pl.ds(64 * l, 64), :] = x_ref[f, l, :, LANES * t : LANES * (t + 1)]

    def keep_edge(slot, field, distance):
        for side in range(2):
            for t in range(2):
                place = pl.ds(edge_row(side, distance), 8, stride=64)
                edge_ref[side, slot, :, pl.ds(LANES * t, LANES)] = f_ref[field, t, place, :]

    for d in range(4):
        keep_edge(d, 0, d)
        keep_edge(4 + d, 1, d)
    keep_edge(8, 2, 0)
    for l in range(8):
        zb_ref[l] = jnp.broadcast_to(zon_ref[l : l + 1, :], (LANES, 64)).T
        mb_ref[l] = jnp.broadcast_to(mer_ref[l : l + 1, :], (LANES, 64)).T

    def keep_heights():
        for d in range(1, 5):
            keep_edge(8 + d, 2, d)

    def write(f, l, value):
        ob_ref[f, l] = value

    stencils(f_ref, h3_ref, v_ref, zb_ref, mb_ref, keep_heights, write)


SIDE = 64
OWN = SIDE - WIDE


def fix_kernel(
    lat_blocks, band,
    ob_ref, inner_ref, wind_ref, height_ref, ra_ref, rb_ref, zb_ref, mb_ref, count_ref, v_ref,
    oe_ref, on_ref, oh_ref, tile_ref, edge_ref,
    f_ref, h3_ref, wz_ref, hz_ref, r_ref, all_ref, sems,
):
    even_lon = is_even("lon")
    level = lax.broadcasted_iota(jnp.int32, (8, LANES), 0)
    polar = is_polar(lat_blocks, 64, band)

    def left(place):
        return jnp.where(even_lon, rb_ref[place, :], ra_ref[place, :])

    def right(place):
        return jnp.where(even_lon, ra_ref[place, :], rb_ref[place, :])

    for i in range(WIDE):
        wz_ref[MAXP + i] = left(pl.ds(8 * i, 8))
        wz_ref[MAXP + SIDE + OWN + i] = right(pl.ds(8 * i, 8))
    wz_ref[pl.ds(MAXP + WIDE, OWN)] = wind_ref[pl.ds(0, OWN)]
    wz_ref[pl.ds(MAXP + SIDE, OWN)] = wind_ref[pl.ds(256 - OWN, OWN)]
    for i in range(SIDE):
        if i < WIDE:
            low = left(pl.ds(HEIGHTS + 4 * i, 8))
        else:
            low = height_ref[pl.ds(4 * (i - WIDE), 8), :]
        if i < OWN:
            high = height_ref[pl.ds(4 * (256 - OWN + i) - 4, 8), :]
        else:
            high = right(pl.ds(HEIGHTS + 4 * (i - OWN) - 4, 8))
        hz_ref[MAXP + i] = jnp.where(level < 4, low, high)

    @pl.when(polar)
    def _():
        count = count_ref[...]
        stream = Stream(group_masks(count))
        scale = undo(count)

        def run(ref, base):
            def steps(chunk, state):
                for u in range(8):
                    i = base + 8 * chunk + u
                    state, tile = stream.step(state, ref[MAXP + i])
                    ref[i] = tile * scale
                return tuple(state)

            lax.fori_loop(0, SIDE // 8, steps, tuple(stream.start()))

        run(wz_ref, 0)
        run(wz_ref, SIDE)
        run(hz_ref, 0)

    wz = wz_ref.reshape(wz_ref.shape[0] * 8, LANES)
    hz = hz_ref.reshape(hz_ref.shape[0] * 8, LANES)
    for f in range(3):
        for q in range(4):
            if f < 2:
                tall = wz[pl.ds(8 * MAXP + 4 * f + q, LANES, stride=8), :]
            else:
                parts = [hz[pl.ds(8 * MAXP + q + 4 * s, SIDE, stride=8), :] for s in range(2)]
                tall = jnp.concatenate(parts, axis=0)
            f_ref[f, 0, pl.ds(LANES * q, LANES), :] = tall.T

    lane = lanes()

    def keep_edge(slot, field, distance):
        for side in range(2):
            near = f_ref[field, 0, pl.ds(edge_row(side, distance), 8, stride=64), :]
            west, east = turn(near, -WIDE), turn(near, WIDE)
            first, second = inner_ref[side, slot, :, :LANES], inner_ref[side, slot, :, LANES:]
            edge_ref[side, slot, :, pl.ds(0, LANES)] = jnp.where(lane < 24, west, first)
            edge_ref[side, slot, :, pl.ds(LANES, LANES)] = jnp.where(lane >= 104, east, second)
            edge_ref[side, slot, :, pl.ds(2 * LANES, LANES)] = jnp.where(lane < 64, east, west)

    for d in range(4):
        keep_edge(d, 0, d)
        keep_edge(4 + d, 1, d)
    keep_edge(8, 2, 0)

    def keep_heights():
        for d in range(1, 5):
            keep_edge(8 + d, 2, d)

    def write(f, l, value):
        r_ref[f, l] = value

    stencils(f_ref, h3_ref, v_ref, zb_ref, mb_ref, keep_heights, write)
    wide_lane = lax.broadcasted_iota(jnp.int32, (64, LANES), 1)
    copies = []
    for f, out in enumerate((oe_ref, on_ref, oh_ref)):
        for l in range(8):
            near = r_ref[f, l]
            west, east = turn(near, -WIDE), turn(near, WIDE)
            all_ref[f, l, :, :LANES] = jnp.where(wide_lane < 22, west, ob_ref[f, l, :, :LANES])
            all_ref[f, l, :, LANES:] = jnp.where(wide_lane >= 106, east, ob_ref[f, l, :, LANES:])
        copy = pltpu.make_async_copy(
            all_ref.at[f, :, pl.ds(8, 48)], out.at[:, pl.ds(8, 48)], sems.at[f]
        )
        copy.start()
        copies.append(copy)
        tile_ref[f, :, :8] = all_ref[f, :, :8]
        tile_ref[f, :, 8:] = all_ref[f, :, 56:]
    for copy in copies:
        copy.wait()


def mixing(v_ref):
    level = lax.broadcasted_iota(jnp.int32, (8, LANES), 0)
    columns = []
    for k in range(8):
        column = jnp.full((8, LANES), v_ref[k, 0], jnp.float32)
        for l in range(1, 8):
            column = jnp.where(level == l, v_ref[k, l], column)
        columns.append(column)
    return columns


def mix(columns, height):
    tiles = []
    for t in range(height.shape[-1] // LANES):
        tile = height[..., t * LANES : (t + 1) * LANES]
        total = None
        for k, column in enumerate(columns):
            term = column * jnp.broadcast_to(tile[..., k : k + 1, :], tile.shape)
            total = term if total is None else total + term
        tiles.append(total)
    return jnp.concatenate(tiles, axis=-1)


def wide(column):
    return jnp.concatenate([column] * (SPAN // LANES), axis=-1)


def finish_kernel(
    lat_blocks,
    edge_ref, tile_ref, ga_ref, gb_ref, zon_ref, mer_ref, v_ref, ie_ref, in_ref, ih_ref,
    oe_ref, on_ref, oh_ref,
    ob_ref, sems,
):
    position = lax.axis_index("lat")
    even_lat = is_even("lat")
    lane = lanes()
    columns = mixing(v_ref)
    copies = []
    for side in range(2):
        top = side == 0
        sense = 1.0 if top else -1.0
        pole = position == (0 if top else lat_blocks - 1)
        turned = jnp.where(pole, -1.0, 1.0)

        def ghost_tile(place):
            a, b = ga_ref[pl.ds(8 * place, 8)], gb_ref[pl.ds(8 * place, 8)]
            return jnp.where(even_lat, b, a) if top else jnp.where(even_lat, a, b)

        pack = ghost_tile(2 * len(EDGE_SLOTS))

        def ghost(field, distance):
            slot = EDGE_SLOTS.index((field, distance))
            third = turn(pack, -REACH - 2 * REACH * slot)
            row = jnp.concatenate([ghost_tile(2 * slot), ghost_tile(2 * slot + 1), third], axis=-1)
            return row * turned if field == 1 else row

        e = {d: edge_ref[side, d] for d in range(4)}
        n = {d: edge_ref[side, 4 + d] for d in range(4)}
        h = {0: edge_ref[side, 8]}
        h2 = {d: edge_ref[side, 8 + d] for d in range(1, 5)}
        for d in range(2):
            e[-1 - d] = ghost(0, d)
            h[-1 - d] = ghost(2, d)
        for d in range(3):
            n[-1 - d] = ghost(1, d)
        for d in (-2, -1, 0):
            slope = sense * (n[d + 1] - n[d - 1])
            h2[d] = mix(columns, h[d] + gravity_weight * (zonal(e[d]) + slope))
        e1, n1 = {}, {}
        for d in range(-1, 4):
            e1[d] = e[d] + divergence_weight * zonal(h2[d])
            n1[d] = n[d] + (divergence_weight * sense) * (h2[d + 1] - h2[d - 1])
        mer_ghost = wide(jnp.where(lane < LANES // 2, turn(pack, LANES // 2), pack))

        def coefficient(ref, d):
            row = d if top else 63 - d
            return jnp.broadcast_to(ref[:, row : row + 1], (8, SPAN))

        zon = {d: coefficient(zon_ref, d) for d in range(3)}
        mer = {d: coefficient(mer_ref, d) for d in range(4)}
        for f, field in enumerate((e1, n1, h2)):
            mer[-1] = mer_ghost if f == 0 else mer_ghost * turned
            ob_ref[f, side] = tile_ref[f, :, 8 * side : 8 * side + 8]
            for d in range(3):
                slope = mer[d + 1] * field[d + 1] - mer[d - 1] * field[d - 1]
                value = field[d] + zon[d] * zonal(field[d]) + sense * slope
                ob_ref[f, side, :, d if top else 7 - d] = value[:, : 2 * LANES]
            out = (oe_ref, on_ref, oh_ref)[f]
            copy = pltpu.make_async_copy(
                ob_ref.at[f, side], out.at[:, pl.ds(56 * side, 8)], sems.at[f, side]
            )
            copy.start()
            copies.append(copy)
    for copy in copies:
        copy.wait()


def body(
    lat_blocks, lon_blocks, axes,
    east_adjoint, north_adjoint, height_adjoint,
    zonal_courant, meridional_courant, vertical_inverse, pass_counts,
):
    f32 = jnp.float32
    fields = tuple(
        pltpu.with_memory_space_constraint(x, pltpu.HBM)
        for x in (east_adjoint, north_adjoint, height_adjoint)
    )

    def in_vmem(*dims):
        return pltpu.VMEM(dims, f32)

    def params():
        return pltpu.CompilerParams(vmem_limit_bytes=40 * 1024 * 1024)

    lon_a, lon_b, winds, heights, edge_rows, local = pl.pallas_call(
        pack_kernel,
        out_shape=(
            in_vmem(PAYLOAD, LANES), in_vmem(PAYLOAD, LANES),
            in_vmem(256, 8, LANES), in_vmem(1024, LANES), in_vmem(256, LANES),
            in_vmem(3, 8, 64, 256),
        ),
        in_specs=[HBM] * 3,
        out_specs=(VMEM,) * 6,
        scratch_shapes=[pltpu.VMEM((LANES, 256), f32), pltpu.SemaphoreType.DMA((3,))],
        compiler_params=params(),
        name="pack",
    )(*fields)

    def other_lon(o):
        return (((o + 1) ^ 1) - 1) % lon_blocks

    recv_a = lax.ppermute(lon_a, "lon", [(o, o ^ 1) for o in range(lon_blocks)])
    recv_b = lax.ppermute(lon_b, "lon", [(o, other_lon(o)) for o in range(lon_blocks)])

    by_row = in_vmem(8, 64, LANES)
    by_count = pltpu.VMEM((8, LANES), jnp.int32)
    inner, inner_edges, zon_wide, mer_wide, counts, edge_counts = pl.pallas_call(
        lambda *refs: interior_kernel(lat_blocks, *refs),
        out_shape=(
            in_vmem(3, 8, 64, 256), in_vmem(2, 13, 8, 256), by_row, by_row, by_count, by_count
        ),
        in_specs=[VMEM] * 3 + [SMEM, VMEM, VMEM, SMEM],
        out_specs=(VMEM,) * 6,
        scratch_shapes=[
            pltpu.VMEM((3, 2, 512, LANES), f32),
            pltpu.VMEM((2, 8, 64, LANES), f32),
            pltpu.VMEM((272, 8, LANES), f32),
            pltpu.VMEM((160, 8, LANES), f32),
        ],
        compiler_params=params(),
        cost_estimate=pl.CostEstimate(flops=100000000, bytes_accessed=20000000, transcendentals=0),
        name="interior",
    )(
        local, winds, heights, pass_counts, zonal_courant, meridional_courant, vertical_inverse
    )

    places = 8 * (2 * len(EDGE_SLOTS) + 1)
    lat_a, lat_b = pl.pallas_call(
        edge_kernel,
        out_shape=(in_vmem(places, LANES),) * 2,
        in_specs=[VMEM] * 5,
        out_specs=(VMEM,) * 2,
        scratch_shapes=[pltpu.VMEM((304, LANES), f32), pltpu.VMEM((264, LANES), f32)],
        compiler_params=params(),
        name="edge",
    )(edge_rows, recv_a, recv_b, edge_counts, meridional_courant)

    def index(a, o):
        return o * lat_blocks + a if axes[0] == "lon" else a * lon_blocks + o

    def other_lat(a, o):
        if a in (0, lat_blocks - 1):
            return a, (o + lon_blocks // 2) % lon_blocks
        return ((a + 1) ^ 1) - 1, o

    pairs = [
        (index(a, o), index(*other_lat(a, o))) for a in range(lat_blocks) for o in range(lon_blocks)
    ]
    ghost_a = lax.ppermute(lat_a, "lat", [(a, a ^ 1) for a in range(lat_blocks)])
    ghost_b = lax.ppermute(lat_b, axes, pairs)

    block = jax.ShapeDtypeStruct(east_adjoint.shape, f32)
    *results, tiles, edges = pl.pallas_call(
        lambda *refs: fix_kernel(lat_blocks, pass_counts.shape[0] // 2, *refs),
        out_shape=(block,) * 3 + (in_vmem(3, 8, 16, 256), in_vmem(2, 13, 8, SPAN)),
        in_specs=[VMEM] * 9 + [SMEM],
        out_specs=(HBM,) * 3 + (VMEM,) * 2,
        scratch_shapes=[
            pltpu.VMEM((3, 1, 512, LANES), f32),
            pltpu.VMEM((1, 8, 64, LANES), f32),
            pltpu.VMEM((MAXP + 2 * SIDE, 8, LANES), f32),
            pltpu.VMEM((MAXP + SIDE, 8, LANES), f32),
            pltpu.VMEM((3, 8, 64, LANES), f32),
            pltpu.VMEM((3, 8, 64, 256), f32),
            pltpu.SemaphoreType.DMA((3,)),
        ],
        compiler_params=params(),
        cost_estimate=pl.CostEstimate(flops=50000000, bytes_accessed=10000000, transcendentals=0),
        name="fix",
    )(
        inner, inner_edges, winds, heights, recv_a, recv_b,
        zon_wide, mer_wide, counts, vertical_inverse,
    )

    return pl.pallas_call(
        lambda *refs: finish_kernel(lat_blocks, *refs),
        out_shape=(block,) * 3,
        in_specs=[VMEM] * 6 + [SMEM] + [HBM] * 3,
        out_specs=(HBM,) * 3,
        input_output_aliases={7: 0, 8: 1, 9: 2},
        scratch_shapes=[
            pltpu.VMEM((3, 2, 8, 8, 256), f32),
            pltpu.SemaphoreType.DMA((3, 2)),
        ],
        compiler_params=params(),
        name="finish",
    )(
        edges, tiles, ghost_a, ghost_b, zonal_courant, meridional_courant, vertical_inverse, *results
    )


def solution(mesh):
    sizes = dict(mesh.shape)
    axes = tuple(mesh.axis_names)
    spread_out = P(None, "lat", "lon")
    return jax.shard_map(
        lambda *args: body(sizes["lat"], sizes["lon"], axes, *args),
        mesh=mesh,
        in_specs=(spread_out,) * 3 + (P(None, "lat"), P(None, "lat"), P(), P()),
        out_specs=(spread_out,) * 3,
        check_vma=False,
    )
```

```python
import jax
import jax.numpy as jnp
from jax import lax
from jax.experimental import pallas as pl
from jax.experimental.pallas import tpu as pltpu
from jax.sharding import PartitionSpec as P

MAXP = 16
REACH = 3
WIDE = MAXP + REACH
LANES = 128
SPAN = 3 * LANES
SHARE = 33

gravity_weight = 0.3
divergence_weight = 0.3

VMEM = pl.BlockSpec(memory_space=pltpu.VMEM)
SMEM = pl.BlockSpec(memory_space=pltpu.SMEM)
HBM = pl.BlockSpec(memory_space=pltpu.HBM)

EDGE_SLOTS = ((0, 0), (0, 1), (1, 0), (1, 1), (1, 2), (2, 0), (2, 1))


HEIGHTS = 8 * WIDE + 4
EDGES = 8 * WIDE + 88
PAYLOAD = EDGES + 24


def lanes():
    return lax.broadcasted_iota(jnp.int32, (8, LANES), 1)


def turn(values, steps):
    return pltpu.roll(values, steps % values.shape[-1], values.ndim - 1)


def zonal(values):
    return turn(values, -1) - turn(values, 1)


def is_even(axis):
    return lax.rem(lax.axis_index(axis), 2) == 0


def row_count(counts_ref, row, rows, lat_blocks):
    band = counts_ref.shape[0] // 2
    blocks = band // rows
    position = lax.axis_index("lat")
    north = position < blocks
    south = position >= lat_blocks - blocks
    place = jnp.where(north, position, jnp.where(south, position - lat_blocks + 2 * blocks, 0))
    return jnp.where(north | south, counts_ref[place * rows + row], 0)


def undo(count):
    power = jnp.left_shift(1, MAXP - count).astype(jnp.float32)
    return power * power * (2.0 ** (-2 * MAXP))


class Stream:
    GROUPS = (1, 1, 2, 4, 8)

    def __init__(self, masks):
        self.masks = masks

    def start(self):
        zero = jnp.zeros((8, LANES), jnp.float32)
        return [zero] * (2 * MAXP + sum(self.GROUPS))

    def step(self, state, tile):
        state = list(state)
        at, later = 0, 2 * MAXP
        for mask, size in zip(self.masks, self.GROUPS):
            entered = tile
            for _ in range(size):
                half = state[at] + tile
                state[at], tile = tile, state[at + 1] + half
                state[at + 1] = half
                at += 2
            delayed = state[later]
            state[later : later + size] = state[later + 1 : later + size] + [entered]
            later += size
            tile = jnp.where(mask, tile, delayed)
        return state, tile


def group_masks(count):
    rest = count - 1
    bits = [jnp.bitwise_and(jnp.right_shift(rest, b), 1) == 1 for b in range(4)]
    used = count > 0
    return [used] + [used & bit for bit in bits]


def pack_kernel(
    e_hbm, n_hbm, h_hbm, a_ref, b_ref, wind_ref, height_ref, edge_ref, x_ref, t_ref, sems
):
    copies = []
    for f, ref in enumerate((e_hbm, n_hbm, h_hbm)):
        for t in range(2):
            copy = pltpu.make_async_copy(
                ref.at[:, :, pl.ds(LANES * t, LANES)],
                x_ref.at[f, t].reshape(8, 64, LANES),
                sems.at[f, t],
            )
            copy.start()
            copies.append(copy)
    winds = wind_ref.reshape(256 * 8, LANES)
    for f in range(3):
        for t in range(2):
            copies[2 * f + t].wait()
            for q in range(4):
                turned = x_ref[f, t, pl.ds(LANES * q, LANES), :].T
                if f < 2:
                    winds[pl.ds(1024 * t + 4 * f + q, LANES, stride=8), :] = turned
                else:
                    height_ref[pl.ds(512 * t + q, LANES, stride=4), :] = turned
    for side in range(2):
        for slot, (field, distance) in enumerate(EDGE_SLOTS):
            row = 63 - distance if side else distance
            place = 8 * (len(EDGE_SLOTS) * side + slot)
            for t in range(2):
                t_ref[t, pl.ds(place, 8), :] = x_ref[field, t, pl.ds(row, 8, stride=64), :]
    for t in range(2):
        t_ref[t, pl.ds(112, 16), :] = jnp.zeros((16, LANES), jnp.float32)
        edge_ref[pl.ds(LANES * t, LANES), :] = t_ref[t].T
    even = is_even("lon")
    last = 256 - WIDE
    for ref, right in ((a_ref, even), (b_ref, jnp.logical_not(even))):
        first = jnp.where(right, last, 0)
        ref[pl.ds(0, 8 * WIDE), :] = wind_ref[pl.ds(first, WIDE)].reshape(8 * WIDE, LANES)
        ref[pl.ds(HEIGHTS, 4 * WIDE), :] = jnp.where(
            right, height_ref[pl.ds(4 * last, 4 * WIDE), :], height_ref[pl.ds(0, 4 * WIDE), :]
        )
        ref[pl.ds(EDGES, WIDE), :] = jnp.where(
            right, edge_ref[pl.ds(last, WIDE), :], edge_ref[pl.ds(0, WIDE), :]
        )


def edge_kernel(
    turned_ref, ra_ref, rb_ref, count_ref, mer_ref, a_ref, b_ref, own_ref, z_ref, o_ref
):
    even_lon = is_even("lon")
    even_lat = is_even("lat")
    lane = lanes()
    halo = pl.ds(EDGES, WIDE)
    z_ref[pl.ds(24, 256), :] = turned_ref[...]
    z_ref[pl.ds(24 - WIDE, WIDE), :] = jnp.where(even_lon, rb_ref[halo, :], ra_ref[halo, :])
    z_ref[pl.ds(280, WIDE), :] = jnp.where(even_lon, ra_ref[halo, :], rb_ref[halo, :])
    z_ref[pl.ds(280 + WIDE, 5), :] = jnp.zeros((5, LANES), jnp.float32)
    count = count_ref[...]
    stream = Stream(group_masks(count))
    scale = undo(count)
    state = stream.start()
    for i in range(SHARE + 2 * MAXP):
        state, tile = stream.step(state, z_ref[pl.ds(24 - WIDE + i, 8, stride=SHARE), :])
        if i >= 2 * MAXP:
            o_ref[pl.ds(i - 2 * MAXP, 8, stride=SHARE), :] = tile * scale
    first = o_ref[pl.ds(REACH, LANES), :].T
    second = o_ref[pl.ds(REACH + LANES, LANES), :].T
    o_ref[pl.ds(REACH, REACH), :] = o_ref[pl.ds(REACH + 2 * LANES, REACH), :]
    third = o_ref[pl.ds(0, LANES), :].T
    packs = []
    for side in range(2):
        sense = -1.0 if side else 1.0

        def row(field, distance):
            slot = EDGE_SLOTS.index((field, distance))
            place = 8 * (len(EDGE_SLOTS) * side + slot)
            own = slice(place, place + 8)
            return jnp.concatenate([first[own], second[own], turn(third[own], -REACH)], axis=-1)

        e0, e1, n0, n1, n2, h0, h1 = (row(*slot) for slot in EDGE_SLOTS)
        outer = h0 + gravity_weight * (zonal(e0) + sense * n1)
        inner = h1 + gravity_weight * (zonal(e1) + sense * (n2 - n0))
        own_ref[side] = outer
        at = 63 if side else 0
        pack = jnp.broadcast_to(mer_ref[:, at : at + 1], (8, LANES))
        out = []
        for slot, value in enumerate((outer, inner, e0, n0)):
            out += [value[:, :LANES], value[:, LANES : 2 * LANES]]
            start = 2 * REACH * slot
            inside = (lane >= start) & (lane < start + 2 * REACH)
            pack = jnp.where(inside, turn(value[:, 2 * LANES :], REACH + start), pack)
        packs.append(out + [pack])
    for place, (top, bottom) in enumerate(zip(*packs)):
        a_ref[pl.ds(8 * place, 8)] = jnp.where(even_lat, bottom, top)
        b_ref[pl.ds(8 * place, 8)] = jnp.where(even_lat, top, bottom)


def following(rows):
    count = rows.shape[0]
    return pltpu.roll(rows, count - 1, 0) - pltpu.roll(rows, 1, 0)


def is_polar(lat_blocks, rows, band):
    position = lax.axis_index("lat")
    return (position < band // rows) | (position >= lat_blocks - band // rows)


def stencils(f_ref, v_ref, zb_ref, mb_ref, keep_heights, write):
    tiles = f_ref.shape[1]

    def whole(f, start, rows):
        place = pl.ds(start, rows)
        return jnp.concatenate([f_ref[f, t, place, :] for t in range(tiles)], axis=-1)

    def weight(k, l):
        return jnp.concatenate([v_ref[k, l]] * tiles, axis=-1)

    for first in range(0, 64, 8):
        old = []
        for l in range(8):
            start = 64 * l + first
            north = whole(1, start, 8)
            above = whole(1, start - 1, 8) if start else pltpu.roll(north, 1, 0)
            below = whole(1, start + 1, 8) if start < 512 - 8 else pltpu.roll(north, 7, 0)
            slope = zonal(whole(0, start, 8)) + (below - above)
            old.append(whole(2, start, 8) + gravity_weight * slope)
        for l in range(8):
            total = weight(0, l) * old[0]
            for k in range(1, 8):
                total = total + weight(k, l) * old[k]
            for t in range(tiles):
                place = pl.ds(64 * l + first, 8)
                f_ref[2, t, place, :] = total[:, LANES * t : LANES * (t + 1)]
    keep_heights()
    for l in range(8):
        h2 = whole(2, 64 * l, 64)
        h2_zonal = zonal(h2)
        e1 = whole(0, 64 * l, 64) + divergence_weight * h2_zonal
        n1 = whole(1, 64 * l, 64) + divergence_weight * following(h2)
        zon = jnp.concatenate([zb_ref[l]] * tiles, axis=-1)
        mer = jnp.concatenate([mb_ref[l]] * tiles, axis=-1)
        for f, field in enumerate((e1, n1, h2)):
            slope = h2_zonal if f == 2 else zonal(field)
            write(f, l, field + zon * slope + following(mer * field))


def edge_row(side, distance):
    return 63 - distance if side else distance


def interior_kernel(
    lat_blocks,
    _, wind_ref, height_ref, counts_ref, zon_ref, mer_ref, v_ref,
    f_ref, ob_ref, edge_ref, zb_ref, mb_ref, count_ref, edge_count_ref, vb_ref, vc_ref,
    wo_ref, ho_ref,
):
    lane = lanes()
    level = lax.broadcasted_iota(jnp.int32, (8, LANES), 0)
    polar = is_polar(lat_blocks, 64, counts_ref.shape[0] // 2)

    @pl.when(polar)
    def _():
        count = jnp.zeros((8, LANES), jnp.int32)
        for row in range(64):
            value = row_count(counts_ref, row, 64, lat_blocks)
            count = jnp.where(jnp.bitwise_and(lane, 63) == row, value, count)
        count_ref[...] = count
        count = jnp.zeros((8, LANES), jnp.int32)
        for side in range(2):
            for slot, (_, distance) in enumerate(EDGE_SLOTS):
                value = row_count(counts_ref, edge_row(side, distance), 64, lat_blocks)
                place = 8 * (len(EDGE_SLOTS) * side + slot)
                count = jnp.where(lane >= place, value, count)
        edge_count_ref[...] = count

    @pl.when(jnp.logical_not(polar))
    def _():
        count_ref[...] = jnp.zeros((8, LANES), jnp.int32)
        edge_count_ref[...] = jnp.zeros((8, LANES), jnp.int32)

    @pl.when(polar)
    def _():
        count = count_ref[...]
        stream = Stream(group_masks(count))
        scale = undo(count)

        def winds(chunk, state):
            for u in range(8):
                i = 8 * chunk + u
                state, tile = stream.step(state, wind_ref[i])
                wo_ref[i] = tile * scale
            return tuple(state)

        lax.fori_loop(0, 32, winds, tuple(stream.start()))

        def heights(chunk, state):
            for u in range(0, 8, 2):
                i = 8 * chunk + u
                low = height_ref[pl.ds(pl.multiple_of(4 * i, 8), 8), :]
                high = height_ref[pl.ds(pl.multiple_of(4 * i + 448, 8), 8), :]
                pair = jnp.where(level < 4, low, pltpu.roll(high, 4, 0))
                state, tile = stream.step(state, pair)
                ho_ref[i] = tile * scale
                pair = jnp.where(level < 4, pltpu.roll(low, 4, 0), high)
                state, tile = stream.step(state, pair)
                ho_ref[i + 1] = tile * scale
            return tuple(state)

        lax.fori_loop(0, 18, heights, tuple(stream.start()))
        wo = wo_ref.reshape(wo_ref.shape[0] * 8, LANES)
        ho = ho_ref.reshape(ho_ref.shape[0] * 8, LANES)
        for f in range(3):
            for q in range(4):
                for t in range(2):
                    if f < 2:
                        tall = wo[pl.ds(8 * (MAXP + LANES * t) + 4 * f + q, LANES, stride=8), :]
                    else:
                        tall = ho[pl.ds(8 * MAXP * (1 + t) + q + 4 * t, LANES, stride=8), :]
                    f_ref[f, t, pl.ds(LANES * q, LANES), :] = tall.T

    def keep_edge(slot, field, distance):
        for side in range(2):
            for t in range(2):
                place = pl.ds(edge_row(side, distance), 8, stride=64)
                edge_ref[side, slot, :, pl.ds(LANES * t, LANES)] = f_ref[field, t, place, :]

    for d in range(4):
        keep_edge(d, 0, d)
        keep_edge(4 + d, 1, d)
    for k in range(8):
        for l in range(8):
            vb_ref[k, l] = jnp.full((8, LANES), v_ref[k, l], jnp.float32)
    for k, column in enumerate(mixing(v_ref)):
        vc_ref[k] = column
    for l in range(8):
        zb_ref[l] = jnp.broadcast_to(zon_ref[l : l + 1, :], (LANES, 64)).T
        mb_ref[l] = jnp.broadcast_to(mer_ref[l : l + 1, :], (LANES, 64)).T

    def keep_heights():
        for d in range(1, 5):
            keep_edge(7 + d, 2, d)

    def write(f, l, value):
        for t in range(2):
            ob_ref[f, t, pl.ds(64 * l, 64), :] = value[:, LANES * t : LANES * (t + 1)]

    stencils(f_ref, vb_ref, zb_ref, mb_ref, keep_heights, write)


SIDE = 64
OWN = SIDE - WIDE


def fix_kernel(
    lat_blocks, band,
    ob_ref, inner_ref, wind_ref, height_ref, ra_ref, rb_ref, zb_ref, mb_ref, count_ref, v_ref,
    all_ref, edge_ref,
    f_ref, wz_ref, hz_ref,
):
    even_lon = is_even("lon")
    level = lax.broadcasted_iota(jnp.int32, (8, LANES), 0)
    polar = is_polar(lat_blocks, 64, band)

    def left(place):
        return jnp.where(even_lon, rb_ref[place, :], ra_ref[place, :])

    def right(place):
        return jnp.where(even_lon, ra_ref[place, :], rb_ref[place, :])

    for i in range(WIDE):
        wz_ref[MAXP + i] = left(pl.ds(8 * i, 8))
        wz_ref[MAXP + SIDE + OWN + i] = right(pl.ds(8 * i, 8))
    wz_ref[pl.ds(MAXP + WIDE, OWN)] = wind_ref[pl.ds(0, OWN)]
    wz_ref[pl.ds(MAXP + SIDE, OWN)] = wind_ref[pl.ds(256 - OWN, OWN)]
    for i in range(SIDE):
        if i < WIDE:
            low = left(pl.ds(HEIGHTS + 4 * i, 8))
        else:
            low = height_ref[pl.ds(4 * (i - WIDE), 8), :]
        if i < OWN:
            high = height_ref[pl.ds(4 * (256 - OWN + i) - 4, 8), :]
        else:
            high = right(pl.ds(HEIGHTS + 4 * (i - OWN) - 4, 8))
        hz_ref[MAXP + i] = jnp.where(level < 4, low, high)

    @pl.when(polar)
    def _():
        count = count_ref[...]
        stream = Stream(group_masks(count))
        scale = undo(count)

        def run(ref, base):
            def steps(chunk, state):
                for u in range(8):
                    i = base + 8 * chunk + u
                    state, tile = stream.step(state, ref[MAXP + i])
                    ref[i] = tile * scale
                return tuple(state)

            lax.fori_loop(0, SIDE // 8, steps, tuple(stream.start()))

        run(wz_ref, 0)
        run(wz_ref, SIDE)
        run(hz_ref, 0)

    wz = wz_ref.reshape(wz_ref.shape[0] * 8, LANES)
    hz = hz_ref.reshape(hz_ref.shape[0] * 8, LANES)
    for f in range(3):
        for q in range(4):
            if f < 2:
                tall = wz[pl.ds(8 * MAXP + 4 * f + q, LANES, stride=8), :]
            else:
                parts = [hz[pl.ds(8 * MAXP + q + 4 * s, SIDE, stride=8), :] for s in range(2)]
                tall = jnp.concatenate(parts, axis=0)
            f_ref[f, 0, pl.ds(LANES * q, LANES), :] = tall.T

    lane = lanes()

    def keep_edge(slot, field, distance):
        for side in range(2):
            near = f_ref[field, 0, pl.ds(edge_row(side, distance), 8, stride=64), :]
            west, east = turn(near, -WIDE), turn(near, WIDE)
            first, second = inner_ref[side, slot, :, :LANES], inner_ref[side, slot, :, LANES:]
            edge_ref[side, slot, :, pl.ds(0, LANES)] = jnp.where(lane < 24, west, first)
            edge_ref[side, slot, :, pl.ds(LANES, LANES)] = jnp.where(lane >= 104, east, second)
            edge_ref[side, slot, :, pl.ds(2 * LANES, LANES)] = jnp.where(lane < 64, east, west)

    for d in range(4):
        keep_edge(d, 0, d)
        keep_edge(4 + d, 1, d)

    def keep_heights():
        for d in range(1, 5):
            keep_edge(7 + d, 2, d)

    wide_lane = lax.broadcasted_iota(jnp.int32, (64, LANES), 1)

    def write(f, l, near):
        west, east = turn(near, -WIDE), turn(near, WIDE)
        rows = pl.ds(64 * l, 64)
        all_ref[f, 0, rows, :] = jnp.where(wide_lane < 22, west, ob_ref[f, 0, rows, :])
        all_ref[f, 1, rows, :] = jnp.where(wide_lane >= 106, east, ob_ref[f, 1, rows, :])

    stencils(f_ref, v_ref, zb_ref, mb_ref, keep_heights, write)


def mixing(v_ref):
    level = lax.broadcasted_iota(jnp.int32, (8, LANES), 0)
    columns = []
    for k in range(8):
        column = jnp.full((8, LANES), v_ref[k, 0], jnp.float32)
        for l in range(1, 8):
            column = jnp.where(level == l, v_ref[k, l], column)
        columns.append(column)
    return columns


def mix(columns, height):
    tiles = []
    for t in range(height.shape[-1] // LANES):
        tile = height[..., t * LANES : (t + 1) * LANES]
        total = None
        for k, column in enumerate(columns):
            term = column * jnp.broadcast_to(tile[..., k : k + 1, :], tile.shape)
            total = term if total is None else total + term
        tiles.append(total)
    return jnp.concatenate(tiles, axis=-1)


def wide(column):
    return jnp.concatenate([column] * (SPAN // LANES), axis=-1)


def finish_kernel(
    lat_blocks,
    edge_ref, own_ref, all_ref, gb_ref, ga_ref, zon_ref, mer_ref, v_ref,
    oe_ref, on_ref, oh_ref,
    ob_ref, sems, edge_sems,
):
    outs = (oe_ref, on_ref, oh_ref)
    copies = []
    for f, out in enumerate(outs):
        for t in range(2):
            copy = pltpu.make_async_copy(
                all_ref.at[f, t].reshape(8, 64, LANES).at[:, pl.ds(8, 48)],
                out.at[:, pl.ds(8, 48), pl.ds(LANES * t, LANES)],
                sems.at[f, t],
            )
            copy.start()
            copies.append(copy)
    position = lax.axis_index("lat")
    even_lat = is_even("lat")
    lane = lanes()
    columns = [v_ref[k] for k in range(8)]
    for side in range(2):
        top = side == 0
        sense = 1.0 if top else -1.0
        pole = position == (0 if top else lat_blocks - 1)
        turned = jnp.where(pole, -1.0, 1.0)

        def ghost_tile(place):
            a, b = ga_ref[pl.ds(8 * place, 8)], gb_ref[pl.ds(8 * place, 8)]
            return jnp.where(even_lat, b, a) if top else jnp.where(even_lat, a, b)

        pack = ghost_tile(8)

        def ghost(slot):
            third = turn(pack, -REACH - 2 * REACH * slot)
            return jnp.concatenate([ghost_tile(2 * slot), ghost_tile(2 * slot + 1), third], axis=-1)

        e = {d: edge_ref[side, d] for d in range(4)}
        n = {d: edge_ref[side, 4 + d] for d in range(4)}
        h2 = {d: edge_ref[side, 7 + d] for d in range(1, 5)}
        e[-1] = ghost(2)
        n[-1] = ghost(3) * turned
        h2[-2] = mix(columns, ghost(1))
        h2[-1] = mix(columns, ghost(0) + (gravity_weight * sense) * n[0])
        h2[0] = mix(columns, own_ref[side] - (gravity_weight * sense) * n[-1])
        e1, n1, h2_zonal = {}, {}, {}
        for d in range(-1, 4):
            h2_zonal[d] = zonal(h2[d])
            e1[d] = e[d] + divergence_weight * h2_zonal[d]
            n1[d] = n[d] + (divergence_weight * sense) * (h2[d + 1] - h2[d - 1])
        mer_ghost = wide(jnp.where(lane < LANES // 2, turn(pack, LANES // 2), pack))

        def coefficient(ref, d):
            row = edge_row(side, d)
            return wide(jnp.broadcast_to(ref[:, row : row + 1], (8, LANES)))

        zon = {d: coefficient(zon_ref, d) for d in range(3)}
        mer = {d: coefficient(mer_ref, d) for d in range(4)}
        for f, field in enumerate((e1, n1, h2)):
            mer[-1] = mer_ghost if f == 0 else mer_ghost * turned
            flow = {d: mer[d] * field[d] for d in range(-1, 4)}
            for t in range(2):
                for l in range(8):
                    ob_ref[f, side, t, pl.ds(8 * l, 8), :] = all_ref[
                        f, t, pl.ds(64 * l + 56 * side, 8), :
                    ]
            for d in range(3):
                slope = h2_zonal[d] if f == 2 else zonal(field[d])
                value = field[d] + zon[d] * slope + sense * (flow[d + 1] - flow[d - 1])
                for t in range(2):
                    ob_ref[f, side, t, pl.ds(d if top else 7 - d, 8, stride=8), :] = value[
                        :, LANES * t : LANES * (t + 1)
                    ]
    for side in range(2):
        for f, out in enumerate(outs):
            for t in range(2):
                copy = pltpu.make_async_copy(
                    ob_ref.at[f, side, t].reshape(8, 8, LANES),
                    out.at[:, pl.ds(56 * side, 8), pl.ds(LANES * t, LANES)],
                    edge_sems.at[f, side, t],
                )
                copy.start()
                copies.append(copy)
    for copy in copies:
        copy.wait()


def body(
    lat_blocks, lon_blocks, axes,
    east_adjoint, north_adjoint, height_adjoint,
    zonal_courant, meridional_courant, vertical_inverse, pass_counts,
):
    f32 = jnp.float32
    fields = tuple(
        pltpu.with_memory_space_constraint(x, pltpu.HBM)
        for x in (east_adjoint, north_adjoint, height_adjoint)
    )

    def in_vmem(*dims):
        return pltpu.VMEM(dims, f32)

    def params():
        return pltpu.CompilerParams(vmem_limit_bytes=40 * 1024 * 1024)

    lon_a, lon_b, winds, heights, edge_rows, local = pl.pallas_call(
        pack_kernel,
        out_shape=(
            in_vmem(PAYLOAD, LANES), in_vmem(PAYLOAD, LANES),
            in_vmem(256, 8, LANES), in_vmem(1024, LANES), in_vmem(256, LANES),
            in_vmem(3, 2, 512, LANES),
        ),
        in_specs=[HBM] * 3,
        out_specs=(VMEM,) * 6,
        scratch_shapes=[pltpu.VMEM((2, LANES, LANES), f32), pltpu.SemaphoreType.DMA((3, 2))],
        compiler_params=params(),
        name="pack",
    )(*fields)

    def other_lon(o):
        return (((o + 1) ^ 1) - 1) % lon_blocks

    recv_a = lax.ppermute(lon_a, "lon", [(o, o ^ 1) for o in range(lon_blocks)])
    recv_b = lax.ppermute(lon_b, "lon", [(o, other_lon(o)) for o in range(lon_blocks)])

    by_row = in_vmem(8, 64, LANES)
    by_count = pltpu.VMEM((8, LANES), jnp.int32)
    _, inner, inner_edges, zon_wide, mer_wide, counts, edge_counts, weights, columns = pl.pallas_call(
        lambda *refs: interior_kernel(lat_blocks, *refs),
        out_shape=(
            in_vmem(3, 2, 512, LANES), in_vmem(3, 2, 512, LANES), in_vmem(2, 12, 8, 256),
            by_row, by_row, by_count, by_count, in_vmem(8, 8, 8, LANES), in_vmem(8, 8, LANES),
        ),
        in_specs=[VMEM] * 3 + [SMEM, VMEM, VMEM, SMEM],
        out_specs=(VMEM,) * 9,
        input_output_aliases={0: 0},
        scratch_shapes=[
            pltpu.VMEM((272, 8, LANES), f32),
            pltpu.VMEM((160, 8, LANES), f32),
        ],
        compiler_params=params(),
        cost_estimate=pl.CostEstimate(flops=100000000, bytes_accessed=20000000, transcendentals=0),
        name="interior",
    )(
        local, winds, heights, pass_counts, zonal_courant, meridional_courant, vertical_inverse
    )

    lat_a, lat_b, own_edges = pl.pallas_call(
        edge_kernel,
        out_shape=(in_vmem(72, LANES), in_vmem(72, LANES), in_vmem(2, 8, SPAN)),
        in_specs=[VMEM] * 5,
        out_specs=(VMEM,) * 3,
        scratch_shapes=[pltpu.VMEM((304, LANES), f32), pltpu.VMEM((264, LANES), f32)],
        compiler_params=params(),
        name="edge",
    )(edge_rows, recv_a, recv_b, edge_counts, meridional_courant)

    def index(a, o):
        return o * lat_blocks + a if axes[0] == "lon" else a * lon_blocks + o

    def other_lat(a, o):
        if a in (0, lat_blocks - 1):
            return a, (o + lon_blocks // 2) % lon_blocks
        return ((a + 1) ^ 1) - 1, o

    pairs = [
        (index(a, o), index(*other_lat(a, o))) for a in range(lat_blocks) for o in range(lon_blocks)
    ]
    ghost_a = lax.ppermute(lat_a, "lat", [(a, a ^ 1) for a in range(lat_blocks)])
    ghost_b = lax.ppermute(lat_b, axes, pairs)

    block = jax.ShapeDtypeStruct(east_adjoint.shape, f32)
    final, edges = pl.pallas_call(
        lambda *refs: fix_kernel(lat_blocks, pass_counts.shape[0] // 2, *refs),
        out_shape=(in_vmem(3, 2, 512, LANES), in_vmem(2, 12, 8, SPAN)),
        in_specs=[VMEM] * 10,
        out_specs=(VMEM,) * 2,
        scratch_shapes=[
            pltpu.VMEM((3, 1, 512, LANES), f32),
            pltpu.VMEM((MAXP + 2 * SIDE, 8, LANES), f32),
            pltpu.VMEM((MAXP + SIDE, 8, LANES), f32),
        ],
        compiler_params=params(),
        cost_estimate=pl.CostEstimate(flops=50000000, bytes_accessed=10000000, transcendentals=0),
        name="fix",
    )(
        inner, inner_edges, winds, heights, recv_a, recv_b, zon_wide, mer_wide, counts, weights,
    )

    return pl.pallas_call(
        lambda *refs: finish_kernel(lat_blocks, *refs),
        out_shape=(block,) * 3,
        in_specs=[VMEM] * 8,
        out_specs=(HBM,) * 3,
        scratch_shapes=[
            pltpu.VMEM((3, 2, 2, 64, LANES), f32),
            pltpu.SemaphoreType.DMA((3, 2)),
            pltpu.SemaphoreType.DMA((3, 2, 2)),
        ],
        compiler_params=params(),
        name="finish",
    )(
        edges, own_edges, final, ghost_b, ghost_a, zonal_courant, meridional_courant, columns
    )


def solution(mesh):
    sizes = dict(mesh.shape)
    axes = tuple(mesh.axis_names)
    spread_out = P(None, "lat", "lon")
    return jax.shard_map(
        lambda *args: body(sizes["lat"], sizes["lon"], axes, *args),
        mesh=mesh,
        in_specs=(spread_out,) * 3 + (P(None, "lat"), P(None, "lat"), P(), P()),
        out_specs=(spread_out,) * 3,
        check_vma=False,
    )
```

```python
import jax
import jax.numpy as jnp
from jax import lax
from jax.experimental import pallas as pl
from jax.experimental.pallas import tpu as pltpu
from jax.sharding import PartitionSpec as P

MAXP = 16
REACH = 3
WIDE = MAXP + REACH
LANES = 128
SPAN = 3 * LANES
SHARE = 33

gravity_weight = 0.3
divergence_weight = 0.3

VMEM = pl.BlockSpec(memory_space=pltpu.VMEM)
SMEM = pl.BlockSpec(memory_space=pltpu.SMEM)
HBM = pl.BlockSpec(memory_space=pltpu.HBM)

EDGE_SLOTS = ((0, 0), (0, 1), (1, 0), (1, 1), (1, 2), (2, 0), (2, 1))


HEIGHTS = 8 * WIDE + 4
EDGES = 8 * WIDE + 88
PAYLOAD = EDGES + 24


def lanes():
    return lax.broadcasted_iota(jnp.int32, (8, LANES), 1)


def turn(values, steps):
    return pltpu.roll(values, steps % values.shape[-1], values.ndim - 1)


def zonal(values):
    return turn(values, -1) - turn(values, 1)


def is_even(axis):
    return lax.rem(lax.axis_index(axis), 2) == 0


def row_count(counts_ref, row, rows, lat_blocks):
    band = counts_ref.shape[0] // 2
    blocks = band // rows
    position = lax.axis_index("lat")
    north = position < blocks
    south = position >= lat_blocks - blocks
    place = jnp.where(north, position, jnp.where(south, position - lat_blocks + 2 * blocks, 0))
    return jnp.where(north | south, counts_ref[place * rows + row], 0)


def undo(count):
    power = jnp.left_shift(1, MAXP - count).astype(jnp.float32)
    return power * power * (2.0 ** (-2 * MAXP))


class Stream:
    GROUPS = (1, 1, 2, 4, 8)

    def __init__(self, masks):
        self.masks = masks

    def start(self):
        zero = jnp.zeros((8, LANES), jnp.float32)
        return [zero] * (2 * MAXP + sum(self.GROUPS))

    def step(self, state, tile):
        state = list(state)
        at, later = 0, 2 * MAXP
        for mask, size in zip(self.masks, self.GROUPS):
            entered = tile
            for _ in range(size):
                half = state[at] + tile
                state[at], tile = tile, state[at + 1] + half
                state[at + 1] = half
                at += 2
            delayed = state[later]
            state[later : later + size] = state[later + 1 : later + size] + [entered]
            later += size
            tile = jnp.where(mask, tile, delayed)
        return state, tile


def group_masks(count):
    rest = count - 1
    bits = [jnp.bitwise_and(jnp.right_shift(rest, b), 1) == 1 for b in range(4)]
    used = count > 0
    return [used] + [used & bit for bit in bits]


def pack_kernel(
    e_hbm, n_hbm, h_hbm, a_ref, b_ref, wind_ref, height_ref, edge_ref, x_ref, t_ref, sems
):
    copies = []
    for f, ref in enumerate((e_hbm, n_hbm, h_hbm)):
        for t in range(2):
            copy = pltpu.make_async_copy(
                ref.at[:, :, pl.ds(LANES * t, LANES)],
                x_ref.at[f, t].reshape(8, 64, LANES),
                sems.at[f, t],
            )
            copy.start()
            copies.append(copy)
    winds = wind_ref.reshape(256 * 8, LANES)
    for f in range(3):
        for t in range(2):
            copies[2 * f + t].wait()
            for q in range(4):
                turned = x_ref[f, t, pl.ds(LANES * q, LANES), :].T
                if f < 2:
                    winds[pl.ds(1024 * t + 4 * f + q, LANES, stride=8), :] = turned
                else:
                    height_ref[pl.ds(512 * t + q, LANES, stride=4), :] = turned
    for side in range(2):
        for slot, (field, distance) in enumerate(EDGE_SLOTS):
            row = 63 - distance if side else distance
            place = 8 * (len(EDGE_SLOTS) * side + slot)
            for t in range(2):
                t_ref[t, pl.ds(place, 8), :] = x_ref[field, t, pl.ds(row, 8, stride=64), :]
    for t in range(2):
        t_ref[t, pl.ds(112, 16), :] = jnp.zeros((16, LANES), jnp.float32)
        edge_ref[pl.ds(LANES * t, LANES), :] = t_ref[t].T
    even = is_even("lon")
    last = 256 - WIDE
    for ref, right in ((a_ref, even), (b_ref, jnp.logical_not(even))):
        first = jnp.where(right, last, 0)
        ref[pl.ds(0, 8 * WIDE), :] = wind_ref[pl.ds(first, WIDE)].reshape(8 * WIDE, LANES)
        ref[pl.ds(HEIGHTS, 4 * WIDE), :] = jnp.where(
            right, height_ref[pl.ds(4 * last, 4 * WIDE), :], height_ref[pl.ds(0, 4 * WIDE), :]
        )
        ref[pl.ds(EDGES, WIDE), :] = jnp.where(
            right, edge_ref[pl.ds(last, WIDE), :], edge_ref[pl.ds(0, WIDE), :]
        )


def edge_kernel(
    turned_ref, rb_ref, ra_ref, count_ref, mer_ref, a_ref, b_ref, own_ref, z_ref, o_ref
):
    even_lon = is_even("lon")
    even_lat = is_even("lat")
    lane = lanes()
    halo = pl.ds(EDGES, WIDE)
    z_ref[pl.ds(24, 256), :] = turned_ref[...]
    z_ref[pl.ds(24 - WIDE, WIDE), :] = jnp.where(even_lon, rb_ref[halo, :], ra_ref[halo, :])
    z_ref[pl.ds(280, WIDE), :] = jnp.where(even_lon, ra_ref[halo, :], rb_ref[halo, :])
    z_ref[pl.ds(280 + WIDE, 5), :] = jnp.zeros((5, LANES), jnp.float32)
    count = count_ref[...]
    stream = Stream(group_masks(count))
    scale = undo(count)
    state = stream.start()
    for i in range(SHARE + 2 * MAXP):
        state, tile = stream.step(state, z_ref[pl.ds(24 - WIDE + i, 8, stride=SHARE), :])
        if i >= 2 * MAXP:
            o_ref[pl.ds(i - 2 * MAXP, 8, stride=SHARE), :] = tile * scale
    first = o_ref[pl.ds(REACH, LANES), :].T
    second = o_ref[pl.ds(REACH + LANES, LANES), :].T
    o_ref[pl.ds(REACH, REACH), :] = o_ref[pl.ds(REACH + 2 * LANES, REACH), :]
    third = o_ref[pl.ds(0, LANES), :].T
    packs = []
    for side in range(2):
        sense = -1.0 if side else 1.0

        def row(field, distance):
            slot = EDGE_SLOTS.index((field, distance))
            place = 8 * (len(EDGE_SLOTS) * side + slot)
            own = slice(place, place + 8)
            return jnp.concatenate([first[own], second[own], turn(third[own], -REACH)], axis=-1)

        e0, e1, n0, n1, n2, h0, h1 = (row(*slot) for slot in EDGE_SLOTS)
        outer = h0 + gravity_weight * (zonal(e0) + sense * n1)
        inner = h1 + gravity_weight * (zonal(e1) + sense * (n2 - n0))
        own_ref[side] = outer
        at = 63 if side else 0
        pack = jnp.broadcast_to(mer_ref[:, at : at + 1], (8, LANES))
        out = []
        for slot, value in enumerate((outer, inner, e0, n0)):
            out += [value[:, :LANES], value[:, LANES : 2 * LANES]]
            start = 2 * REACH * slot
            inside = (lane >= start) & (lane < start + 2 * REACH)
            pack = jnp.where(inside, turn(value[:, 2 * LANES :], REACH + start), pack)
        packs.append(out + [pack])
    for place, (top, bottom) in enumerate(zip(*packs)):
        a_ref[pl.ds(8 * place, 8)] = jnp.where(even_lat, bottom, top)
        b_ref[pl.ds(8 * place, 8)] = jnp.where(even_lat, top, bottom)


def following(rows):
    count = rows.shape[0]
    return pltpu.roll(rows, count - 1, 0) - pltpu.roll(rows, 1, 0)


def is_polar(lat_blocks, rows, band):
    position = lax.axis_index("lat")
    return (position < band // rows) | (position >= lat_blocks - band // rows)


def stencils(f_ref, v_ref, zb_ref, mb_ref, keep_heights, write):
    tiles = f_ref.shape[1]

    def whole(f, start, rows):
        place = pl.ds(start, rows)
        return jnp.concatenate([f_ref[f, t, place, :] for t in range(tiles)], axis=-1)

    def weight(k, l):
        return jnp.concatenate([v_ref[k, l]] * tiles, axis=-1)

    for first in range(0, 64, 8):
        old = []
        for l in range(8):
            start = 64 * l + first
            north = whole(1, start, 8)
            above = whole(1, start - 1, 8) if start else pltpu.roll(north, 1, 0)
            below = whole(1, start + 1, 8) if start < 512 - 8 else pltpu.roll(north, 7, 0)
            slope = zonal(whole(0, start, 8)) + (below - above)
            old.append(whole(2, start, 8) + gravity_weight * slope)
        for l in range(8):
            total = weight(0, l) * old[0]
            for k in range(1, 8):
                total = total + weight(k, l) * old[k]
            for t in range(tiles):
                place = pl.ds(64 * l + first, 8)
                f_ref[2, t, place, :] = total[:, LANES * t : LANES * (t + 1)]
    keep_heights()
    for l in range(8):
        h2 = whole(2, 64 * l, 64)
        h2_zonal = zonal(h2)
        e1 = whole(0, 64 * l, 64) + divergence_weight * h2_zonal
        n1 = whole(1, 64 * l, 64) + divergence_weight * following(h2)
        zon = jnp.concatenate([zb_ref[l]] * tiles, axis=-1)
        mer = jnp.concatenate([mb_ref[l]] * tiles, axis=-1)
        for f, field in enumerate((e1, n1, h2)):
            slope = h2_zonal if f == 2 else zonal(field)
            write(f, l, field + zon * slope + following(mer * field))


def edge_row(side, distance):
    return 63 - distance if side else distance


def interior_kernel(
    lat_blocks,
    _, wind_ref, height_ref, counts_ref, zon_ref, mer_ref, v_ref,
    f_ref, ob_ref, edge_ref, zb_ref, mb_ref, count_ref, edge_count_ref, vb_ref, vc_ref,
    wo_ref, ho_ref,
):
    lane = lanes()
    level = lax.broadcasted_iota(jnp.int32, (8, LANES), 0)
    polar = is_polar(lat_blocks, 64, counts_ref.shape[0] // 2)

    @pl.when(polar)
    def _():
        count = jnp.zeros((8, LANES), jnp.int32)
        for row in range(64):
            value = row_count(counts_ref, row, 64, lat_blocks)
            count = jnp.where(jnp.bitwise_and(lane, 63) == row, value, count)
        count_ref[...] = count
        count = jnp.zeros((8, LANES), jnp.int32)
        for side in range(2):
            for slot, (_, distance) in enumerate(EDGE_SLOTS):
                value = row_count(counts_ref, edge_row(side, distance), 64, lat_blocks)
                place = 8 * (len(EDGE_SLOTS) * side + slot)
                count = jnp.where(lane >= place, value, count)
        edge_count_ref[...] = count

    @pl.when(jnp.logical_not(polar))
    def _():
        count_ref[...] = jnp.zeros((8, LANES), jnp.int32)
        edge_count_ref[...] = jnp.zeros((8, LANES), jnp.int32)

    @pl.when(polar)
    def _():
        count = count_ref[...]
        stream = Stream(group_masks(count))
        scale = undo(count)

        def winds(chunk, state):
            for u in range(8):
                i = 8 * chunk + u
                state, tile = stream.step(state, wind_ref[i])
                wo_ref[i] = tile * scale
            return tuple(state)

        lax.fori_loop(0, 32, winds, tuple(stream.start()))

        def heights(chunk, state):
            for u in range(0, 8, 2):
                i = 8 * chunk + u
                low = height_ref[pl.ds(pl.multiple_of(4 * i, 8), 8), :]
                high = height_ref[pl.ds(pl.multiple_of(4 * i + 448, 8), 8), :]
                pair = jnp.where(level < 4, low, pltpu.roll(high, 4, 0))
                state, tile = stream.step(state, pair)
                ho_ref[i] = tile * scale
                pair = jnp.where(level < 4, pltpu.roll(low, 4, 0), high)
                state, tile = stream.step(state, pair)
                ho_ref[i + 1] = tile * scale
            return tuple(state)

        lax.fori_loop(0, 18, heights, tuple(stream.start()))
        wo = wo_ref.reshape(wo_ref.shape[0] * 8, LANES)
        ho = ho_ref.reshape(ho_ref.shape[0] * 8, LANES)
        for f in range(3):
            for q in range(4):
                for t in range(2):
                    if f < 2:
                        tall = wo[pl.ds(8 * (MAXP + LANES * t) + 4 * f + q, LANES, stride=8), :]
                    else:
                        tall = ho[pl.ds(8 * MAXP * (1 + t) + q + 4 * t, LANES, stride=8), :]
                    f_ref[f, t, pl.ds(LANES * q, LANES), :] = tall.T

    def keep_edge(slot, field, distance):
        for side in range(2):
            for t in range(2):
                place = pl.ds(edge_row(side, distance), 8, stride=64)
                edge_ref[side, slot, :, pl.ds(LANES * t, LANES)] = f_ref[field, t, place, :]

    for d in range(4):
        keep_edge(d, 0, d)
        keep_edge(4 + d, 1, d)
    for k in range(8):
        for l in range(8):
            vb_ref[k, l] = jnp.full((8, LANES), v_ref[k, l], jnp.float32)
    for k, column in enumerate(mixing(v_ref)):
        vc_ref[k] = column
    for l in range(8):
        zb_ref[l] = jnp.broadcast_to(zon_ref[l : l + 1, :], (LANES, 64)).T
        mb_ref[l] = jnp.broadcast_to(mer_ref[l : l + 1, :], (LANES, 64)).T

    def keep_heights():
        for d in range(1, 5):
            keep_edge(7 + d, 2, d)

    def write(f, l, value):
        for t in range(2):
            ob_ref[f, t, pl.ds(64 * l, 64), :] = value[:, LANES * t : LANES * (t + 1)]

    stencils(f_ref, vb_ref, zb_ref, mb_ref, keep_heights, write)


SIDE = 64
OWN = SIDE - WIDE


def fix_kernel(
    lat_blocks, band,
    ob_ref, inner_ref, wind_ref, height_ref, rb_ref, ra_ref, zb_ref, mb_ref, count_ref, v_ref,
    all_ref, edge_ref,
    f_ref, wz_ref, hz_ref,
):
    even_lon = is_even("lon")
    level = lax.broadcasted_iota(jnp.int32, (8, LANES), 0)
    polar = is_polar(lat_blocks, 64, band)

    def left(place):
        return jnp.where(even_lon, rb_ref[place, :], ra_ref[place, :])

    def right(place):
        return jnp.where(even_lon, ra_ref[place, :], rb_ref[place, :])

    for i in range(WIDE):
        wz_ref[MAXP + i] = left(pl.ds(8 * i, 8))
        wz_ref[MAXP + SIDE + OWN + i] = right(pl.ds(8 * i, 8))
    wz_ref[pl.ds(MAXP + WIDE, OWN)] = wind_ref[pl.ds(0, OWN)]
    wz_ref[pl.ds(MAXP + SIDE, OWN)] = wind_ref[pl.ds(256 - OWN, OWN)]
    for i in range(SIDE):
        if i < WIDE:
            low = left(pl.ds(HEIGHTS + 4 * i, 8))
        else:
            low = height_ref[pl.ds(4 * (i - WIDE), 8), :]
        if i < OWN:
            high = height_ref[pl.ds(4 * (256 - OWN + i) - 4, 8), :]
        else:
            high = right(pl.ds(HEIGHTS + 4 * (i - OWN) - 4, 8))
        hz_ref[MAXP + i] = jnp.where(level < 4, low, high)

    @pl.when(polar)
    def _():
        count = count_ref[...]
        stream = Stream(group_masks(count))
        scale = undo(count)

        def run(ref, base):
            def steps(chunk, state):
                for u in range(8):
                    i = base + 8 * chunk + u
                    state, tile = stream.step(state, ref[MAXP + i])
                    ref[i] = tile * scale
                return tuple(state)

            lax.fori_loop(0, SIDE // 8, steps, tuple(stream.start()))

        run(wz_ref, 0)
        run(wz_ref, SIDE)
        run(hz_ref, 0)

    wz = wz_ref.reshape(wz_ref.shape[0] * 8, LANES)
    hz = hz_ref.reshape(hz_ref.shape[0] * 8, LANES)
    for f in range(3):
        for q in range(4):
            if f < 2:
                tall = wz[pl.ds(8 * MAXP + 4 * f + q, LANES, stride=8), :]
            else:
                parts = [hz[pl.ds(8 * MAXP + q + 4 * s, SIDE, stride=8), :] for s in range(2)]
                tall = jnp.concatenate(parts, axis=0)
            f_ref[f, 0, pl.ds(LANES * q, LANES), :] = tall.T

    lane = lanes()

    def keep_edge(slot, field, distance):
        for side in range(2):
            near = f_ref[field, 0, pl.ds(edge_row(side, distance), 8, stride=64), :]
            west, east = turn(near, -WIDE), turn(near, WIDE)
            first, second = inner_ref[side, slot, :, :LANES], inner_ref[side, slot, :, LANES:]
            edge_ref[side, slot, :, pl.ds(0, LANES)] = jnp.where(lane < 24, west, first)
            edge_ref[side, slot, :, pl.ds(LANES, LANES)] = jnp.where(lane >= 104, east, second)
            edge_ref[side, slot, :, pl.ds(2 * LANES, LANES)] = jnp.where(lane < 64, east, west)

    for d in range(4):
        keep_edge(d, 0, d)
        keep_edge(4 + d, 1, d)

    def keep_heights():
        for d in range(1, 5):
            keep_edge(7 + d, 2, d)

    wide_lane = lax.broadcasted_iota(jnp.int32, (64, LANES), 1)

    def write(f, l, near):
        west, east = turn(near, -WIDE), turn(near, WIDE)
        rows = pl.ds(64 * l, 64)
        all_ref[f, 0, rows, :] = jnp.where(wide_lane < 22, west, ob_ref[f, 0, rows, :])
        all_ref[f, 1, rows, :] = jnp.where(wide_lane >= 106, east, ob_ref[f, 1, rows, :])

    stencils(f_ref, v_ref, zb_ref, mb_ref, keep_heights, write)


def mixing(v_ref):
    level = lax.broadcasted_iota(jnp.int32, (8, LANES), 0)
    columns = []
    for k in range(8):
        column = jnp.full((8, LANES), v_ref[k, 0], jnp.float32)
        for l in range(1, 8):
            column = jnp.where(level == l, v_ref[k, l], column)
        columns.append(column)
    return columns


def mix(columns, height):
    tiles = []
    for t in range(height.shape[-1] // LANES):
        tile = height[..., t * LANES : (t + 1) * LANES]
        total = None
        for k, column in enumerate(columns):
            term = column * jnp.broadcast_to(tile[..., k : k + 1, :], tile.shape)
            total = term if total is None else total + term
        tiles.append(total)
    return jnp.concatenate(tiles, axis=-1)


def wide(column):
    return jnp.concatenate([column] * (SPAN // LANES), axis=-1)


def finish_kernel(
    lat_blocks,
    edge_ref, own_ref, all_ref, gb_ref, ga_ref, zon_ref, mer_ref, v_ref,
    oe_ref, on_ref, oh_ref,
    ob_ref, sems, edge_sems,
):
    outs = (oe_ref, on_ref, oh_ref)
    copies = []
    for f, out in enumerate(outs):
        for t in range(2):
            copy = pltpu.make_async_copy(
                all_ref.at[f, t].reshape(8, 64, LANES).at[:, pl.ds(8, 48)],
                out.at[:, pl.ds(8, 48), pl.ds(LANES * t, LANES)],
                sems.at[f, t],
            )
            copy.start()
            copies.append(copy)
    position = lax.axis_index("lat")
    even_lat = is_even("lat")
    lane = lanes()
    columns = [v_ref[k] for k in range(8)]
    for side in range(2):
        top = side == 0
        sense = 1.0 if top else -1.0
        pole = position == (0 if top else lat_blocks - 1)
        turned = jnp.where(pole, -1.0, 1.0)

        def ghost_tile(place):
            a, b = ga_ref[pl.ds(8 * place, 8)], gb_ref[pl.ds(8 * place, 8)]
            return jnp.where(even_lat, b, a) if top else jnp.where(even_lat, a, b)

        pack = ghost_tile(8)

        def ghost(slot):
            third = turn(pack, -REACH - 2 * REACH * slot)
            return jnp.concatenate([ghost_tile(2 * slot), ghost_tile(2 * slot + 1), third], axis=-1)

        e = {d: edge_ref[side, d] for d in range(4)}
        n = {d: edge_ref[side, 4 + d] for d in range(4)}
        h2 = {d: edge_ref[side, 7 + d] for d in range(1, 5)}
        e[-1] = ghost(2)
        n[-1] = ghost(3) * turned
        h2[-2] = mix(columns, ghost(1))
        h2[-1] = mix(columns, ghost(0) + (gravity_weight * sense) * n[0])
        h2[0] = mix(columns, own_ref[side] - (gravity_weight * sense) * n[-1])
        e1, n1, h2_zonal = {}, {}, {}
        for d in range(-1, 4):
            h2_zonal[d] = zonal(h2[d])
            e1[d] = e[d] + divergence_weight * h2_zonal[d]
            n1[d] = n[d] + (divergence_weight * sense) * (h2[d + 1] - h2[d - 1])
        mer_ghost = wide(jnp.where(lane < LANES // 2, turn(pack, LANES // 2), pack))

        def coefficient(ref, d):
            row = edge_row(side, d)
            return wide(jnp.broadcast_to(ref[:, row : row + 1], (8, LANES)))

        zon = {d: coefficient(zon_ref, d) for d in range(3)}
        mer = {d: coefficient(mer_ref, d) for d in range(4)}
        for f, field in enumerate((e1, n1, h2)):
            mer[-1] = mer_ghost if f == 0 else mer_ghost * turned
            flow = {d: mer[d] * field[d] for d in range(-1, 4)}
            for t in range(2):
                for l in range(8):
                    ob_ref[f, side, t, pl.ds(8 * l, 8), :] = all_ref[
                        f, t, pl.ds(64 * l + 56 * side, 8), :
                    ]
            for d in range(3):
                slope = h2_zonal[d] if f == 2 else zonal(field[d])
                value = field[d] + zon[d] * slope + sense * (flow[d + 1] - flow[d - 1])
                for t in range(2):
                    ob_ref[f, side, t, pl.ds(d if top else 7 - d, 8, stride=8), :] = value[
                        :, LANES * t : LANES * (t + 1)
                    ]
    for side in range(2):
        for f, out in enumerate(outs):
            for t in range(2):
                copy = pltpu.make_async_copy(
                    ob_ref.at[f, side, t].reshape(8, 8, LANES),
                    out.at[:, pl.ds(56 * side, 8), pl.ds(LANES * t, LANES)],
                    edge_sems.at[f, side, t],
                )
                copy.start()
                copies.append(copy)
    for copy in copies:
        copy.wait()


def body(
    lat_blocks, lon_blocks, axes,
    east_adjoint, north_adjoint, height_adjoint,
    zonal_courant, meridional_courant, vertical_inverse, pass_counts,
):
    f32 = jnp.float32
    fields = tuple(
        pltpu.with_memory_space_constraint(x, pltpu.HBM)
        for x in (east_adjoint, north_adjoint, height_adjoint)
    )

    def in_vmem(*dims):
        return pltpu.VMEM(dims, f32)

    def params():
        return pltpu.CompilerParams(vmem_limit_bytes=40 * 1024 * 1024)

    lon_a, lon_b, winds, heights, edge_rows, local = pl.pallas_call(
        pack_kernel,
        out_shape=(
            in_vmem(PAYLOAD, LANES), in_vmem(PAYLOAD, LANES),
            in_vmem(256, 8, LANES), in_vmem(1024, LANES), in_vmem(256, LANES),
            in_vmem(3, 2, 512, LANES),
        ),
        in_specs=[HBM] * 3,
        out_specs=(VMEM,) * 6,
        scratch_shapes=[pltpu.VMEM((2, LANES, LANES), f32), pltpu.SemaphoreType.DMA((3, 2))],
        compiler_params=params(),
        name="pack",
    )(*fields)

    def other_lon(o):
        return (((o + 1) ^ 1) - 1) % lon_blocks

    recv_a = lax.ppermute(lon_a, "lon", [(o, o ^ 1) for o in range(lon_blocks)])
    recv_b = lax.ppermute(lon_b, "lon", [(o, other_lon(o)) for o in range(lon_blocks)])

    by_row = in_vmem(8, 64, LANES)
    by_count = pltpu.VMEM((8, LANES), jnp.int32)
    _, inner, inner_edges, zon_wide, mer_wide, counts, edge_counts, weights, columns = pl.pallas_call(
        lambda *refs: interior_kernel(lat_blocks, *refs),
        out_shape=(
            in_vmem(3, 2, 512, LANES), in_vmem(3, 2, 512, LANES), in_vmem(2, 12, 8, 256),
            by_row, by_row, by_count, by_count, in_vmem(8, 8, 8, LANES), in_vmem(8, 8, LANES),
        ),
        in_specs=[VMEM] * 3 + [SMEM, VMEM, VMEM, SMEM],
        out_specs=(VMEM,) * 9,
        input_output_aliases={0: 0},
        scratch_shapes=[
            pltpu.VMEM((272, 8, LANES), f32),
            pltpu.VMEM((160, 8, LANES), f32),
        ],
        compiler_params=params(),
        cost_estimate=pl.CostEstimate(flops=100000000, bytes_accessed=20000000, transcendentals=0),
        name="interior",
    )(
        local, winds, heights, pass_counts, zonal_courant, meridional_courant, vertical_inverse
    )

    lat_a, lat_b, own_edges = pl.pallas_call(
        edge_kernel,
        out_shape=(in_vmem(72, LANES), in_vmem(72, LANES), in_vmem(2, 8, SPAN)),
        in_specs=[VMEM] * 5,
        out_specs=(VMEM,) * 3,
        scratch_shapes=[pltpu.VMEM((304, LANES), f32), pltpu.VMEM((264, LANES), f32)],
        compiler_params=params(),
        name="edge",
    )(edge_rows, recv_b, recv_a, edge_counts, meridional_courant)

    def index(a, o):
        return o * lat_blocks + a if axes[0] == "lon" else a * lon_blocks + o

    def other_lat(a, o):
        if a in (0, lat_blocks - 1):
            return a, (o + lon_blocks // 2) % lon_blocks
        return ((a + 1) ^ 1) - 1, o

    pairs = [
        (index(a, o), index(*other_lat(a, o))) for a in range(lat_blocks) for o in range(lon_blocks)
    ]
    ghost_a = lax.ppermute(lat_a, "lat", [(a, a ^ 1) for a in range(lat_blocks)])
    ghost_b = lax.ppermute(lat_b, axes, pairs)

    block = jax.ShapeDtypeStruct(east_adjoint.shape, f32)
    final, edges = pl.pallas_call(
        lambda *refs: fix_kernel(lat_blocks, pass_counts.shape[0] // 2, *refs),
        out_shape=(in_vmem(3, 2, 512, LANES), in_vmem(2, 12, 8, SPAN)),
        in_specs=[VMEM] * 10,
        out_specs=(VMEM,) * 2,
        scratch_shapes=[
            pltpu.VMEM((3, 1, 512, LANES), f32),
            pltpu.VMEM((MAXP + 2 * SIDE, 8, LANES), f32),
            pltpu.VMEM((MAXP + SIDE, 8, LANES), f32),
        ],
        compiler_params=params(),
        cost_estimate=pl.CostEstimate(flops=50000000, bytes_accessed=10000000, transcendentals=0),
        name="fix",
    )(
        inner, inner_edges, winds, heights, recv_b, recv_a, zon_wide, mer_wide, counts, weights,
    )

    return pl.pallas_call(
        lambda *refs: finish_kernel(lat_blocks, *refs),
        out_shape=(block,) * 3,
        in_specs=[VMEM] * 8,
        out_specs=(HBM,) * 3,
        scratch_shapes=[
            pltpu.VMEM((3, 2, 2, 64, LANES), f32),
            pltpu.SemaphoreType.DMA((3, 2)),
            pltpu.SemaphoreType.DMA((3, 2, 2)),
        ],
        compiler_params=params(),
        name="finish",
    )(
        edges, own_edges, final, ghost_b, ghost_a, zonal_courant, meridional_courant, columns
    )


def solution(mesh):
    sizes = dict(mesh.shape)
    axes = tuple(mesh.axis_names)
    spread_out = P(None, "lat", "lon")
    return jax.shard_map(
        lambda *args: body(sizes["lat"], sizes["lon"], axes, *args),
        mesh=mesh,
        in_specs=(spread_out,) * 3 + (P(None, "lat"), P(None, "lat"), P(), P()),
        out_specs=(spread_out,) * 3,
        check_vma=False,
    )
```

```python
import jax
import jax.numpy as jnp
from jax import lax
from jax.experimental import pallas as pl
from jax.experimental.pallas import tpu as pltpu
from jax.sharding import PartitionSpec as P

MAXP = 16
REACH = 3
WIDE = MAXP + REACH
LANES = 128
SPAN = 3 * LANES
SHARE = 33

gravity_weight = 0.3
divergence_weight = 0.3

VMEM = pl.BlockSpec(memory_space=pltpu.VMEM)
SMEM = pl.BlockSpec(memory_space=pltpu.SMEM)
HBM = pl.BlockSpec(memory_space=pltpu.HBM)

EDGE_SLOTS = ((0, 0), (0, 1), (1, 0), (1, 1), (1, 2), (2, 0), (2, 1))


HEIGHTS = 8 * WIDE + 4
EDGES = 8 * WIDE + 88
PAYLOAD = EDGES + 24


def lanes():
    return lax.broadcasted_iota(jnp.int32, (8, LANES), 1)


def turn(values, steps):
    return pltpu.roll(values, steps % values.shape[-1], values.ndim - 1)


def zonal(values):
    return turn(values, -1) - turn(values, 1)


def is_even(axis):
    return lax.rem(lax.axis_index(axis), 2) == 0


def row_count(counts_ref, row, rows, lat_blocks):
    band = counts_ref.shape[0] // 2
    blocks = band // rows
    position = lax.axis_index("lat")
    north = position < blocks
    south = position >= lat_blocks - blocks
    place = jnp.where(north, position, jnp.where(south, position - lat_blocks + 2 * blocks, 0))
    return jnp.where(north | south, counts_ref[place * rows + row], 0)


def undo(count):
    power = jnp.left_shift(1, MAXP - count).astype(jnp.float32)
    return power * power * (2.0 ** (-2 * MAXP))


class Stream:
    GROUPS = (1, 1, 2, 4, 8)

    def __init__(self, masks):
        self.masks = masks

    def start(self):
        zero = jnp.zeros((8, LANES), jnp.float32)
        return [zero] * (2 * MAXP + sum(self.GROUPS))

    def step(self, state, tile):
        state = list(state)
        at, later = 0, 2 * MAXP
        for mask, size in zip(self.masks, self.GROUPS):
            entered = tile
            for _ in range(size):
                half = state[at] + tile
                state[at], tile = tile, state[at + 1] + half
                state[at + 1] = half
                at += 2
            delayed = state[later]
            state[later : later + size] = state[later + 1 : later + size] + [entered]
            later += size
            tile = jnp.where(mask, tile, delayed)
        return state, tile


def group_masks(count):
    rest = count - 1
    bits = [jnp.bitwise_and(jnp.right_shift(rest, b), 1) == 1 for b in range(4)]
    used = count > 0
    return [used] + [used & bit for bit in bits]


def pack_kernel(
    e_hbm, n_hbm, h_hbm, a_ref, b_ref, wind_ref, height_ref, edge_ref, x_ref, t_ref, sems
):
    copies = []
    for f, ref in enumerate((e_hbm, n_hbm, h_hbm)):
        for t in range(2):
            copy = pltpu.make_async_copy(
                ref.at[:, :, pl.ds(LANES * t, LANES)],
                x_ref.at[f, t].reshape(8, 64, LANES),
                sems.at[f, t],
            )
            copy.start()
            copies.append(copy)
    winds = wind_ref.reshape(256 * 8, LANES)
    for f in range(3):
        for t in range(2):
            copies[2 * f + t].wait()
            for q in range(4):
                turned = x_ref[f, t, pl.ds(LANES * q, LANES), :].T
                if f < 2:
                    winds[pl.ds(1024 * t + 4 * f + q, LANES, stride=8), :] = turned
                else:
                    height_ref[pl.ds(512 * t + q, LANES, stride=4), :] = turned
    for side in range(2):
        for slot, (field, distance) in enumerate(EDGE_SLOTS):
            row = 63 - distance if side else distance
            place = 8 * (len(EDGE_SLOTS) * side + slot)
            for t in range(2):
                t_ref[t, pl.ds(place, 8), :] = x_ref[field, t, pl.ds(row, 8, stride=64), :]
    for t in range(2):
        t_ref[t, pl.ds(112, 16), :] = jnp.zeros((16, LANES), jnp.float32)
        edge_ref[pl.ds(LANES * t, LANES), :] = t_ref[t].T
    even = is_even("lon")
    last = 256 - WIDE
    for ref, right in ((a_ref, even), (b_ref, jnp.logical_not(even))):
        first = jnp.where(right, last, 0)
        ref[pl.ds(0, 8 * WIDE), :] = wind_ref[pl.ds(first, WIDE)].reshape(8 * WIDE, LANES)
        ref[pl.ds(HEIGHTS, 4 * WIDE), :] = jnp.where(
            right, height_ref[pl.ds(4 * last, 4 * WIDE), :], height_ref[pl.ds(0, 4 * WIDE), :]
        )
        ref[pl.ds(EDGES, WIDE), :] = jnp.where(
            right, edge_ref[pl.ds(last, WIDE), :], edge_ref[pl.ds(0, WIDE), :]
        )


def edge_kernel(
    lat_blocks, band,
    turned_ref, rb_ref, ra_ref, count_ref, mer_ref, a_ref, b_ref, own_ref, z_ref, o_ref
):
    even_lon = is_even("lon")
    even_lat = is_even("lat")
    lane = lanes()
    halo = pl.ds(EDGES, WIDE)
    z_ref[pl.ds(24, 256), :] = turned_ref[...]
    z_ref[pl.ds(24 - WIDE, WIDE), :] = jnp.where(even_lon, rb_ref[halo, :], ra_ref[halo, :])
    z_ref[pl.ds(280, WIDE), :] = jnp.where(even_lon, ra_ref[halo, :], rb_ref[halo, :])
    z_ref[pl.ds(280 + WIDE, 5), :] = jnp.zeros((5, LANES), jnp.float32)
    polar = is_polar(lat_blocks, 64, band)

    @pl.when(jnp.logical_not(polar))
    def _():
        o_ref[...] = z_ref[pl.ds(24 - REACH, 8 * SHARE), :]

    @pl.when(polar)
    def _():
        count = count_ref[...]
        stream = Stream(group_masks(count))
        scale = undo(count)
        state = stream.start()
        for i in range(SHARE + 2 * MAXP):
            state, tile = stream.step(state, z_ref[pl.ds(24 - WIDE + i, 8, stride=SHARE), :])
            if i >= 2 * MAXP:
                o_ref[pl.ds(i - 2 * MAXP, 8, stride=SHARE), :] = tile * scale

    first = o_ref[pl.ds(REACH, LANES), :].T
    second = o_ref[pl.ds(REACH + LANES, LANES), :].T
    o_ref[pl.ds(REACH, REACH), :] = o_ref[pl.ds(REACH + 2 * LANES, REACH), :]
    third = o_ref[pl.ds(0, LANES), :].T
    packs = []
    for side in range(2):
        sense = -1.0 if side else 1.0

        def row(field, distance):
            slot = EDGE_SLOTS.index((field, distance))
            place = 8 * (len(EDGE_SLOTS) * side + slot)
            own = slice(place, place + 8)
            return jnp.concatenate([first[own], second[own], turn(third[own], -REACH)], axis=-1)

        e0, e1, n0, n1, n2, h0, h1 = (row(*slot) for slot in EDGE_SLOTS)
        outer = h0 + gravity_weight * (zonal(e0) + sense * n1)
        inner = h1 + gravity_weight * (zonal(e1) + sense * (n2 - n0))
        own_ref[side] = outer
        at = 63 if side else 0
        pack = jnp.broadcast_to(mer_ref[:, at : at + 1], (8, LANES))
        out = []
        for slot, value in enumerate((outer, inner, e0, n0)):
            out += [value[:, :LANES], value[:, LANES : 2 * LANES]]
            start = 2 * REACH * slot
            inside = (lane >= start) & (lane < start + 2 * REACH)
            pack = jnp.where(inside, turn(value[:, 2 * LANES :], REACH + start), pack)
        packs.append(out + [pack])
    for place, (top, bottom) in enumerate(zip(*packs)):
        a_ref[pl.ds(8 * place, 8)] = jnp.where(even_lat, bottom, top)
        b_ref[pl.ds(8 * place, 8)] = jnp.where(even_lat, top, bottom)


def following(rows):
    count = rows.shape[0]
    return pltpu.roll(rows, count - 1, 0) - pltpu.roll(rows, 1, 0)


def is_polar(lat_blocks, rows, band):
    position = lax.axis_index("lat")
    return (position < band // rows) | (position >= lat_blocks - band // rows)


def leaves_results(lat_blocks, rows, band):
    position = lax.axis_index("lat")
    return (position == band // rows - 1) | (position >= lat_blocks - band // rows)


def whole(f_ref, f, start, rows):
    tiles = range(f_ref.shape[1])
    return jnp.concatenate([f_ref[f, t, pl.ds(start, rows), :] for t in tiles], axis=-1)


def new_heights(f_ref, v_ref):
    tiles = f_ref.shape[1]

    def weight(k, l):
        return jnp.concatenate([v_ref[k, l]] * tiles, axis=-1)

    for first in range(0, 64, 8):
        old = []
        for l in range(8):
            start = 64 * l + first
            north = whole(f_ref, 1, start, 8)
            above = whole(f_ref, 1, start - 1, 8) if start else pltpu.roll(north, 1, 0)
            below = whole(f_ref, 1, start + 1, 8) if start < 512 - 8 else pltpu.roll(north, 7, 0)
            slope = zonal(whole(f_ref, 0, start, 8)) + (below - above)
            old.append(whole(f_ref, 2, start, 8) + gravity_weight * slope)
        for l in range(8):
            total = weight(0, l) * old[0]
            for k in range(1, 8):
                total = total + weight(k, l) * old[k]
            for t in range(tiles):
                place = pl.ds(64 * l + first, 8)
                f_ref[2, t, place, :] = total[:, LANES * t : LANES * (t + 1)]


def results(f_ref, zb_ref, mb_ref, write):
    tiles = f_ref.shape[1]
    for l in range(8):
        h2 = whole(f_ref, 2, 64 * l, 64)
        h2_zonal = zonal(h2)
        e1 = whole(f_ref, 0, 64 * l, 64) + divergence_weight * h2_zonal
        n1 = whole(f_ref, 1, 64 * l, 64) + divergence_weight * following(h2)
        zon = jnp.concatenate([zb_ref[l]] * tiles, axis=-1)
        mer = jnp.concatenate([mb_ref[l]] * tiles, axis=-1)
        for f, field in enumerate((e1, n1, h2)):
            slope = h2_zonal if f == 2 else zonal(field)
            write(f, l, field + zon * slope + following(mer * field))


def edge_row(side, distance):
    return 63 - distance if side else distance


def inner_results(f_ref, zb_ref, mb_ref, ob_ref):
    def write(f, l, value):
        for t in range(2):
            ob_ref[f, t, pl.ds(64 * l, 64), :] = value[:, LANES * t : LANES * (t + 1)]

    results(f_ref, zb_ref, mb_ref, write)


def interior_kernel(
    lat_blocks,
    _, wind_ref, height_ref, counts_ref, zon_ref, mer_ref, v_ref,
    f_ref, ob_ref, edge_ref, zb_ref, mb_ref, count_ref, edge_count_ref, vb_ref, vc_ref,
    wo_ref, ho_ref,
):
    lane = lanes()
    level = lax.broadcasted_iota(jnp.int32, (8, LANES), 0)
    polar = is_polar(lat_blocks, 64, counts_ref.shape[0] // 2)

    @pl.when(polar)
    def _():
        count = jnp.zeros((8, LANES), jnp.int32)
        for row in range(64):
            value = row_count(counts_ref, row, 64, lat_blocks)
            count = jnp.where(jnp.bitwise_and(lane, 63) == row, value, count)
        count_ref[...] = count
        count = jnp.zeros((8, LANES), jnp.int32)
        for side in range(2):
            for slot, (_, distance) in enumerate(EDGE_SLOTS):
                value = row_count(counts_ref, edge_row(side, distance), 64, lat_blocks)
                place = 8 * (len(EDGE_SLOTS) * side + slot)
                count = jnp.where(lane >= place, value, count)
        edge_count_ref[...] = count

    @pl.when(jnp.logical_not(polar))
    def _():
        count_ref[...] = jnp.zeros((8, LANES), jnp.int32)
        edge_count_ref[...] = jnp.zeros((8, LANES), jnp.int32)

    @pl.when(polar)
    def _():
        count = count_ref[...]
        stream = Stream(group_masks(count))
        scale = undo(count)

        def winds(chunk, state):
            for u in range(8):
                i = 8 * chunk + u
                state, tile = stream.step(state, wind_ref[i])
                wo_ref[i] = tile * scale
            return tuple(state)

        lax.fori_loop(0, 32, winds, tuple(stream.start()))

        def heights(chunk, state):
            for u in range(0, 8, 2):
                i = 8 * chunk + u
                low = height_ref[pl.ds(pl.multiple_of(4 * i, 8), 8), :]
                high = height_ref[pl.ds(pl.multiple_of(4 * i + 448, 8), 8), :]
                pair = jnp.where(level < 4, low, pltpu.roll(high, 4, 0))
                state, tile = stream.step(state, pair)
                ho_ref[i] = tile * scale
                pair = jnp.where(level < 4, pltpu.roll(low, 4, 0), high)
                state, tile = stream.step(state, pair)
                ho_ref[i + 1] = tile * scale
            return tuple(state)

        lax.fori_loop(0, 18, heights, tuple(stream.start()))
        wo = wo_ref.reshape(wo_ref.shape[0] * 8, LANES)
        ho = ho_ref.reshape(ho_ref.shape[0] * 8, LANES)
        for f in range(3):
            for q in range(4):
                for t in range(2):
                    if f < 2:
                        tall = wo[pl.ds(8 * (MAXP + LANES * t) + 4 * f + q, LANES, stride=8), :]
                    else:
                        tall = ho[pl.ds(8 * MAXP * (1 + t) + q + 4 * t, LANES, stride=8), :]
                    f_ref[f, t, pl.ds(LANES * q, LANES), :] = tall.T

    def keep_edge(slot, field, distance):
        for side in range(2):
            for t in range(2):
                place = pl.ds(edge_row(side, distance), 8, stride=64)
                edge_ref[side, slot, :, pl.ds(LANES * t, LANES)] = f_ref[field, t, place, :]

    for d in range(4):
        keep_edge(d, 0, d)
        keep_edge(4 + d, 1, d)
    for k in range(8):
        for l in range(8):
            vb_ref[k, l] = jnp.full((8, LANES), v_ref[k, l], jnp.float32)
    for k, column in enumerate(mixing(v_ref)):
        vc_ref[k] = column
    for l in range(8):
        zb_ref[l] = jnp.broadcast_to(zon_ref[l : l + 1, :], (LANES, 64)).T
        mb_ref[l] = jnp.broadcast_to(mer_ref[l : l + 1, :], (LANES, 64)).T

    new_heights(f_ref, vb_ref)
    for d in range(1, 5):
        keep_edge(7 + d, 2, d)

    @pl.when(jnp.logical_not(leaves_results(lat_blocks, 64, counts_ref.shape[0] // 2)))
    def _():
        inner_results(f_ref, zb_ref, mb_ref, ob_ref)


SIDE = 64
OWN = SIDE - WIDE


def fix_kernel(
    lat_blocks, band,
    _, inner_f_ref, inner_ref, wind_ref, height_ref, rb_ref, ra_ref, zb_ref, mb_ref, count_ref, v_ref,
    ob_ref, all_ref, edge_ref,
    f_ref, wz_ref, hz_ref,
):
    even_lon = is_even("lon")
    level = lax.broadcasted_iota(jnp.int32, (8, LANES), 0)
    polar = is_polar(lat_blocks, 64, band)

    @pl.when(leaves_results(lat_blocks, 64, band))
    def _():
        inner_results(inner_f_ref, zb_ref, mb_ref, ob_ref)

    def left(place):
        return jnp.where(even_lon, rb_ref[place, :], ra_ref[place, :])

    def right(place):
        return jnp.where(even_lon, ra_ref[place, :], rb_ref[place, :])

    for i in range(WIDE):
        wz_ref[MAXP + i] = left(pl.ds(8 * i, 8))
        wz_ref[MAXP + SIDE + OWN + i] = right(pl.ds(8 * i, 8))
    wz_ref[pl.ds(MAXP + WIDE, OWN)] = wind_ref[pl.ds(0, OWN)]
    wz_ref[pl.ds(MAXP + SIDE, OWN)] = wind_ref[pl.ds(256 - OWN, OWN)]
    for i in range(SIDE):
        if i < WIDE:
            low = left(pl.ds(HEIGHTS + 4 * i, 8))
        else:
            low = height_ref[pl.ds(4 * (i - WIDE), 8), :]
        if i < OWN:
            high = height_ref[pl.ds(4 * (256 - OWN + i) - 4, 8), :]
        else:
            high = right(pl.ds(HEIGHTS + 4 * (i - OWN) - 4, 8))
        hz_ref[MAXP + i] = jnp.where(level < 4, low, high)

    @pl.when(polar)
    def _():
        count = count_ref[...]
        stream = Stream(group_masks(count))
        scale = undo(count)

        def run(ref, base):
            def steps(chunk, state):
                for u in range(8):
                    i = base + 8 * chunk + u
                    state, tile = stream.step(state, ref[MAXP + i])
                    ref[i] = tile * scale
                return tuple(state)

            lax.fori_loop(0, SIDE // 8, steps, tuple(stream.start()))

        run(wz_ref, 0)
        run(wz_ref, SIDE)
        run(hz_ref, 0)

    wz = wz_ref.reshape(wz_ref.shape[0] * 8, LANES)
    hz = hz_ref.reshape(hz_ref.shape[0] * 8, LANES)
    for f in range(3):
        for q in range(4):
            if f < 2:
                tall = wz[pl.ds(8 * MAXP + 4 * f + q, LANES, stride=8), :]
            else:
                parts = [hz[pl.ds(8 * MAXP + q + 4 * s, SIDE, stride=8), :] for s in range(2)]
                tall = jnp.concatenate(parts, axis=0)
            f_ref[f, 0, pl.ds(LANES * q, LANES), :] = tall.T

    lane = lanes()

    def keep_edge(slot, field, distance):
        for side in range(2):
            near = f_ref[field, 0, pl.ds(edge_row(side, distance), 8, stride=64), :]
            west, east = turn(near, -WIDE), turn(near, WIDE)
            first, second = inner_ref[side, slot, :, :LANES], inner_ref[side, slot, :, LANES:]
            edge_ref[side, slot, :, pl.ds(0, LANES)] = jnp.where(lane < 24, west, first)
            edge_ref[side, slot, :, pl.ds(LANES, LANES)] = jnp.where(lane >= 104, east, second)
            edge_ref[side, slot, :, pl.ds(2 * LANES, LANES)] = jnp.where(lane < 64, east, west)

    for d in range(4):
        keep_edge(d, 0, d)
        keep_edge(4 + d, 1, d)

    new_heights(f_ref, v_ref)
    for d in range(1, 5):
        keep_edge(7 + d, 2, d)
    wide_lane = lax.broadcasted_iota(jnp.int32, (64, LANES), 1)

    def write(f, l, near):
        west, east = turn(near, -WIDE), turn(near, WIDE)
        rows = pl.ds(64 * l, 64)
        all_ref[f, 0, rows, :] = jnp.where(wide_lane < 22, west, ob_ref[f, 0, rows, :])
        all_ref[f, 1, rows, :] = jnp.where(wide_lane >= 106, east, ob_ref[f, 1, rows, :])

    results(f_ref, zb_ref, mb_ref, write)


def mixing(v_ref):
    level = lax.broadcasted_iota(jnp.int32, (8, LANES), 0)
    columns = []
    for k in range(8):
        column = jnp.full((8, LANES), v_ref[k, 0], jnp.float32)
        for l in range(1, 8):
            column = jnp.where(level == l, v_ref[k, l], column)
        columns.append(column)
    return columns


def mix(columns, height):
    tiles = []
    for t in range(height.shape[-1] // LANES):
        tile = height[..., t * LANES : (t + 1) * LANES]
        total = None
        for k, column in enumerate(columns):
            term = column * jnp.broadcast_to(tile[..., k : k + 1, :], tile.shape)
            total = term if total is None else total + term
        tiles.append(total)
    return jnp.concatenate(tiles, axis=-1)


def wide(column):
    return jnp.concatenate([column] * (SPAN // LANES), axis=-1)


def finish_kernel(
    lat_blocks,
    edge_ref, own_ref, all_ref, gb_ref, ga_ref, zon_ref, mer_ref, v_ref,
    oe_ref, on_ref, oh_ref,
    ob_ref, sems, edge_sems,
):
    outs = (oe_ref, on_ref, oh_ref)
    copies = []
    for f, out in enumerate(outs):
        for t in range(2):
            copy = pltpu.make_async_copy(
                all_ref.at[f, t].reshape(8, 64, LANES).at[:, pl.ds(8, 48)],
                out.at[:, pl.ds(8, 48), pl.ds(LANES * t, LANES)],
                sems.at[f, t],
            )
            copy.start()
            copies.append(copy)
    position = lax.axis_index("lat")
    even_lat = is_even("lat")
    lane = lanes()
    columns = [v_ref[k] for k in range(8)]
    for side in range(2):
        top = side == 0
        sense = 1.0 if top else -1.0
        pole = position == (0 if top else lat_blocks - 1)
        turned = jnp.where(pole, -1.0, 1.0)

        def ghost_tile(place):
            a, b = ga_ref[pl.ds(8 * place, 8)], gb_ref[pl.ds(8 * place, 8)]
            return jnp.where(even_lat, b, a) if top else jnp.where(even_lat, a, b)

        pack = ghost_tile(8)

        def ghost(slot):
            third = turn(pack, -REACH - 2 * REACH * slot)
            return jnp.concatenate([ghost_tile(2 * slot), ghost_tile(2 * slot + 1), third], axis=-1)

        e = {d: edge_ref[side, d] for d in range(4)}
        n = {d: edge_ref[side, 4 + d] for d in range(4)}
        h2 = {d: edge_ref[side, 7 + d] for d in range(1, 5)}
        e[-1] = ghost(2)
        n[-1] = ghost(3) * turned
        h2[-2] = mix(columns, ghost(1))
        h2[-1] = mix(columns, ghost(0) + (gravity_weight * sense) * n[0])
        h2[0] = mix(columns, own_ref[side] - (gravity_weight * sense) * n[-1])
        e1, n1, h2_zonal = {}, {}, {}
        for d in range(-1, 4):
            h2_zonal[d] = zonal(h2[d])
            e1[d] = e[d] + divergence_weight * h2_zonal[d]
            n1[d] = n[d] + (divergence_weight * sense) * (h2[d + 1] - h2[d - 1])
        mer_ghost = wide(jnp.where(lane < LANES // 2, turn(pack, LANES // 2), pack))

        def coefficient(ref, d):
            row = edge_row(side, d)
            return wide(jnp.broadcast_to(ref[:, row : row + 1], (8, LANES)))

        zon = {d: coefficient(zon_ref, d) for d in range(3)}
        mer = {d: coefficient(mer_ref, d) for d in range(4)}
        for f, field in enumerate((e1, n1, h2)):
            mer[-1] = mer_ghost if f == 0 else mer_ghost * turned
            flow = {d: mer[d] * field[d] for d in range(-1, 4)}
            for t in range(2):
                for l in range(8):
                    ob_ref[f, side, t, pl.ds(8 * l, 8), :] = all_ref[
                        f, t, pl.ds(64 * l + 56 * side, 8), :
                    ]
            for d in range(3 if f == 1 else 2):
                slope = h2_zonal[d] if f == 2 else zonal(field[d])
                value = field[d] + zon[d] * slope + sense * (flow[d + 1] - flow[d - 1])
                for t in range(2):
                    ob_ref[f, side, t, pl.ds(d if top else 7 - d, 8, stride=8), :] = value[
                        :, LANES * t : LANES * (t + 1)
                    ]
    for side in range(2):
        for f, out in enumerate(outs):
            for t in range(2):
                copy = pltpu.make_async_copy(
                    ob_ref.at[f, side, t].reshape(8, 8, LANES),
                    out.at[:, pl.ds(56 * side, 8), pl.ds(LANES * t, LANES)],
                    edge_sems.at[f, side, t],
                )
                copy.start()
                copies.append(copy)
    for copy in copies:
        copy.wait()


def body(
    lat_blocks, lon_blocks, axes,
    east_adjoint, north_adjoint, height_adjoint,
    zonal_courant, meridional_courant, vertical_inverse, pass_counts,
):
    f32 = jnp.float32
    fields = tuple(
        pltpu.with_memory_space_constraint(x, pltpu.HBM)
        for x in (east_adjoint, north_adjoint, height_adjoint)
    )

    def in_vmem(*dims):
        return pltpu.VMEM(dims, f32)

    def params():
        return pltpu.CompilerParams(vmem_limit_bytes=40 * 1024 * 1024)

    lon_a, lon_b, winds, heights, edge_rows, local = pl.pallas_call(
        pack_kernel,
        out_shape=(
            in_vmem(PAYLOAD, LANES), in_vmem(PAYLOAD, LANES),
            in_vmem(256, 8, LANES), in_vmem(1024, LANES), in_vmem(256, LANES),
            in_vmem(3, 2, 512, LANES),
        ),
        in_specs=[HBM] * 3,
        out_specs=(VMEM,) * 6,
        scratch_shapes=[pltpu.VMEM((2, LANES, LANES), f32), pltpu.SemaphoreType.DMA((3, 2))],
        compiler_params=params(),
        name="pack",
    )(*fields)

    def other_lon(o):
        return (((o + 1) ^ 1) - 1) % lon_blocks

    recv_a = lax.ppermute(lon_a, "lon", [(o, o ^ 1) for o in range(lon_blocks)])
    recv_b = lax.ppermute(lon_b, "lon", [(o, other_lon(o)) for o in range(lon_blocks)])

    by_row = in_vmem(8, 64, LANES)
    by_count = pltpu.VMEM((8, LANES), jnp.int32)
    inner_f, inner, inner_edges, zon_wide, mer_wide, counts, edge_counts, weights, columns = pl.pallas_call(
        lambda *refs: interior_kernel(lat_blocks, *refs),
        out_shape=(
            in_vmem(3, 2, 512, LANES), in_vmem(3, 2, 512, LANES), in_vmem(2, 12, 8, 256),
            by_row, by_row, by_count, by_count, in_vmem(8, 8, 8, LANES), in_vmem(8, 8, LANES),
        ),
        in_specs=[VMEM] * 3 + [SMEM, VMEM, VMEM, SMEM],
        out_specs=(VMEM,) * 9,
        input_output_aliases={0: 0},
        scratch_shapes=[
            pltpu.VMEM((272, 8, LANES), f32),
            pltpu.VMEM((160, 8, LANES), f32),
        ],
        compiler_params=params(),
        cost_estimate=pl.CostEstimate(flops=100000000, bytes_accessed=20000000, transcendentals=0),
        name="interior",
    )(
        local, winds, heights, pass_counts, zonal_courant, meridional_courant, vertical_inverse
    )

    band = pass_counts.shape[0] // 2
    lat_a, lat_b, own_edges = pl.pallas_call(
        lambda *refs: edge_kernel(lat_blocks, band, *refs),
        out_shape=(in_vmem(72, LANES), in_vmem(72, LANES), in_vmem(2, 8, SPAN)),
        in_specs=[VMEM] * 5,
        out_specs=(VMEM,) * 3,
        scratch_shapes=[pltpu.VMEM((304, LANES), f32), pltpu.VMEM((264, LANES), f32)],
        compiler_params=params(),
        name="edge",
    )(edge_rows, recv_b, recv_a, edge_counts, meridional_courant)

    def index(a, o):
        return o * lat_blocks + a if axes[0] == "lon" else a * lon_blocks + o

    def other_lat(a, o):
        if a in (0, lat_blocks - 1):
            return a, (o + lon_blocks // 2) % lon_blocks
        return ((a + 1) ^ 1) - 1, o

    pairs = [
        (index(a, o), index(*other_lat(a, o))) for a in range(lat_blocks) for o in range(lon_blocks)
    ]
    ghost_a = lax.ppermute(lat_a, "lat", [(a, a ^ 1) for a in range(lat_blocks)])
    ghost_b = lax.ppermute(lat_b, axes, pairs)

    block = jax.ShapeDtypeStruct(east_adjoint.shape, f32)
    _, final, edges = pl.pallas_call(
        lambda *refs: fix_kernel(lat_blocks, band, *refs),
        out_shape=(
            in_vmem(3, 2, 512, LANES), in_vmem(3, 2, 512, LANES), in_vmem(2, 12, 8, SPAN)
        ),
        in_specs=[VMEM] * 11,
        out_specs=(VMEM,) * 3,
        input_output_aliases={0: 0},
        scratch_shapes=[
            pltpu.VMEM((3, 1, 512, LANES), f32),
            pltpu.VMEM((MAXP + 2 * SIDE, 8, LANES), f32),
            pltpu.VMEM((MAXP + SIDE, 8, LANES), f32),
        ],
        compiler_params=params(),
        cost_estimate=pl.CostEstimate(flops=50000000, bytes_accessed=10000000, transcendentals=0),
        name="fix",
    )(
        inner, inner_f, inner_edges, winds, heights, recv_b, recv_a, zon_wide, mer_wide, counts, weights,
    )

    return pl.pallas_call(
        lambda *refs: finish_kernel(lat_blocks, *refs),
        out_shape=(block,) * 3,
        in_specs=[VMEM] * 8,
        out_specs=(HBM,) * 3,
        scratch_shapes=[
            pltpu.VMEM((3, 2, 2, 64, LANES), f32),
            pltpu.SemaphoreType.DMA((3, 2)),
            pltpu.SemaphoreType.DMA((3, 2, 2)),
        ],
        compiler_params=params(),
        name="finish",
    )(
        edges, own_edges, final, ghost_b, ghost_a, zonal_courant, meridional_courant, columns
    )


def solution(mesh):
    sizes = dict(mesh.shape)
    axes = tuple(mesh.axis_names)
    spread_out = P(None, "lat", "lon")
    return jax.shard_map(
        lambda *args: body(sizes["lat"], sizes["lon"], axes, *args),
        mesh=mesh,
        in_specs=(spread_out,) * 3 + (P(None, "lat"), P(None, "lat"), P(), P()),
        out_specs=(spread_out,) * 3,
        check_vma=False,
    )
```

```python
import jax
import jax.numpy as jnp
from jax import lax
from jax.experimental import pallas as pl
from jax.experimental.pallas import tpu as pltpu
from jax.sharding import PartitionSpec as P

MAXP = 16
REACH = 3
WIDE = MAXP + REACH
LANES = 128
SPAN = 3 * LANES
SHARE = 33

gravity_weight = 0.3
divergence_weight = 0.3

VMEM = pl.BlockSpec(memory_space=pltpu.VMEM)
SMEM = pl.BlockSpec(memory_space=pltpu.SMEM)
HBM = pl.BlockSpec(memory_space=pltpu.HBM)

EDGE_SLOTS = ((0, 0), (0, 1), (1, 0), (1, 1), (1, 2), (2, 0), (2, 1))


HEIGHTS = 8 * WIDE
EDGES = 12 * WIDE
PAYLOAD = 248


def lanes():
    return lax.broadcasted_iota(jnp.int32, (8, LANES), 1)


def turn(values, steps):
    return pltpu.roll(values, steps % values.shape[-1], values.ndim - 1)


def zonal(values):
    return turn(values, -1) - turn(values, 1)


def is_even(axis):
    return lax.rem(lax.axis_index(axis), 2) == 0


def row_count(counts_ref, row, rows, lat_blocks):
    band = counts_ref.shape[0] // 2
    blocks = band // rows
    position = lax.axis_index("lat")
    north = position < blocks
    south = position >= lat_blocks - blocks
    place = jnp.where(north, position, jnp.where(south, position - lat_blocks + 2 * blocks, 0))
    return jnp.where(north | south, counts_ref[place * rows + row], 0)


def undo(count):
    power = jnp.left_shift(1, MAXP - count).astype(jnp.float32)
    return power * power * (2.0 ** (-2 * MAXP))


class Stream:
    GROUPS = (1, 1, 2, 4, 8)

    def __init__(self, masks):
        self.masks = masks

    def start(self):
        zero = jnp.zeros((8, LANES), jnp.float32)
        return [zero] * (2 * MAXP + sum(self.GROUPS))

    def step(self, state, tile):
        state = list(state)
        at, later = 0, 2 * MAXP
        for mask, size in zip(self.masks, self.GROUPS):
            entered = tile
            for _ in range(size):
                half = state[at] + tile
                state[at], tile = tile, state[at + 1] + half
                state[at + 1] = half
                at += 2
            delayed = state[later]
            state[later : later + size] = state[later + 1 : later + size] + [entered]
            later += size
            tile = jnp.where(mask, tile, delayed)
        return state, tile


def group_masks(count):
    rest = count - 1
    bits = [jnp.bitwise_and(jnp.right_shift(rest, b), 1) == 1 for b in range(4)]
    used = count > 0
    return [used] + [used & bit for bit in bits]


def pack_kernel(
    e_hbm, n_hbm, h_hbm, a_ref, b_ref, wind_ref, height_ref, edge_ref, x_ref, t_ref, sems
):
    copies = []
    for f, ref in enumerate((e_hbm, n_hbm, h_hbm)):
        for t in range(2):
            copy = pltpu.make_async_copy(
                ref.at[:, :, pl.ds(LANES * t, LANES)],
                x_ref.at[f, t].reshape(8, 64, LANES),
                sems.at[f, t],
            )
            copy.start()
            copies.append(copy)
    winds = wind_ref.reshape(256 * 8, LANES)
    for f in range(3):
        for t in range(2):
            copies[2 * f + t].wait()
            for q in range(4):
                turned = x_ref[f, t, pl.ds(LANES * q, LANES), :].T
                if f < 2:
                    winds[pl.ds(1024 * t + 4 * f + q, LANES, stride=8), :] = turned
                else:
                    height_ref[pl.ds(512 * t + q, LANES, stride=4), :] = turned
    for side in range(2):
        for slot, (field, distance) in enumerate(EDGE_SLOTS):
            row = 63 - distance if side else distance
            place = 8 * (len(EDGE_SLOTS) * side + slot)
            for t in range(2):
                t_ref[t, pl.ds(place, 8), :] = x_ref[field, t, pl.ds(row, 8, stride=64), :]
    for t in range(2):
        t_ref[t, pl.ds(112, 16), :] = jnp.zeros((16, LANES), jnp.float32)
        edge_ref[pl.ds(LANES * t, LANES), :] = t_ref[t].T
    even = is_even("lon")
    last = 256 - WIDE
    for ref, right in ((a_ref, even), (b_ref, jnp.logical_not(even))):
        first = jnp.where(right, last, 0)
        ref[pl.ds(0, 8 * WIDE), :] = wind_ref[pl.ds(first, WIDE)].reshape(8 * WIDE, LANES)
        ref[pl.ds(HEIGHTS, 4 * WIDE), :] = jnp.where(
            right, height_ref[pl.ds(4 * last, 4 * WIDE), :], height_ref[pl.ds(0, 4 * WIDE), :]
        )
        ref[pl.ds(EDGES, WIDE), :] = jnp.where(
            right, edge_ref[pl.ds(last, WIDE), :], edge_ref[pl.ds(0, WIDE), :]
        )


def edge_kernel(
    lat_blocks, band,
    turned_ref, rb_ref, ra_ref, count_ref, mer_ref, a_ref, b_ref, own_ref, z_ref, o_ref
):
    even_lon = is_even("lon")
    even_lat = is_even("lat")
    lane = lanes()
    halo = pl.ds(EDGES, WIDE)
    z_ref[pl.ds(24, 256), :] = turned_ref[...]
    z_ref[pl.ds(24 - WIDE, WIDE), :] = jnp.where(even_lon, rb_ref[halo, :], ra_ref[halo, :])
    z_ref[pl.ds(280, WIDE), :] = jnp.where(even_lon, ra_ref[halo, :], rb_ref[halo, :])
    z_ref[pl.ds(280 + WIDE, 5), :] = jnp.zeros((5, LANES), jnp.float32)
    polar = is_polar(lat_blocks, 64, band)

    @pl.when(jnp.logical_not(polar))
    def _():
        o_ref[...] = z_ref[pl.ds(24 - REACH, 8 * SHARE), :]

    @pl.when(polar)
    def _():
        count = count_ref[...]
        stream = Stream(group_masks(count))
        scale = undo(count)
        state = stream.start()
        for i in range(SHARE + 2 * MAXP):
            state, tile = stream.step(state, z_ref[pl.ds(24 - WIDE + i, 8, stride=SHARE), :])
            if i >= 2 * MAXP:
                o_ref[pl.ds(i - 2 * MAXP, 8, stride=SHARE), :] = tile * scale

    first = o_ref[pl.ds(REACH, LANES), :].T
    second = o_ref[pl.ds(REACH + LANES, LANES), :].T
    o_ref[pl.ds(REACH, REACH), :] = o_ref[pl.ds(REACH + 2 * LANES, REACH), :]
    third = o_ref[pl.ds(0, LANES), :].T
    packs = []
    for side in range(2):
        sense = -1.0 if side else 1.0

        def row(field, distance):
            slot = EDGE_SLOTS.index((field, distance))
            place = 8 * (len(EDGE_SLOTS) * side + slot)
            own = slice(place, place + 8)
            return jnp.concatenate([first[own], second[own], turn(third[own], -REACH)], axis=-1)

        e0, e1, n0, n1, n2, h0, h1 = (row(*slot) for slot in EDGE_SLOTS)
        outer = h0 + gravity_weight * (zonal(e0) + sense * n1)
        inner = h1 + gravity_weight * (zonal(e1) + sense * (n2 - n0))
        own_ref[side] = outer
        at = 63 if side else 0
        pack = jnp.broadcast_to(mer_ref[:, at : at + 1], (8, LANES))
        out = []
        for slot, value in enumerate((outer, inner, e0, n0)):
            out += [value[:, :LANES], value[:, LANES : 2 * LANES]]
            start = 2 * REACH * slot
            inside = (lane >= start) & (lane < start + 2 * REACH)
            pack = jnp.where(inside, turn(value[:, 2 * LANES :], REACH + start), pack)
        packs.append(out + [pack])
    for place, (top, bottom) in enumerate(zip(*packs)):
        a_ref[pl.ds(8 * place, 8)] = jnp.where(even_lat, bottom, top)
        b_ref[pl.ds(8 * place, 8)] = jnp.where(even_lat, top, bottom)


def following(rows):
    count = rows.shape[0]
    return pltpu.roll(rows, count - 1, 0) - pltpu.roll(rows, 1, 0)


def is_polar(lat_blocks, rows, band):
    position = lax.axis_index("lat")
    return (position < band // rows) | (position >= lat_blocks - band // rows)


def leaves_results(lat_blocks, rows, band):
    position = lax.axis_index("lat")
    return (position == band // rows - 1) | (position >= lat_blocks - band // rows)


def whole(f_ref, f, start, rows):
    tiles = range(f_ref.shape[1])
    return jnp.concatenate([f_ref[f, t, pl.ds(start, rows), :] for t in tiles], axis=-1)


def new_heights(f_ref, v_ref):
    tiles = f_ref.shape[1]

    def weight(k, l):
        return jnp.concatenate([v_ref[k, l]] * tiles, axis=-1)

    for first in range(0, 64, 8):
        old = []
        for l in range(8):
            start = 64 * l + first
            north = whole(f_ref, 1, start, 8)
            above = whole(f_ref, 1, start - 1, 8) if start else pltpu.roll(north, 1, 0)
            below = whole(f_ref, 1, start + 1, 8) if start < 512 - 8 else pltpu.roll(north, 7, 0)
            slope = zonal(whole(f_ref, 0, start, 8)) + (below - above)
            old.append(whole(f_ref, 2, start, 8) + gravity_weight * slope)
        for l in range(8):
            total = weight(0, l) * old[0]
            for k in range(1, 8):
                total = total + weight(k, l) * old[k]
            for t in range(tiles):
                place = pl.ds(64 * l + first, 8)
                f_ref[2, t, place, :] = total[:, LANES * t : LANES * (t + 1)]


def results(f_ref, zb_ref, mb_ref, write):
    tiles = f_ref.shape[1]
    for l in range(8):
        h2 = whole(f_ref, 2, 64 * l, 64)
        h2_zonal = zonal(h2)
        e1 = whole(f_ref, 0, 64 * l, 64) + divergence_weight * h2_zonal
        n1 = whole(f_ref, 1, 64 * l, 64) + divergence_weight * following(h2)
        zon = jnp.concatenate([zb_ref[l]] * tiles, axis=-1)
        mer = jnp.concatenate([mb_ref[l]] * tiles, axis=-1)
        for f, field in enumerate((e1, n1, h2)):
            slope = h2_zonal if f == 2 else zonal(field)
            write(f, l, field + zon * slope + following(mer * field))


def edge_row(side, distance):
    return 63 - distance if side else distance


def inner_results(f_ref, zb_ref, mb_ref, ob_ref):
    def write(f, l, value):
        for t in range(2):
            ob_ref[f, t, pl.ds(64 * l, 64), :] = value[:, LANES * t : LANES * (t + 1)]

    results(f_ref, zb_ref, mb_ref, write)


def interior_kernel(
    lat_blocks,
    _, wind_ref, height_ref, counts_ref, zon_ref, mer_ref, v_ref,
    f_ref, ob_ref, edge_ref, zb_ref, mb_ref, count_ref, edge_count_ref, vb_ref, vc_ref,
    wo_ref, ho_ref,
):
    lane = lanes()
    level = lax.broadcasted_iota(jnp.int32, (8, LANES), 0)
    polar = is_polar(lat_blocks, 64, counts_ref.shape[0] // 2)

    @pl.when(polar)
    def _():
        count = jnp.zeros((8, LANES), jnp.int32)
        for row in range(64):
            value = row_count(counts_ref, row, 64, lat_blocks)
            count = jnp.where(jnp.bitwise_and(lane, 63) == row, value, count)
        count_ref[...] = count
        count = jnp.zeros((8, LANES), jnp.int32)
        for side in range(2):
            for slot, (_, distance) in enumerate(EDGE_SLOTS):
                value = row_count(counts_ref, edge_row(side, distance), 64, lat_blocks)
                place = 8 * (len(EDGE_SLOTS) * side + slot)
                count = jnp.where(lane >= place, value, count)
        edge_count_ref[...] = count

    @pl.when(jnp.logical_not(polar))
    def _():
        count_ref[...] = jnp.zeros((8, LANES), jnp.int32)
        edge_count_ref[...] = jnp.zeros((8, LANES), jnp.int32)

    @pl.when(polar)
    def _():
        count = count_ref[...]
        stream = Stream(group_masks(count))
        scale = undo(count)

        def winds(chunk, state):
            for u in range(8):
                i = 8 * chunk + u
                state, tile = stream.step(state, wind_ref[i])
                wo_ref[i] = tile * scale
            return tuple(state)

        lax.fori_loop(0, 32, winds, tuple(stream.start()))

        def heights(chunk, state):
            for u in range(0, 8, 2):
                i = 8 * chunk + u
                low = height_ref[pl.ds(pl.multiple_of(4 * i, 8), 8), :]
                high = height_ref[pl.ds(pl.multiple_of(4 * i + 448, 8), 8), :]
                pair = jnp.where(level < 4, low, pltpu.roll(high, 4, 0))
                state, tile = stream.step(state, pair)
                ho_ref[i] = tile * scale
                pair = jnp.where(level < 4, pltpu.roll(low, 4, 0), high)
                state, tile = stream.step(state, pair)
                ho_ref[i + 1] = tile * scale
            return tuple(state)

        lax.fori_loop(0, 18, heights, tuple(stream.start()))
        wo = wo_ref.reshape(wo_ref.shape[0] * 8, LANES)
        ho = ho_ref.reshape(ho_ref.shape[0] * 8, LANES)
        for f in range(3):
            for q in range(4):
                for t in range(2):
                    if f < 2:
                        tall = wo[pl.ds(8 * (MAXP + LANES * t) + 4 * f + q, LANES, stride=8), :]
                    else:
                        tall = ho[pl.ds(8 * MAXP * (1 + t) + q + 4 * t, LANES, stride=8), :]
                    f_ref[f, t, pl.ds(LANES * q, LANES), :] = tall.T

    def keep_edge(slot, field, distance):
        for side in range(2):
            for t in range(2):
                place = pl.ds(edge_row(side, distance), 8, stride=64)
                edge_ref[side, slot, :, pl.ds(LANES * t, LANES)] = f_ref[field, t, place, :]

    for d in range(4):
        keep_edge(d, 0, d)
        keep_edge(4 + d, 1, d)
    for k in range(8):
        for l in range(8):
            vb_ref[k, l] = jnp.full((8, LANES), v_ref[k, l], jnp.float32)
    for k, column in enumerate(mixing(v_ref)):
        vc_ref[k] = column
    for l in range(8):
        zb_ref[l] = jnp.broadcast_to(zon_ref[l : l + 1, :], (LANES, 64)).T
        mb_ref[l] = jnp.broadcast_to(mer_ref[l : l + 1, :], (LANES, 64)).T

    new_heights(f_ref, vb_ref)
    for d in range(1, 5):
        keep_edge(7 + d, 2, d)

    @pl.when(jnp.logical_not(leaves_results(lat_blocks, 64, counts_ref.shape[0] // 2)))
    def _():
        inner_results(f_ref, zb_ref, mb_ref, ob_ref)


SIDE = 64
OWN = SIDE - WIDE


def fix_kernel(
    lat_blocks, band,
    _, inner_f_ref, inner_ref, wind_ref, height_ref, rb_ref, ra_ref, zb_ref, mb_ref, count_ref, v_ref,
    ob_ref, all_ref, edge_ref,
    f_ref, wz_ref, hz_ref,
):
    even_lon = is_even("lon")
    level = lax.broadcasted_iota(jnp.int32, (8, LANES), 0)
    polar = is_polar(lat_blocks, 64, band)

    @pl.when(leaves_results(lat_blocks, 64, band))
    def _():
        inner_results(inner_f_ref, zb_ref, mb_ref, ob_ref)

    def left(place):
        return jnp.where(even_lon, rb_ref[place, :], ra_ref[place, :])

    def right(place):
        return jnp.where(even_lon, ra_ref[place, :], rb_ref[place, :])

    for i in range(WIDE):
        wz_ref[MAXP + i] = left(pl.ds(8 * i, 8))
        wz_ref[MAXP + SIDE + OWN + i] = right(pl.ds(8 * i, 8))
    wz_ref[pl.ds(MAXP + WIDE, OWN)] = wind_ref[pl.ds(0, OWN)]
    wz_ref[pl.ds(MAXP + SIDE, OWN)] = wind_ref[pl.ds(256 - OWN, OWN)]
    for i in range(SIDE):
        if i < WIDE:
            low = left(pl.ds(HEIGHTS + 4 * i, 8))
        else:
            low = height_ref[pl.ds(4 * (i - WIDE), 8), :]
        if i < OWN:
            high = height_ref[pl.ds(4 * (256 - OWN + i) - 4, 8), :]
        else:
            high = right(pl.ds(HEIGHTS + 4 * (i - OWN) - 4, 8))
        hz_ref[MAXP + i] = jnp.where(level < 4, low, high)

    @pl.when(polar)
    def _():
        count = count_ref[...]
        stream = Stream(group_masks(count))
        scale = undo(count)

        def run(ref, base):
            def steps(chunk, state):
                for u in range(8):
                    i = base + 8 * chunk + u
                    state, tile = stream.step(state, ref[MAXP + i])
                    ref[i] = tile * scale
                return tuple(state)

            lax.fori_loop(0, SIDE // 8, steps, tuple(stream.start()))

        run(wz_ref, 0)
        run(wz_ref, SIDE)
        run(hz_ref, 0)

    wz = wz_ref.reshape(wz_ref.shape[0] * 8, LANES)
    hz = hz_ref.reshape(hz_ref.shape[0] * 8, LANES)
    for f in range(3):
        for q in range(4):
            if f < 2:
                tall = wz[pl.ds(8 * MAXP + 4 * f + q, LANES, stride=8), :]
            else:
                parts = [hz[pl.ds(8 * MAXP + q + 4 * s, SIDE, stride=8), :] for s in range(2)]
                tall = jnp.concatenate(parts, axis=0)
            f_ref[f, 0, pl.ds(LANES * q, LANES), :] = tall.T

    lane = lanes()

    def keep_edge(slot, field, distance):
        for side in range(2):
            near = f_ref[field, 0, pl.ds(edge_row(side, distance), 8, stride=64), :]
            west, east = turn(near, -WIDE), turn(near, WIDE)
            first, second = inner_ref[side, slot, :, :LANES], inner_ref[side, slot, :, LANES:]
            edge_ref[side, slot, :, pl.ds(0, LANES)] = jnp.where(lane < 24, west, first)
            edge_ref[side, slot, :, pl.ds(LANES, LANES)] = jnp.where(lane >= 104, east, second)
            edge_ref[side, slot, :, pl.ds(2 * LANES, LANES)] = jnp.where(lane < 64, east, west)

    for d in range(4):
        keep_edge(d, 0, d)
        keep_edge(4 + d, 1, d)

    new_heights(f_ref, v_ref)
    for d in range(1, 5):
        keep_edge(7 + d, 2, d)
    wide_lane = lax.broadcasted_iota(jnp.int32, (64, LANES), 1)

    def write(f, l, near):
        west, east = turn(near, -WIDE), turn(near, WIDE)
        rows = pl.ds(64 * l, 64)
        all_ref[f, 0, rows, :] = jnp.where(wide_lane < 22, west, ob_ref[f, 0, rows, :])
        all_ref[f, 1, rows, :] = jnp.where(wide_lane >= 106, east, ob_ref[f, 1, rows, :])

    results(f_ref, zb_ref, mb_ref, write)


def mixing(v_ref):
    level = lax.broadcasted_iota(jnp.int32, (8, LANES), 0)
    columns = []
    for k in range(8):
        column = jnp.full((8, LANES), v_ref[k, 0], jnp.float32)
        for l in range(1, 8):
            column = jnp.where(level == l, v_ref[k, l], column)
        columns.append(column)
    return columns


def mix(columns, height):
    tiles = []
    for t in range(height.shape[-1] // LANES):
        tile = height[..., t * LANES : (t + 1) * LANES]
        total = None
        for k, column in enumerate(columns):
            term = column * jnp.broadcast_to(tile[..., k : k + 1, :], tile.shape)
            total = term if total is None else total + term
        tiles.append(total)
    return jnp.concatenate(tiles, axis=-1)


def wide(column):
    return jnp.concatenate([column] * (SPAN // LANES), axis=-1)


def finish_kernel(
    lat_blocks,
    edge_ref, own_ref, all_ref, gb_ref, ga_ref, zon_ref, mer_ref, v_ref,
    oe_ref, on_ref, oh_ref,
    ob_ref, sems, edge_sems,
):
    outs = (oe_ref, on_ref, oh_ref)
    copies = []
    for f, out in enumerate(outs):
        for t in range(2):
            copy = pltpu.make_async_copy(
                all_ref.at[f, t].reshape(8, 64, LANES).at[:, pl.ds(8, 48)],
                out.at[:, pl.ds(8, 48), pl.ds(LANES * t, LANES)],
                sems.at[f, t],
            )
            copy.start()
            copies.append(copy)
    position = lax.axis_index("lat")
    even_lat = is_even("lat")
    lane = lanes()
    columns = [v_ref[k] for k in range(8)]
    for side in range(2):
        top = side == 0
        sense = 1.0 if top else -1.0
        pole = position == (0 if top else lat_blocks - 1)
        turned = jnp.where(pole, -1.0, 1.0)

        def ghost_tile(place):
            a, b = ga_ref[pl.ds(8 * place, 8)], gb_ref[pl.ds(8 * place, 8)]
            return jnp.where(even_lat, b, a) if top else jnp.where(even_lat, a, b)

        pack = ghost_tile(8)

        def ghost(slot):
            third = turn(pack, -REACH - 2 * REACH * slot)
            return jnp.concatenate([ghost_tile(2 * slot), ghost_tile(2 * slot + 1), third], axis=-1)

        e = {d: edge_ref[side, d] for d in range(4)}
        n = {d: edge_ref[side, 4 + d] for d in range(4)}
        h2 = {d: edge_ref[side, 7 + d] for d in range(1, 5)}
        e[-1] = ghost(2)
        n[-1] = ghost(3) * turned
        h2[-2] = mix(columns, ghost(1))
        h2[-1] = mix(columns, ghost(0) + (gravity_weight * sense) * n[0])
        h2[0] = mix(columns, own_ref[side] - (gravity_weight * sense) * n[-1])
        e1, n1, h2_zonal = {}, {}, {}
        for d in range(-1, 4):
            h2_zonal[d] = zonal(h2[d])
            e1[d] = e[d] + divergence_weight * h2_zonal[d]
            n1[d] = n[d] + (divergence_weight * sense) * (h2[d + 1] - h2[d - 1])
        mer_ghost = wide(jnp.where(lane < LANES // 2, turn(pack, LANES // 2), pack))

        def coefficient(ref, d):
            row = edge_row(side, d)
            return wide(jnp.broadcast_to(ref[:, row : row + 1], (8, LANES)))

        zon = {d: coefficient(zon_ref, d) for d in range(3)}
        mer = {d: coefficient(mer_ref, d) for d in range(4)}
        for f, field in enumerate((e1, n1, h2)):
            mer[-1] = mer_ghost if f == 0 else mer_ghost * turned
            flow = {d: mer[d] * field[d] for d in range(-1, 4)}
            for t in range(2):
                for l in range(8):
                    ob_ref[f, side, t, pl.ds(8 * l, 8), :] = all_ref[
                        f, t, pl.ds(64 * l + 56 * side, 8), :
                    ]
            for d in range(3 if f == 1 else 2):
                slope = h2_zonal[d] if f == 2 else zonal(field[d])
                value = field[d] + zon[d] * slope + sense * (flow[d + 1] - flow[d - 1])
                for t in range(2):
                    ob_ref[f, side, t, pl.ds(d if top else 7 - d, 8, stride=8), :] = value[
                        :, LANES * t : LANES * (t + 1)
                    ]
    for side in range(2):
        for f, out in enumerate(outs):
            for t in range(2):
                copy = pltpu.make_async_copy(
                    ob_ref.at[f, side, t].reshape(8, 8, LANES),
                    out.at[:, pl.ds(56 * side, 8), pl.ds(LANES * t, LANES)],
                    edge_sems.at[f, side, t],
                )
                copy.start()
                copies.append(copy)
    for copy in copies:
        copy.wait()


def body(
    lat_blocks, lon_blocks, axes,
    east_adjoint, north_adjoint, height_adjoint,
    zonal_courant, meridional_courant, vertical_inverse, pass_counts,
):
    f32 = jnp.float32
    fields = tuple(
        pltpu.with_memory_space_constraint(x, pltpu.HBM)
        for x in (east_adjoint, north_adjoint, height_adjoint)
    )

    def in_vmem(*dims):
        return pltpu.VMEM(dims, f32)

    def params():
        return pltpu.CompilerParams(vmem_limit_bytes=40 * 1024 * 1024)

    lon_a, lon_b, winds, heights, edge_rows, local = pl.pallas_call(
        pack_kernel,
        out_shape=(
            in_vmem(PAYLOAD, LANES), in_vmem(PAYLOAD, LANES),
            in_vmem(256, 8, LANES), in_vmem(1024, LANES), in_vmem(256, LANES),
            in_vmem(3, 2, 512, LANES),
        ),
        in_specs=[HBM] * 3,
        out_specs=(VMEM,) * 6,
        scratch_shapes=[pltpu.VMEM((2, LANES, LANES), f32), pltpu.SemaphoreType.DMA((3, 2))],
        compiler_params=params(),
        name="pack",
    )(*fields)

    def other_lon(o):
        return (((o + 1) ^ 1) - 1) % lon_blocks

    recv_a = lax.ppermute(lon_a, "lon", [(o, o ^ 1) for o in range(lon_blocks)])
    recv_b = lax.ppermute(lon_b, "lon", [(o, other_lon(o)) for o in range(lon_blocks)])

    by_row = in_vmem(8, 64, LANES)
    by_count = pltpu.VMEM((8, LANES), jnp.int32)
    inner_f, inner, inner_edges, zon_wide, mer_wide, counts, edge_counts, weights, columns = pl.pallas_call(
        lambda *refs: interior_kernel(lat_blocks, *refs),
        out_shape=(
            in_vmem(3, 2, 512, LANES), in_vmem(3, 2, 512, LANES), in_vmem(2, 12, 8, 256),
            by_row, by_row, by_count, by_count, in_vmem(8, 8, 8, LANES), in_vmem(8, 8, LANES),
        ),
        in_specs=[VMEM] * 3 + [SMEM, VMEM, VMEM, SMEM],
        out_specs=(VMEM,) * 9,
        input_output_aliases={0: 0},
        scratch_shapes=[
            pltpu.VMEM((272, 8, LANES), f32),
            pltpu.VMEM((160, 8, LANES), f32),
        ],
        compiler_params=params(),
        cost_estimate=pl.CostEstimate(flops=100000000, bytes_accessed=20000000, transcendentals=0),
        name="interior",
    )(
        local, winds, heights, pass_counts, zonal_courant, meridional_courant, vertical_inverse
    )

    band = pass_counts.shape[0] // 2
    lat_a, lat_b, own_edges = pl.pallas_call(
        lambda *refs: edge_kernel(lat_blocks, band, *refs),
        out_shape=(in_vmem(72, LANES), in_vmem(72, LANES), in_vmem(2, 8, SPAN)),
        in_specs=[VMEM] * 5,
        out_specs=(VMEM,) * 3,
        scratch_shapes=[pltpu.VMEM((304, LANES), f32), pltpu.VMEM((264, LANES), f32)],
        compiler_params=params(),
        name="edge",
    )(edge_rows, recv_b, recv_a, edge_counts, meridional_courant)

    def index(a, o):
        return o * lat_blocks + a if axes[0] == "lon" else a * lon_blocks + o

    def other_lat(a, o):
        if a in (0, lat_blocks - 1):
            return a, (o + lon_blocks // 2) % lon_blocks
        return ((a + 1) ^ 1) - 1, o

    pairs = [
        (index(a, o), index(*other_lat(a, o))) for a in range(lat_blocks) for o in range(lon_blocks)
    ]
    ghost_a = lax.ppermute(lat_a, "lat", [(a, a ^ 1) for a in range(lat_blocks)])
    ghost_b = lax.ppermute(lat_b, axes, pairs)

    block = jax.ShapeDtypeStruct(east_adjoint.shape, f32)
    _, final, edges = pl.pallas_call(
        lambda *refs: fix_kernel(lat_blocks, band, *refs),
        out_shape=(
            in_vmem(3, 2, 512, LANES), in_vmem(3, 2, 512, LANES), in_vmem(2, 12, 8, SPAN)
        ),
        in_specs=[VMEM] * 11,
        out_specs=(VMEM,) * 3,
        input_output_aliases={0: 0},
        scratch_shapes=[
            pltpu.VMEM((3, 1, 512, LANES), f32),
            pltpu.VMEM((MAXP + 2 * SIDE, 8, LANES), f32),
            pltpu.VMEM((MAXP + SIDE, 8, LANES), f32),
        ],
        compiler_params=params(),
        cost_estimate=pl.CostEstimate(flops=50000000, bytes_accessed=10000000, transcendentals=0),
        name="fix",
    )(
        inner, inner_f, inner_edges, winds, heights, recv_b, recv_a, zon_wide, mer_wide, counts, weights,
    )

    return pl.pallas_call(
        lambda *refs: finish_kernel(lat_blocks, *refs),
        out_shape=(block,) * 3,
        in_specs=[VMEM] * 8,
        out_specs=(HBM,) * 3,
        scratch_shapes=[
            pltpu.VMEM((3, 2, 2, 64, LANES), f32),
            pltpu.SemaphoreType.DMA((3, 2)),
            pltpu.SemaphoreType.DMA((3, 2, 2)),
        ],
        compiler_params=params(),
        name="finish",
    )(
        edges, own_edges, final, ghost_b, ghost_a, zonal_courant, meridional_courant, columns
    )


def solution(mesh):
    sizes = dict(mesh.shape)
    axes = tuple(mesh.axis_names)
    spread_out = P(None, "lat", "lon")
    return jax.shard_map(
        lambda *args: body(sizes["lat"], sizes["lon"], axes, *args),
        mesh=mesh,
        in_specs=(spread_out,) * 3 + (P(None, "lat"), P(None, "lat"), P(), P()),
        out_specs=(spread_out,) * 3,
        check_vma=False,
    )
```

```python
import jax
import jax.numpy as jnp
from jax import lax
from jax.experimental import pallas as pl
from jax.experimental.pallas import tpu as pltpu
from jax.sharding import PartitionSpec as P

MAXP = 16
REACH = 3
WIDE = MAXP + REACH
LANES = 128
SPAN = 3 * LANES
SHARE = 33

gravity_weight = 0.3
divergence_weight = 0.3

VMEM = pl.BlockSpec(memory_space=pltpu.VMEM)
SMEM = pl.BlockSpec(memory_space=pltpu.SMEM)
HBM = pl.BlockSpec(memory_space=pltpu.HBM)

EDGE_SLOTS = ((0, 0), (0, 1), (1, 0), (1, 1), (1, 2), (2, 0), (2, 1))


HEIGHTS = 8 * WIDE
EDGES = 12 * WIDE
PAYLOAD = 248


def lanes():
    return lax.broadcasted_iota(jnp.int32, (8, LANES), 1)


def turn(values, steps):
    return pltpu.roll(values, steps % values.shape[-1], values.ndim - 1)


def zonal(values):
    return turn(values, -1) - turn(values, 1)


def is_even(axis):
    return lax.rem(lax.axis_index(axis), 2) == 0


def row_count(counts_ref, row, rows, lat_blocks):
    band = counts_ref.shape[0] // 2
    blocks = band // rows
    position = lax.axis_index("lat")
    north = position < blocks
    south = position >= lat_blocks - blocks
    place = jnp.where(north, position, jnp.where(south, position - lat_blocks + 2 * blocks, 0))
    return jnp.where(north | south, counts_ref[place * rows + row], 0)


def undo(count):
    power = jnp.left_shift(1, MAXP - count).astype(jnp.float32)
    return power * power * (2.0 ** (-2 * MAXP))


class Stream:
    GROUPS = (1, 1, 2, 4, 8)

    def __init__(self, masks):
        self.masks = masks

    def start(self):
        zero = jnp.zeros((8, LANES), jnp.float32)
        return [zero] * (2 * MAXP + sum(self.GROUPS))

    def step(self, state, tile):
        state = list(state)
        at, later = 0, 2 * MAXP
        for mask, size in zip(self.masks, self.GROUPS):
            entered = tile
            for _ in range(size):
                half = state[at] + tile
                state[at], tile = tile, state[at + 1] + half
                state[at + 1] = half
                at += 2
            delayed = state[later]
            state[later : later + size] = state[later + 1 : later + size] + [entered]
            later += size
            tile = jnp.where(mask, tile, delayed)
        return state, tile


def group_masks(count):
    rest = count - 1
    bits = [jnp.bitwise_and(jnp.right_shift(rest, b), 1) == 1 for b in range(4)]
    used = count > 0
    return [used] + [used & bit for bit in bits]


def pack_kernel(
    e_hbm, n_hbm, h_hbm, a_ref, b_ref, wind_ref, height_ref, edge_ref, x_ref, t_ref, sems
):
    copies = []
    for f, ref in enumerate((e_hbm, n_hbm, h_hbm)):
        for t in range(2):
            copy = pltpu.make_async_copy(
                ref.at[:, :, pl.ds(LANES * t, LANES)],
                x_ref.at[f, t].reshape(8, 64, LANES),
                sems.at[f, t],
            )
            copy.start()
            copies.append(copy)
    winds = wind_ref.reshape(256 * 8, LANES)
    for f in range(3):
        for t in range(2):
            copies[2 * f + t].wait()
            for q in range(4):
                turned = x_ref[f, t, pl.ds(LANES * q, LANES), :].T
                if f < 2:
                    winds[pl.ds(1024 * t + 4 * f + q, LANES, stride=8), :] = turned
                else:
                    height_ref[pl.ds(512 * t + q, LANES, stride=4), :] = turned
    for side in range(2):
        for slot, (field, distance) in enumerate(EDGE_SLOTS):
            row = 63 - distance if side else distance
            place = 8 * (len(EDGE_SLOTS) * side + slot)
            for t in range(2):
                t_ref[t, pl.ds(place, 8), :] = x_ref[field, t, pl.ds(row, 8, stride=64), :]
    for t in range(2):
        t_ref[t, pl.ds(112, 16), :] = jnp.zeros((16, LANES), jnp.float32)
        edge_ref[pl.ds(LANES * t, LANES), :] = t_ref[t].T
    even = is_even("lon")
    last = 256 - WIDE
    for ref, right in ((a_ref, even), (b_ref, jnp.logical_not(even))):
        first = jnp.where(right, last, 0)
        ref[pl.ds(0, 8 * WIDE), :] = wind_ref[pl.ds(first, WIDE)].reshape(8 * WIDE, LANES)
        ref[pl.ds(HEIGHTS, 4 * WIDE), :] = jnp.where(
            right, height_ref[pl.ds(4 * last, 4 * WIDE), :], height_ref[pl.ds(0, 4 * WIDE), :]
        )
        ref[pl.ds(EDGES, WIDE), :] = jnp.where(
            right, edge_ref[pl.ds(last, WIDE), :], edge_ref[pl.ds(0, WIDE), :]
        )


def edge_kernel(
    lat_blocks, band,
    turned_ref, rb_ref, ra_ref, count_ref, mer_ref, a_ref, b_ref, own_ref, z_ref, o_ref
):
    even_lon = is_even("lon")
    even_lat = is_even("lat")
    lane = lanes()
    polar = is_polar(lat_blocks, 64, band)

    @pl.when(jnp.logical_not(polar))
    def _():
        west, east = pl.ds(EDGES + MAXP, REACH), pl.ds(EDGES, REACH)
        o_ref[pl.ds(0, REACH), :] = jnp.where(even_lon, rb_ref[west, :], ra_ref[west, :])
        o_ref[pl.ds(REACH, 256), :] = turned_ref[...]
        o_ref[pl.ds(REACH + 256, REACH), :] = jnp.where(even_lon, ra_ref[east, :], rb_ref[east, :])

    @pl.when(polar)
    def _():
        halo = pl.ds(EDGES, WIDE)
        z_ref[pl.ds(24, 256), :] = turned_ref[...]
        z_ref[pl.ds(24 - WIDE, WIDE), :] = jnp.where(even_lon, rb_ref[halo, :], ra_ref[halo, :])
        z_ref[pl.ds(280, WIDE), :] = jnp.where(even_lon, ra_ref[halo, :], rb_ref[halo, :])
        z_ref[pl.ds(280 + WIDE, 5), :] = jnp.zeros((5, LANES), jnp.float32)
        count = count_ref[...]
        stream = Stream(group_masks(count))
        scale = undo(count)
        state = stream.start()
        for i in range(SHARE + 2 * MAXP):
            state, tile = stream.step(state, z_ref[pl.ds(24 - WIDE + i, 8, stride=SHARE), :])
            if i >= 2 * MAXP:
                o_ref[pl.ds(i - 2 * MAXP, 8, stride=SHARE), :] = tile * scale

    first = o_ref[pl.ds(REACH, LANES), :].T
    second = o_ref[pl.ds(REACH + LANES, LANES), :].T
    o_ref[pl.ds(REACH, REACH), :] = o_ref[pl.ds(REACH + 2 * LANES, REACH), :]
    third = o_ref[pl.ds(0, LANES), :].T
    packs = []
    for side in range(2):
        sense = -1.0 if side else 1.0

        def row(field, distance):
            slot = EDGE_SLOTS.index((field, distance))
            place = 8 * (len(EDGE_SLOTS) * side + slot)
            own = slice(place, place + 8)
            return jnp.concatenate([first[own], second[own], turn(third[own], -REACH)], axis=-1)

        e0, e1, n0, n1, n2, h0, h1 = (row(*slot) for slot in EDGE_SLOTS)
        outer = h0 + gravity_weight * (zonal(e0) + sense * n1)
        inner = h1 + gravity_weight * (zonal(e1) + sense * (n2 - n0))
        own_ref[side] = outer
        at = 63 if side else 0
        pack = jnp.broadcast_to(mer_ref[:, at : at + 1], (8, LANES))
        out = []
        for slot, value in enumerate((outer, inner, e0, n0)):
            out += [value[:, :LANES], value[:, LANES : 2 * LANES]]
            start = 2 * REACH * slot
            inside = (lane >= start) & (lane < start + 2 * REACH)
            pack = jnp.where(inside, turn(value[:, 2 * LANES :], REACH + start), pack)
        packs.append(out + [pack])
    for place, (top, bottom) in enumerate(zip(*packs)):
        a_ref[pl.ds(8 * place, 8)] = jnp.where(even_lat, bottom, top)
        b_ref[pl.ds(8 * place, 8)] = jnp.where(even_lat, top, bottom)


def following(rows):
    count = rows.shape[0]
    return pltpu.roll(rows, count - 1, 0) - pltpu.roll(rows, 1, 0)


def is_polar(lat_blocks, rows, band):
    position = lax.axis_index("lat")
    return (position < band // rows) | (position >= lat_blocks - band // rows)


def leaves_results(lat_blocks, rows, band):
    position = lax.axis_index("lat")
    return (position == band // rows - 1) | (position >= lat_blocks - band // rows)


def whole(f_ref, f, start, rows):
    tiles = range(f_ref.shape[1])
    return jnp.concatenate([f_ref[f, t, pl.ds(start, rows), :] for t in tiles], axis=-1)


def new_heights(f_ref, v_ref):
    tiles = f_ref.shape[1]

    def weight(k, l):
        return jnp.concatenate([v_ref[k, l]] * tiles, axis=-1)

    for first in range(0, 64, 8):
        old = []
        for l in range(8):
            start = 64 * l + first
            north = whole(f_ref, 1, start, 8)
            above = whole(f_ref, 1, start - 1, 8) if start else pltpu.roll(north, 1, 0)
            below = whole(f_ref, 1, start + 1, 8) if start < 512 - 8 else pltpu.roll(north, 7, 0)
            slope = zonal(whole(f_ref, 0, start, 8)) + (below - above)
            old.append(whole(f_ref, 2, start, 8) + gravity_weight * slope)
        for l in range(8):
            total = weight(0, l) * old[0]
            for k in range(1, 8):
                total = total + weight(k, l) * old[k]
            for t in range(tiles):
                place = pl.ds(64 * l + first, 8)
                f_ref[2, t, place, :] = total[:, LANES * t : LANES * (t + 1)]


def results(f_ref, zb_ref, mb_ref, write):
    tiles = f_ref.shape[1]
    for l in range(8):
        h2 = whole(f_ref, 2, 64 * l, 64)
        h2_zonal = zonal(h2)
        e1 = whole(f_ref, 0, 64 * l, 64) + divergence_weight * h2_zonal
        n1 = whole(f_ref, 1, 64 * l, 64) + divergence_weight * following(h2)
        zon = jnp.concatenate([zb_ref[l]] * tiles, axis=-1)
        mer = jnp.concatenate([mb_ref[l]] * tiles, axis=-1)
        for f, field in enumerate((e1, n1, h2)):
            slope = h2_zonal if f == 2 else zonal(field)
            write(f, l, field + zon * slope + following(mer * field))


def edge_row(side, distance):
    return 63 - distance if side else distance


def inner_results(f_ref, zb_ref, mb_ref, ob_ref):
    def write(f, l, value):
        for t in range(2):
            ob_ref[f, t, pl.ds(64 * l, 64), :] = value[:, LANES * t : LANES * (t + 1)]

    results(f_ref, zb_ref, mb_ref, write)


def interior_kernel(
    lat_blocks,
    _, wind_ref, height_ref, counts_ref, zon_ref, mer_ref, v_ref,
    f_ref, ob_ref, edge_ref, zb_ref, mb_ref, count_ref, edge_count_ref, vb_ref, vc_ref,
    wo_ref, ho_ref,
):
    lane = lanes()
    level = lax.broadcasted_iota(jnp.int32, (8, LANES), 0)
    polar = is_polar(lat_blocks, 64, counts_ref.shape[0] // 2)

    @pl.when(polar)
    def _():
        count = jnp.zeros((8, LANES), jnp.int32)
        for row in range(64):
            value = row_count(counts_ref, row, 64, lat_blocks)
            count = jnp.where(jnp.bitwise_and(lane, 63) == row, value, count)
        count_ref[...] = count
        count = jnp.zeros((8, LANES), jnp.int32)
        for side in range(2):
            for slot, (_, distance) in enumerate(EDGE_SLOTS):
                value = row_count(counts_ref, edge_row(side, distance), 64, lat_blocks)
                place = 8 * (len(EDGE_SLOTS) * side + slot)
                count = jnp.where(lane >= place, value, count)
        edge_count_ref[...] = count

    @pl.when(jnp.logical_not(polar))
    def _():
        count_ref[...] = jnp.zeros((8, LANES), jnp.int32)
        edge_count_ref[...] = jnp.zeros((8, LANES), jnp.int32)

    @pl.when(polar)
    def _():
        count = count_ref[...]
        stream = Stream(group_masks(count))
        scale = undo(count)

        def winds(chunk, state):
            for u in range(8):
                i = 8 * chunk + u
                state, tile = stream.step(state, wind_ref[i])
                wo_ref[i] = tile * scale
            return tuple(state)

        lax.fori_loop(0, 32, winds, tuple(stream.start()))

        def heights(chunk, state):
            for u in range(0, 8, 2):
                i = 8 * chunk + u
                low = height_ref[pl.ds(pl.multiple_of(4 * i, 8), 8), :]
                high = height_ref[pl.ds(pl.multiple_of(4 * i + 448, 8), 8), :]
                pair = jnp.where(level < 4, low, pltpu.roll(high, 4, 0))
                state, tile = stream.step(state, pair)
                ho_ref[i] = tile * scale
                pair = jnp.where(level < 4, pltpu.roll(low, 4, 0), high)
                state, tile = stream.step(state, pair)
                ho_ref[i + 1] = tile * scale
            return tuple(state)

        lax.fori_loop(0, 18, heights, tuple(stream.start()))
        wo = wo_ref.reshape(wo_ref.shape[0] * 8, LANES)
        ho = ho_ref.reshape(ho_ref.shape[0] * 8, LANES)
        for f in range(3):
            for q in range(4):
                for t in range(2):
                    if f < 2:
                        tall = wo[pl.ds(8 * (MAXP + LANES * t) + 4 * f + q, LANES, stride=8), :]
                    else:
                        tall = ho[pl.ds(8 * MAXP * (1 + t) + q + 4 * t, LANES, stride=8), :]
                    f_ref[f, t, pl.ds(LANES * q, LANES), :] = tall.T

    def keep_edge(slot, field, distance):
        for side in range(2):
            for t in range(2):
                place = pl.ds(edge_row(side, distance), 8, stride=64)
                edge_ref[side, slot, :, pl.ds(LANES * t, LANES)] = f_ref[field, t, place, :]

    for d in range(4):
        keep_edge(d, 0, d)
        keep_edge(4 + d, 1, d)
    for k in range(8):
        for l in range(8):
            vb_ref[k, l] = jnp.full((8, LANES), v_ref[k, l], jnp.float32)
    for k, column in enumerate(mixing(v_ref)):
        vc_ref[k] = column
    for l in range(8):
        zb_ref[l] = jnp.broadcast_to(zon_ref[l : l + 1, :], (LANES, 64)).T
        mb_ref[l] = jnp.broadcast_to(mer_ref[l : l + 1, :], (LANES, 64)).T

    new_heights(f_ref, vb_ref)
    for d in range(1, 5):
        keep_edge(7 + d, 2, d)

    @pl.when(jnp.logical_not(leaves_results(lat_blocks, 64, counts_ref.shape[0] // 2)))
    def _():
        inner_results(f_ref, zb_ref, mb_ref, ob_ref)


SIDE = 64
OWN = SIDE - WIDE


def fix_kernel(
    lat_blocks, band,
    _, inner_f_ref, inner_ref, wind_ref, height_ref, rb_ref, ra_ref, zb_ref, mb_ref, count_ref, v_ref,
    ob_ref, all_ref, edge_ref,
    f_ref, wz_ref, hz_ref,
):
    even_lon = is_even("lon")
    level = lax.broadcasted_iota(jnp.int32, (8, LANES), 0)
    polar = is_polar(lat_blocks, 64, band)

    @pl.when(leaves_results(lat_blocks, 64, band))
    def _():
        inner_results(inner_f_ref, zb_ref, mb_ref, ob_ref)

    def left(place):
        return jnp.where(even_lon, rb_ref[place, :], ra_ref[place, :])

    def right(place):
        return jnp.where(even_lon, ra_ref[place, :], rb_ref[place, :])

    for i in range(WIDE):
        wz_ref[MAXP + i] = left(pl.ds(8 * i, 8))
        wz_ref[MAXP + SIDE + OWN + i] = right(pl.ds(8 * i, 8))
    wz_ref[pl.ds(MAXP + WIDE, OWN)] = wind_ref[pl.ds(0, OWN)]
    wz_ref[pl.ds(MAXP + SIDE, OWN)] = wind_ref[pl.ds(256 - OWN, OWN)]
    for i in range(SIDE):
        if i < WIDE:
            low = left(pl.ds(HEIGHTS + 4 * i, 8))
        else:
            low = height_ref[pl.ds(4 * (i - WIDE), 8), :]
        if i < OWN:
            high = height_ref[pl.ds(4 * (256 - OWN + i) - 4, 8), :]
        else:
            high = right(pl.ds(HEIGHTS + 4 * (i - OWN) - 4, 8))
        hz_ref[MAXP + i] = jnp.where(level < 4, low, high)

    @pl.when(polar)
    def _():
        count = count_ref[...]
        stream = Stream(group_masks(count))
        scale = undo(count)

        def run(ref, base):
            def steps(chunk, state):
                for u in range(8):
                    i = base + 8 * chunk + u
                    state, tile = stream.step(state, ref[MAXP + i])
                    ref[i] = tile * scale
                return tuple(state)

            lax.fori_loop(0, SIDE // 8, steps, tuple(stream.start()))

        run(wz_ref, 0)
        run(wz_ref, SIDE)
        run(hz_ref, 0)

    wz = wz_ref.reshape(wz_ref.shape[0] * 8, LANES)
    hz = hz_ref.reshape(hz_ref.shape[0] * 8, LANES)
    for f in range(3):
        for q in range(4):
            if f < 2:
                tall = wz[pl.ds(8 * MAXP + 4 * f + q, LANES, stride=8), :]
            else:
                parts = [hz[pl.ds(8 * MAXP + q + 4 * s, SIDE, stride=8), :] for s in range(2)]
                tall = jnp.concatenate(parts, axis=0)
            f_ref[f, 0, pl.ds(LANES * q, LANES), :] = tall.T

    lane = lanes()

    def keep_edge(slot, field, distance):
        for side in range(2):
            near = f_ref[field, 0, pl.ds(edge_row(side, distance), 8, stride=64), :]
            west, east = turn(near, -WIDE), turn(near, WIDE)
            first, second = inner_ref[side, slot, :, :LANES], inner_ref[side, slot, :, LANES:]
            edge_ref[side, slot, :, pl.ds(0, LANES)] = jnp.where(lane < 24, west, first)
            edge_ref[side, slot, :, pl.ds(LANES, LANES)] = jnp.where(lane >= 104, east, second)
            edge_ref[side, slot, :, pl.ds(2 * LANES, LANES)] = jnp.where(lane < 64, east, west)

    for d in range(4):
        keep_edge(d, 0, d)
        keep_edge(4 + d, 1, d)

    new_heights(f_ref, v_ref)
    for d in range(1, 5):
        keep_edge(7 + d, 2, d)
    wide_lane = lax.broadcasted_iota(jnp.int32, (64, LANES), 1)

    def write(f, l, near):
        west, east = turn(near, -WIDE), turn(near, WIDE)
        rows = pl.ds(64 * l, 64)
        all_ref[f, 0, rows, :] = jnp.where(wide_lane < 22, west, ob_ref[f, 0, rows, :])
        all_ref[f, 1, rows, :] = jnp.where(wide_lane >= 106, east, ob_ref[f, 1, rows, :])

    results(f_ref, zb_ref, mb_ref, write)


def mixing(v_ref):
    level = lax.broadcasted_iota(jnp.int32, (8, LANES), 0)
    columns = []
    for k in range(8):
        column = jnp.full((8, LANES), v_ref[k, 0], jnp.float32)
        for l in range(1, 8):
            column = jnp.where(level == l, v_ref[k, l], column)
        columns.append(column)
    return columns


def mix(columns, height):
    tiles = []
    for t in range(height.shape[-1] // LANES):
        tile = height[..., t * LANES : (t + 1) * LANES]
        total = None
        for k, column in enumerate(columns):
            term = column * jnp.broadcast_to(tile[..., k : k + 1, :], tile.shape)
            total = term if total is None else total + term
        tiles.append(total)
    return jnp.concatenate(tiles, axis=-1)


def wide(column):
    return jnp.concatenate([column] * (SPAN // LANES), axis=-1)


def finish_kernel(
    lat_blocks,
    edge_ref, own_ref, all_ref, gb_ref, ga_ref, zon_ref, mer_ref, v_ref,
    oe_ref, on_ref, oh_ref,
    ob_ref, sems, edge_sems,
):
    outs = (oe_ref, on_ref, oh_ref)
    copies = []
    for f, out in enumerate(outs):
        for t in range(2):
            copy = pltpu.make_async_copy(
                all_ref.at[f, t].reshape(8, 64, LANES).at[:, pl.ds(8, 48)],
                out.at[:, pl.ds(8, 48), pl.ds(LANES * t, LANES)],
                sems.at[f, t],
            )
            copy.start()
            copies.append(copy)
    position = lax.axis_index("lat")
    even_lat = is_even("lat")
    lane = lanes()
    columns = [v_ref[k] for k in range(8)]
    for side in range(2):
        top = side == 0
        sense = 1.0 if top else -1.0
        pole = position == (0 if top else lat_blocks - 1)
        turned = jnp.where(pole, -1.0, 1.0)

        def ghost_tile(place):
            a, b = ga_ref[pl.ds(8 * place, 8)], gb_ref[pl.ds(8 * place, 8)]
            return jnp.where(even_lat, b, a) if top else jnp.where(even_lat, a, b)

        pack = ghost_tile(8)

        def ghost(slot):
            third = turn(pack, -REACH - 2 * REACH * slot)
            return jnp.concatenate([ghost_tile(2 * slot), ghost_tile(2 * slot + 1), third], axis=-1)

        e = {d: edge_ref[side, d] for d in range(4)}
        n = {d: edge_ref[side, 4 + d] for d in range(4)}
        h2 = {d: edge_ref[side, 7 + d] for d in range(1, 5)}
        e[-1] = ghost(2)
        n[-1] = ghost(3) * turned
        h2[-2] = mix(columns, ghost(1))
        h2[-1] = mix(columns, ghost(0) + (gravity_weight * sense) * n[0])
        h2[0] = mix(columns, own_ref[side] - (gravity_weight * sense) * n[-1])
        e1, n1, h2_zonal = {}, {}, {}
        for d in range(-1, 4):
            h2_zonal[d] = zonal(h2[d])
            e1[d] = e[d] + divergence_weight * h2_zonal[d]
            n1[d] = n[d] + (divergence_weight * sense) * (h2[d + 1] - h2[d - 1])
        mer_ghost = wide(jnp.where(lane < LANES // 2, turn(pack, LANES // 2), pack))

        def coefficient(ref, d):
            row = edge_row(side, d)
            return wide(jnp.broadcast_to(ref[:, row : row + 1], (8, LANES)))

        zon = {d: coefficient(zon_ref, d) for d in range(3)}
        mer = {d: coefficient(mer_ref, d) for d in range(4)}
        for f, field in enumerate((e1, n1, h2)):
            mer[-1] = mer_ghost if f == 0 else mer_ghost * turned
            flow = {d: mer[d] * field[d] for d in range(-1, 4)}
            for t in range(2):
                for l in range(8):
                    ob_ref[f, side, t, pl.ds(8 * l, 8), :] = all_ref[
                        f, t, pl.ds(64 * l + 56 * side, 8), :
                    ]
            for d in range(3 if f == 1 else 2):
                slope = h2_zonal[d] if f == 2 else zonal(field[d])
                value = field[d] + zon[d] * slope + sense * (flow[d + 1] - flow[d - 1])
                for t in range(2):
                    ob_ref[f, side, t, pl.ds(d if top else 7 - d, 8, stride=8), :] = value[
                        :, LANES * t : LANES * (t + 1)
                    ]
    for side in range(2):
        for f, out in enumerate(outs):
            for t in range(2):
                copy = pltpu.make_async_copy(
                    ob_ref.at[f, side, t].reshape(8, 8, LANES),
                    out.at[:, pl.ds(56 * side, 8), pl.ds(LANES * t, LANES)],
                    edge_sems.at[f, side, t],
                )
                copy.start()
                copies.append(copy)
    for copy in copies:
        copy.wait()


def body(
    lat_blocks, lon_blocks, axes,
    east_adjoint, north_adjoint, height_adjoint,
    zonal_courant, meridional_courant, vertical_inverse, pass_counts,
):
    f32 = jnp.float32
    fields = tuple(
        pltpu.with_memory_space_constraint(x, pltpu.HBM)
        for x in (east_adjoint, north_adjoint, height_adjoint)
    )

    def in_vmem(*dims):
        return pltpu.VMEM(dims, f32)

    def params():
        return pltpu.CompilerParams(vmem_limit_bytes=40 * 1024 * 1024)

    lon_a, lon_b, winds, heights, edge_rows, local = pl.pallas_call(
        pack_kernel,
        out_shape=(
            in_vmem(PAYLOAD, LANES), in_vmem(PAYLOAD, LANES),
            in_vmem(256, 8, LANES), in_vmem(1024, LANES), in_vmem(256, LANES),
            in_vmem(3, 2, 512, LANES),
        ),
        in_specs=[HBM] * 3,
        out_specs=(VMEM,) * 6,
        scratch_shapes=[pltpu.VMEM((2, LANES, LANES), f32), pltpu.SemaphoreType.DMA((3, 2))],
        compiler_params=params(),
        name="pack",
    )(*fields)

    def other_lon(o):
        return (((o + 1) ^ 1) - 1) % lon_blocks

    recv_a = lax.ppermute(lon_a, "lon", [(o, o ^ 1) for o in range(lon_blocks)])
    recv_b = lax.ppermute(lon_b, "lon", [(o, other_lon(o)) for o in range(lon_blocks)])

    by_row = in_vmem(8, 64, LANES)
    by_count = pltpu.VMEM((8, LANES), jnp.int32)
    inner_f, inner, inner_edges, zon_wide, mer_wide, counts, edge_counts, weights, columns = pl.pallas_call(
        lambda *refs: interior_kernel(lat_blocks, *refs),
        out_shape=(
            in_vmem(3, 2, 512, LANES), in_vmem(3, 2, 512, LANES), in_vmem(2, 12, 8, 256),
            by_row, by_row, by_count, by_count, in_vmem(8, 8, 8, LANES), in_vmem(8, 8, LANES),
        ),
        in_specs=[VMEM] * 3 + [SMEM, VMEM, VMEM, SMEM],
        out_specs=(VMEM,) * 9,
        input_output_aliases={0: 0},
        scratch_shapes=[
            pltpu.VMEM((272, 8, LANES), f32),
            pltpu.VMEM((160, 8, LANES), f32),
        ],
        compiler_params=params(),
        cost_estimate=pl.CostEstimate(flops=100000000, bytes_accessed=20000000, transcendentals=0),
        name="interior",
    )(
        local, winds, heights, pass_counts, zonal_courant, meridional_courant, vertical_inverse
    )

    band = pass_counts.shape[0] // 2
    lat_a, lat_b, own_edges = pl.pallas_call(
        lambda *refs: edge_kernel(lat_blocks, band, *refs),
        out_shape=(in_vmem(72, LANES), in_vmem(72, LANES), in_vmem(2, 8, SPAN)),
        in_specs=[VMEM] * 5,
        out_specs=(VMEM,) * 3,
        scratch_shapes=[pltpu.VMEM((304, LANES), f32), pltpu.VMEM((264, LANES), f32)],
        compiler_params=params(),
        name="edge",
    )(edge_rows, recv_b, recv_a, edge_counts, meridional_courant)

    def index(a, o):
        return o * lat_blocks + a if axes[0] == "lon" else a * lon_blocks + o

    def other_lat(a, o):
        if a in (0, lat_blocks - 1):
            return a, (o + lon_blocks // 2) % lon_blocks
        return ((a + 1) ^ 1) - 1, o

    pairs = [
        (index(a, o), index(*other_lat(a, o))) for a in range(lat_blocks) for o in range(lon_blocks)
    ]
    ghost_a = lax.ppermute(lat_a, "lat", [(a, a ^ 1) for a in range(lat_blocks)])
    ghost_b = lax.ppermute(lat_b, axes, pairs)

    block = jax.ShapeDtypeStruct(east_adjoint.shape, f32)
    _, final, edges = pl.pallas_call(
        lambda *refs: fix_kernel(lat_blocks, band, *refs),
        out_shape=(
            in_vmem(3, 2, 512, LANES), in_vmem(3, 2, 512, LANES), in_vmem(2, 12, 8, SPAN)
        ),
        in_specs=[VMEM] * 11,
        out_specs=(VMEM,) * 3,
        input_output_aliases={0: 0},
        scratch_shapes=[
            pltpu.VMEM((3, 1, 512, LANES), f32),
            pltpu.VMEM((MAXP + 2 * SIDE, 8, LANES), f32),
            pltpu.VMEM((MAXP + SIDE, 8, LANES), f32),
        ],
        compiler_params=params(),
        cost_estimate=pl.CostEstimate(flops=50000000, bytes_accessed=10000000, transcendentals=0),
        name="fix",
    )(
        inner, inner_f, inner_edges, winds, heights, recv_b, recv_a, zon_wide, mer_wide, counts, weights,
    )

    return pl.pallas_call(
        lambda *refs: finish_kernel(lat_blocks, *refs),
        out_shape=(block,) * 3,
        in_specs=[VMEM] * 8,
        out_specs=(HBM,) * 3,
        scratch_shapes=[
            pltpu.VMEM((3, 2, 2, 64, LANES), f32),
            pltpu.SemaphoreType.DMA((3, 2)),
            pltpu.SemaphoreType.DMA((3, 2, 2)),
        ],
        compiler_params=params(),
        name="finish",
    )(
        edges, own_edges, final, ghost_b, ghost_a, zonal_courant, meridional_courant, columns
    )


def solution(mesh):
    sizes = dict(mesh.shape)
    axes = tuple(mesh.axis_names)
    spread_out = P(None, "lat", "lon")
    return jax.shard_map(
        lambda *args: body(sizes["lat"], sizes["lon"], axes, *args),
        mesh=mesh,
        in_specs=(spread_out,) * 3 + (P(None, "lat"), P(None, "lat"), P(), P()),
        out_specs=(spread_out,) * 3,
        check_vma=False,
    )
```
